32 devices in a mesh: dp: 8 (over z, x), tensor: 4 (over y, core).
Axes of the slice: x: 2, y: 2, z: 4, core: 2. Of those that a mesh axis runs over, the one named last changes fastest.
Arguments:
- tokens: bfloat16 [16384, 1024], P('dp'), may hold values from -6 to 6
- cotangent: bfloat16 [16384, 1024], P('dp'), may hold values from -6 to 6
- lengths: int32 [8], P('dp'), may hold values from 200 to 2048, as said below
- joint_weight: float32 [1024, 3072], P('dp', 'tensor'), as said below
- output_weight: float32 [1024, 1024], P('tensor', 'dp'), as said below
- widen_weight: float32 [1024, 4096], P('dp', 'tensor'), as said below
- narrow_weight: float32 [4096, 1024], P('tensor', 'dp'), as said below
- shared_vectors: float32 [6, 1024], P(None, 'dp'), as said below
- split_vectors: float32 [4, 1536], P('tensor', 'dp'), may hold values from -1.75 to 1.75
- joint_first: float32 [1024, 3072], P('dp', 'tensor'), may hold values from -0.00018310547 to 0.00018310547
- joint_second: float32 [1024, 3072], P('dp', 'tensor'), may hold values from 4.207952e-09 to 1.6673019e-08
- output_first: float32 [1024, 1024], P('tensor', 'dp'), may hold values from -0.00018310547 to 0.00018310547
- output_second: float32 [1024, 1024], P('tensor', 'dp'), may hold values from 4.207952e-09 to 1.6673019e-08
- widen_first: float32 [1024, 4096], P('dp', 'tensor'), may hold values from -0.00018310547 to 0.00018310547
- widen_second: float32 [1024, 4096], P('dp', 'tensor'), may hold values from 4.207952e-09 to 1.6673019e-08
- narrow_first: float32 [4096, 1024], P('tensor', 'dp'), may hold values from -0.00018310547 to 0.00018310547
- narrow_second: float32 [4096, 1024], P('tensor', 'dp'), may hold values from 4.207952e-09 to 1.6673019e-08
- shared_first: float32 [6, 1024], P(None, 'dp'), may hold values from -0.00048828125 to 0.00048828125
- shared_second: float32 [6, 1024], P(None, 'dp'), may hold values from 3.7315804e-08 to 1.5085112e-07
- split_first: float32 [4, 1536], P('tensor', 'dp'), may hold values from -0.00048828125 to 0.00048828125
- split_second: float32 [4, 1536], P('tensor', 'dp'), may hold values from 3.7315804e-08 to 1.5085112e-07
Outputs:
- layer_output: bfloat16 [16384, 1024], P('dp')
- input_grad: bfloat16 [16384, 1024], P('dp')
- grad_norm: float32 [], replicated
- joint_master: float32 [1024, 3072], P('dp', 'tensor')
- joint_moment: float32 [1024, 3072], P('dp', 'tensor')
- joint_variance: float32 [1024, 3072], P('dp', 'tensor')
- output_master: float32 [1024, 1024], P('tensor', 'dp')
- output_moment: float32 [1024, 1024], P('tensor', 'dp')
- output_variance: float32 [1024, 1024], P('tensor', 'dp')
- widen_master: float32 [1024, 4096], P('dp', 'tensor')
- widen_moment: float32 [1024, 4096], P('dp', 'tensor')
- widen_variance: float32 [1024, 4096], P('dp', 'tensor')
- narrow_master: float32 [4096, 1024], P('tensor', 'dp')
- narrow_moment: float32 [4096, 1024], P('tensor', 'dp')
- narrow_variance: float32 [4096, 1024], P('tensor', 'dp')
- shared_master: float32 [6, 1024], P(None, 'dp')
- shared_moment: float32 [6, 1024], P(None, 'dp')
- shared_variance: float32 [6, 1024], P(None, 'dp')
- split_master: float32 [4, 1536], P('tensor', 'dp')
- split_moment: float32 [4, 1536], P('tensor', 'dp')
- split_variance: float32 [4, 1536], P('tensor', 'dp')
The draws below stay inside these ranges and needn't reach their ends.
Inputs may be any that keep to these rules, and one draw needn't show every extreme that they name: `lengths`: one sequence's length in its row of 2048 slots. `joint_weight`: master weights. `output_weight`: master weights. `widen_weight`: master weights. `narrow_weight`: master weights. `shared_vectors`: gains and shifts.
All inputs are finite; a program needn't handle non-finite values.
Results may differ from the reference program's by a relative error of at most 0.02.
The reference program's roundings to bfloat16 on the way count: a program that leaves them out, or rounds other values in their place, can miss the bound.
Values may be sent and summed in bfloat16 or wider, within the bound.
A program may use at most 256 MiB of HBM per device.

```python
import math
import jax
import jax.numpy as jnp
from jax import lax

D = 1024
HEADS = 16
FF = 4096
LEN = 2048
SHORT = 200
STEP = 10
SEQS = 8
TOKENS = 16384
PARAMS = 12595200
N_TENSOR = 4


def rising_scale(extent, growth):
    fraction = jnp.arange(extent, dtype=jnp.float32) / max(extent - 1, 1)
    return jnp.exp(math.log(growth) * (fraction - 0.5))


def draw_lengths(key, part):
    key = jax.random.fold_in(key, 17)
    order_ids = jnp.arange(SEQS, dtype=jnp.int32)
    spread_len = LEN - SHORT
    lowest = SHORT + spread_len * 3 * order_ids // (5 * max(SEQS - 1, 1))
    drawn = jax.random.randint(key, (SEQS,), lowest, lowest + 2 * spread_len // 5 + 1)
    drawn = drawn.at[0].set(SHORT).at[SEQS - 1].set(LEN)
    return drawn.astype(jnp.int32)


def draw_joint_weight(key, part):
    key = jax.random.fold_in(key, 11)
    values = jax.random.normal(key, (D, 3 * D), jnp.float32)
    growth = 3.0
    return values * rising_scale(3 * D, growth)[None, :] / math.sqrt(D)


def draw_output_weight(key, part):
    key = jax.random.fold_in(key, 13)
    values = jax.random.normal(key, (D, D), jnp.float32)
    growth = 3.0
    return values * rising_scale(D, growth)[:, None] * (6.0 / math.sqrt(D))


def draw_widen_weight(key, part):
    key = jax.random.fold_in(key, 19)
    values = jax.random.normal(key, (D, FF), jnp.float32)
    growth = 3.0
    return values * rising_scale(FF, growth)[None, :] / math.sqrt(D)


def draw_narrow_weight(key, part):
    key = jax.random.fold_in(key, 29)
    values = jax.random.normal(key, (FF, D), jnp.float32)
    growth = 3.0
    return values * rising_scale(FF, growth)[:, None] * (1.5 / math.sqrt(FF))


def draw_shared_vectors(key, part):
    key = jax.random.fold_in(key, 23)
    noise = jax.random.normal(key, (6, D), jnp.float32)
    growth = 3.0
    row_ids = jnp.arange(6, dtype=jnp.int32)
    is_gain = (row_ids % 2 == 0) & (row_ids < 4)
    gains = rising_scale(D, growth)[None, :] * (1.0 + 0.15 * noise)
    return jnp.where(is_gain[:, None], gains, 0.3 * noise)


def levels(rng, dims, shards, smallest, high):
    def one(axis_at, shards_of):
        steps = jax.random.uniform(jax.random.fold_in(jax.random.fold_in(rng, 6), axis_at), (shards_of,), jnp.float32, smallest / len(shards), high / len(shards))
        return jnp.repeat(jnp.exp(steps), dims[axis_at] // shards_of).reshape((-1,) + (1,) * (len(dims) - axis_at - 1))

    factor_of = one(*shards[0])
    for cut in shards[1:]:
        factor_of = factor_of * one(*cut)
    return factor_of


def gaussian(stream_key, shape, scale, reach, shards=(), kind=jnp.bfloat16):
    factor_of = levels(stream_key, shape, shards, -0.22, 0.18) if shards else 1.0
    values = jax.random.normal(stream_key, shape, jnp.float32) * scale * factor_of
    return jnp.minimum(jnp.maximum(values, -reach), reach).astype(kind)


def setup_inputs(seed: int = 0) -> dict:
    key_list = jax.random.split(jax.random.key(seed), 22)
    return {
        "tokens": gaussian(key_list[0], (TOKENS, D), 1.0, 6.0, ((0, 8),)),
        "cotangent": gaussian(key_list[1], (TOKENS, D), 1.0, 6.0, ((0, 8),)),
        "lengths": draw_lengths(jax.random.fold_in(key_list[21], 71), 0),
        "joint_weight": draw_joint_weight(jax.random.fold_in(key_list[21], 71), 0),
        "output_weight": draw_output_weight(jax.random.fold_in(key_list[21], 71), 0),
        "widen_weight": draw_widen_weight(jax.random.fold_in(key_list[21], 71), 0),
        "narrow_weight": draw_narrow_weight(jax.random.fold_in(key_list[21], 71), 0),
        "shared_vectors": draw_shared_vectors(jax.random.fold_in(key_list[21], 71), 0),
        "split_vectors": gaussian(key_list[8], (N_TENSOR, (2 * D + FF) // N_TENSOR), 0.3, 1.75, ((0, 4), (1, 8)), jnp.float32),
        "joint_first": gaussian(key_list[9], (D, 3 * D), (0.11 / PARAMS ** 0.5), 0.00018310547, ((0, 8), (1, 4)), jnp.float32),
        "joint_second": jnp.clip(jnp.exp(math.log(1.6673018521373706e-08) - 1.37681564 * jax.random.uniform(key_list[10], (D, 3 * D), jnp.float32) ** levels(key_list[10], (D, 3 * D), ((0, 8), (1, 4)), -0.2, 0.2)), 4.2079522089011334e-09, 1.6673018521373706e-08),
        "output_first": gaussian(key_list[11], (D, D), (0.11 / PARAMS ** 0.5), 0.00018310547, ((0, 4), (1, 8)), jnp.float32),
        "output_second": jnp.clip(jnp.exp(math.log(1.6673018521373706e-08) - 1.37681564 * jax.random.uniform(key_list[12], (D, D), jnp.float32) ** levels(key_list[12], (D, D), ((0, 4), (1, 8)), -0.2, 0.2)), 4.2079522089011334e-09, 1.6673018521373706e-08),
        "widen_first": gaussian(key_list[13], (D, FF), (0.11 / PARAMS ** 0.5), 0.00018310547, ((0, 8), (1, 4)), jnp.float32),
        "widen_second": jnp.clip(jnp.exp(math.log(1.6673018521373706e-08) - 1.37681564 * jax.random.uniform(key_list[14], (D, FF), jnp.float32) ** levels(key_list[14], (D, FF), ((0, 8), (1, 4)), -0.2, 0.2)), 4.2079522089011334e-09, 1.6673018521373706e-08),
        "narrow_first": gaussian(key_list[15], (FF, D), (0.11 / PARAMS ** 0.5), 0.00018310547, ((0, 4), (1, 8)), jnp.float32),
        "narrow_second": jnp.clip(jnp.exp(math.log(1.6673018521373706e-08) - 1.37681564 * jax.random.uniform(key_list[16], (FF, D), jnp.float32) ** levels(key_list[16], (FF, D), ((0, 4), (1, 8)), -0.2, 0.2)), 4.2079522089011334e-09, 1.6673018521373706e-08),
        "shared_first": gaussian(key_list[17], (6, D), (0.33 / PARAMS ** 0.5), 0.00048828125, ((1, 8),), jnp.float32),
        "shared_second": jnp.clip(jnp.exp(math.log(1.5085112181623117e-07) - 1.3968765 * jax.random.uniform(key_list[18], (6, D), jnp.float32) ** levels(key_list[18], (6, D), ((1, 8),), -0.2, 0.2)), 3.7315803780302303e-08, 1.5085112181623117e-07),
        "split_first": gaussian(key_list[19], (N_TENSOR, (2 * D + FF) // N_TENSOR), (0.33 / PARAMS ** 0.5), 0.00048828125, ((0, 4), (1, 8)), jnp.float32),
        "split_second": jnp.clip(jnp.exp(math.log(1.5085112181623117e-07) - 1.3968765 * jax.random.uniform(key_list[20], (N_TENSOR, (2 * D + FF) // N_TENSOR), jnp.float32) ** levels(key_list[20], (N_TENSOR, (2 * D + FF) // N_TENSOR), ((0, 4), (1, 8)), -0.2, 0.2)), 3.7315803780302303e-08, 1.5085112181623117e-07),
    }


NORM_EPSILON = 1e-05
CLIP_LIMIT = 1.0
BETA_FIRST = 0.9
BETA_SECOND = 0.95
ADAM_EPSILON = 1e-08
MATRIX_RATE = 0.05
OUTPUT_RATE = 0.2
VECTOR_RATE = 0.6
MATRIX_DECAY = 0.1
MASKED_SCORE = -1e+30
HIGHEST = lax.Precision.HIGHEST

@jax.custom_vjp
def low(v):
    return lax.optimization_barrier(v.astype(jnp.bfloat16)).astype(jnp.float32)

@jax.custom_vjp
def low_back(v):
    return v

def low_keep(v):
    return (low(v), None)

def low_pass(kept, grad):
    return (grad,)

def back_keep(v):
    return (v, None)

def back_low(kept, grad):
    return (low(grad),)
low.defvjp(low_keep, low_pass)
low_back.defvjp(back_keep, back_low)

def layer_norm(values, gain, shift):
    centred = values - lax.optimization_barrier(jnp.mean(values, axis=-1, keepdims=True))
    spread = lax.optimization_barrier(jnp.mean(centred * centred, axis=-1, keepdims=True))
    return centred * lax.rsqrt(spread + NORM_EPSILON) * gain + shift

def matmul(left, right):
    return jnp.dot(left, right, precision=HIGHEST, preferred_element_type=jnp.float32)

def layer(inputs, joint_weight, output_weight, widen_weight, narrow_weight, shared_vectors, split_vectors, length):
    joint_low = low(joint_weight)
    output_low = low(output_weight)
    widen_low = low(widen_weight)
    narrow_low = low(narrow_weight)
    shared_low = low(shared_vectors)
    split_low = low(split_vectors)
    head_size = D // HEADS
    group_cols = D // N_TENSOR
    group_units = FF // N_TENSOR
    query_bias = split_low[:, :group_cols].reshape(HEADS, head_size)
    value_bias = split_low[:, group_cols:2 * group_cols].reshape(HEADS, head_size)
    widen_bias = split_low[:, 2 * group_cols:].reshape(FF)
    positions = jnp.arange(LEN, dtype=jnp.int32)
    live_rows = (positions < length).astype(jnp.float32)[:, None]
    attn_input = low(layer_norm(inputs, shared_low[0], shared_low[1]))
    joint_parts = []
    for group in range(N_TENSOR):
        group_input = low_back(attn_input)
        joint_parts.append(matmul(group_input, joint_low[:, group * 3 * group_cols:(group + 1) * 3 * group_cols]))
    joint = jnp.concatenate(joint_parts, axis=1).reshape(LEN, HEADS, 3, head_size)
    projected = jnp.stack([joint[:, :, 0] + query_bias, joint[:, :, 1], joint[:, :, 2] + value_bias])
    projected = low(low_back(projected))
    queries = projected[0]
    keys_all = projected[1]
    values_all = projected[2]
    slopes = jnp.exp2(-8.0 * (jnp.arange(HEADS, dtype=jnp.int32) + 1).astype(jnp.float32) / HEADS)
    block_rows = min(512, LEN)
    score_scale = 1.0 / math.sqrt(head_size)

    def attend(first_row):
        block_queries = lax.dynamic_slice_in_dim(queries, first_row, block_rows, 0)
        scores = jnp.einsum('qhd,khd->hqk', block_queries, keys_all, precision=HIGHEST) * score_scale
        row_ids = first_row + jnp.arange(block_rows, dtype=jnp.int32)
        offset = (positions[None, :] - row_ids[:, None]).astype(jnp.float32)
        scores = low_back(scores + slopes[:, None, None] * offset[None])
        allowed = (positions[None, :] <= row_ids[:, None]) & (positions[None, :] < length)
        scores = jnp.where(allowed[None], scores, MASKED_SCORE)
        highest = lax.optimization_barrier(jnp.max(scores, axis=-1, keepdims=True))
        weights = jnp.exp(scores - highest)
        probabilities = low(weights / lax.optimization_barrier(jnp.sum(weights, axis=-1, keepdims=True)))
        return jnp.einsum('hqk,khd->qhd', probabilities, values_all, precision=HIGHEST)
    starts = jnp.arange(LEN // block_rows, dtype=jnp.int32) * block_rows
    blocks = lax.map(jax.checkpoint(attend), starts)
    heads_out = low(low_back(blocks.reshape(LEN, D)))
    attn_parts = []
    for group in range(N_TENSOR):
        columns = heads_out[:, group * group_cols:(group + 1) * group_cols]
        attn_parts.append(low(matmul(columns, output_low[group * group_cols:(group + 1) * group_cols])))
    hidden_one = inputs + low_back(sum(attn_parts)) + shared_low[4]
    mlp_input = low(layer_norm(hidden_one, shared_low[2], shared_low[3]))
    mlp_parts = []
    for group in range(N_TENSOR):
        group_input = low_back(mlp_input)
        lower = group * group_units
        upper_unit = (group + 1) * group_units
        widened = low_back(matmul(group_input, widen_low[:, lower:upper_unit]) + widen_bias[lower:upper_unit])
        activated = low(jax.nn.gelu(widened, approximate=True))
        mlp_parts.append(low(matmul(activated, narrow_low[lower:upper_unit])))
    result = hidden_one + low_back(sum(mlp_parts)) + shared_low[5]
    return result * live_rows

def adam_step(master, moment, variance, gradient, rate, decay):
    moment_new = BETA_FIRST * moment + (1.0 - BETA_FIRST) * gradient
    variance_new = BETA_SECOND * variance + (1.0 - BETA_SECOND) * gradient * gradient
    moment_hat = moment_new / (1.0 - BETA_FIRST ** STEP)
    variance_hat = variance_new / (1.0 - BETA_SECOND ** STEP)
    master_new = master - rate * (moment_hat / (jnp.sqrt(variance_hat) + ADAM_EPSILON) + decay * master)
    return (master_new, moment_new, variance_new)

def reference(tokens, cotangent, lengths, joint_weight, output_weight, widen_weight, narrow_weight, shared_vectors, split_vectors, joint_first, joint_second, output_first, output_second, widen_first, widen_second, narrow_first, narrow_second, shared_first, shared_second, split_first, split_second):
    inputs_all = tokens.astype(jnp.float32).reshape(SEQS, LEN, D)
    incoming_all = cotangent.astype(jnp.float32).reshape(SEQS, LEN, D)
    params = (joint_weight, output_weight, widen_weight, narrow_weight, shared_vectors, split_vectors)
    zeros_init = tuple((jnp.zeros_like(param) for param in params))

    def one_row(totals, entry):
        row_inputs, row_incoming, length = entry

        def apply_layer(row_values, joint, output, widen, narrow, shared, split):
            return layer(row_values, joint, output, widen, narrow, shared, split, length)
        row_out, pull = jax.vjp(apply_layer, row_inputs, *params)
        grads = pull(row_incoming)
        new_totals = tuple((total + grad for total, grad in zip(totals, grads[1:])))
        return (new_totals, (row_out, grads[0]))
    grads, (outputs, input_grads) = lax.scan(one_row, zeros_init, (inputs_all, incoming_all, lengths))
    layer_output = outputs.reshape(TOKENS, D).astype(jnp.bfloat16)
    input_grad = input_grads.reshape(TOKENS, D).astype(jnp.bfloat16)
    squares = jnp.float32(0.0)
    for grad in grads:
        squares = squares + jnp.sum(grad * grad)
    grad_norm = jnp.sqrt(squares)
    factor = jnp.minimum(1.0, CLIP_LIMIT / (grad_norm + 1e-06))
    firsts = (joint_first, output_first, widen_first, narrow_first, shared_first, split_first)
    seconds = (joint_second, output_second, widen_second, narrow_second, shared_second, split_second)
    rates = (MATRIX_RATE, OUTPUT_RATE, MATRIX_RATE, MATRIX_RATE, VECTOR_RATE, VECTOR_RATE)
    decays = (MATRIX_DECAY, MATRIX_DECAY, MATRIX_DECAY, MATRIX_DECAY, 0.0, 0.0)
    updates = []
    for position in range(6):
        updates.append(adam_step(params[position], firsts[position], seconds[position], factor * grads[position], rates[position], decays[position]))
    return (layer_output, input_grad, grad_norm, updates[0][0], updates[0][1], updates[0][2], updates[1][0], updates[1][1], updates[1][2], updates[2][0], updates[2][1], updates[2][2], updates[3][0], updates[3][1], updates[3][2], updates[4][0], updates[4][1], updates[4][2], updates[5][0], updates[5][1], updates[5][2])
```

```python
import functools
import math

import jax
import jax.numpy as jnp
from jax import lax
from jax.experimental import pallas as pl
from jax.experimental.pallas import tpu as pltpu
from jax.sharding import PartitionSpec as P

F32, BF = jnp.float32, jnp.bfloat16

D = 1024
HEADS = 16
STEP = 10


NORM_EPSILON = 1e-05
CLIP_LIMIT = 1.0
BETA_FIRST = 0.9
BETA_SECOND = 0.95
ADAM_EPSILON = 1e-08
MATRIX_RATE = 0.05
OUTPUT_RATE = 0.2
VECTOR_RATE = 0.6
MATRIX_DECAY = 0.1


def by_kind(values):
    rows, cols = values.shape
    size = D // HEADS
    return jnp.swapaxes(values.reshape(rows, cols // (3 * size), 3, size), 1, 2).reshape(rows, cols)


def by_head(values):
    rows, cols = values.shape
    size = D // HEADS
    return jnp.swapaxes(values.reshape(rows, 3, cols // (3 * size), size), 1, 2).reshape(rows, cols)


NN = (((1,), (0,)), ((), ()))
NT = (((1,), (1,)), ((), ()))
TN = (((0,), (0,)), ((), ()))
LOW = -1e30


def dot(left, right, dims=NN):
    return lax.dot_general(left, right, dims, preferred_element_type=F32)


def three(values):
    high = values.astype(BF).astype(F32)
    rest = values - high
    middle = rest.astype(BF).astype(F32)
    return high, middle, rest - middle


def stack_rows(shape, rows):
    ids = lax.broadcasted_iota(jnp.int32, shape, 0)
    out = jnp.zeros(shape, F32)
    for at, row in enumerate(rows):
        out = jnp.where(ids == at, row, out)
    return out.astype(BF)


def head_tile(ref, rows, col, head, d):
    lane = col + (head // 2) * 128
    tile = ref[rows, lane:lane + 128].astype(F32)
    if head % 2:
        tile = pltpu.roll(tile, 64, 1)
    return tile


def fill_keys(qkv_ref, ka_ref, heads, d, slope_of, first, count):
    rows = pl.ds(first, count)
    lanes = lax.broadcasted_iota(jnp.int32, (count, 128), 1)
    position = (lax.broadcasted_iota(jnp.int32, (count, 128), 0) + first).astype(F32)
    for head in range(heads):
        high, middle, low = three(position * slope_of(head))
        tile = head_tile(qkv_ref, rows, heads * d, head, d)
        for at, part in enumerate((high, middle, low, 1.0, 1.0, 1.0)):
            tile = jnp.where(lanes == d + at, part, tile)
        ka_ref[head, rows, :] = jnp.where(lanes < d + 6, tile, 0.0).astype(BF)


def causal(scores, bk, bq):
    kid = lax.broadcasted_iota(jnp.int32, (bk, bq), 0)
    qid = lax.broadcasted_iota(jnp.int32, (bk, bq), 1)
    return jnp.where(kid <= qid, scores, LOW)


def slope_fn(heads, total_heads):
    rank = lax.axis_index("tensor")
    def slope_of(head):
        index = jnp.full((1, 128), rank * heads + head + 1, jnp.int32).astype(F32)
        return jnp.exp2(index * (-8.0 / total_heads))
    return slope_of


def attend_kernel(heads, d, total_heads, bq, qkv_ref, wo_ref, part_ref, ot_ref, lse_ref, ka_ref, vt_ref):
    i = pl.program_id(0)
    blocks = pl.num_programs(0)
    width = heads * d

    rows_i = pl.ds(pl.multiple_of(i * bq, bq), bq)
    fill_keys(qkv_ref, ka_ref, heads, d, slope_fn(heads, total_heads), pl.multiple_of(i * bq, bq), bq)
    vt_ref[i] = qkv_ref[rows_i, 2 * width:3 * width].T
    qt = qkv_ref[rows_i, 0:width].T
    ones = stack_rows((128 - d, bq), (1.0, 1.0, 1.0))
    queries = [jnp.concatenate([qt[h * d:(h + 1) * d], ones], axis=0) for h in range(heads)]

    def block(j, carry, last):
        out = []
        kr = pl.ds(pl.multiple_of(j * bq, bq), bq)
        for h in range(heads):
            m, l, acc = carry[h]
            s = dot(ka_ref[h, kr, :], queries[h])
            if last:
                s = causal(s, bq, bq)
            top = jnp.maximum(m, jnp.max(s, axis=0, keepdims=True))
            p = jnp.exp(s - top)
            scale = jnp.exp(m - top)
            l = l * scale + jnp.sum(p, axis=0, keepdims=True)
            acc = acc * scale + dot(vt_ref[j, h * d:(h + 1) * d, :], p.astype(BF))
            out.append((top, l, acc))
        return tuple(out)

    start = (jnp.full((1, bq), LOW, F32), jnp.zeros((1, bq), F32), jnp.zeros((d, bq), F32))
    carry = lax.fori_loop(0, i, lambda j, c: block(j, c, False), (start,) * heads)
    carry = block(i, carry, True)
    for h in range(heads):
        m, l, acc = carry[h]
        ot_ref[h * d:(h + 1) * d, :] = acc / l
        lse_ref[0, h:h + 1, :] = m + jnp.log(l)
    part_ref[...] = dot(ot_ref[...].astype(BF), wo_ref[...], TN).astype(BF)


def attend(qkv, wo, heads, d, total_heads, bq=512):
    n, width = qkv.shape[0], heads * d
    bq = min(bq, n)
    nb = n // bq
    feats = wo.shape[1]
    return pl.pallas_call(
        functools.partial(attend_kernel, heads, d, total_heads, bq),
        grid=(nb,),
        in_specs=[pl.BlockSpec(qkv.shape, lambda i: (0, 0)), pl.BlockSpec(wo.shape, lambda i: (0, 0))],
        out_specs=[pl.BlockSpec((bq, feats), lambda i: (i, 0)), pl.BlockSpec((width, bq), lambda i: (0, i)),
                   pl.BlockSpec((1, heads, bq), lambda i: (i, 0, 0))],
        out_shape=[jax.ShapeDtypeStruct((n, feats), BF), jax.ShapeDtypeStruct((width, n), F32),
                   jax.ShapeDtypeStruct((nb, heads, bq), F32)],
        scratch_shapes=[pltpu.VMEM((heads, n, 128), BF), pltpu.VMEM((nb, width, bq), BF)],
        compiler_params=pltpu.CompilerParams(vmem_limit_bytes=48 * 2**20),
        name="attend",
    )(qkv, wo)


def attend_back_kernel(heads, d, total_heads, bq, qkv_ref, wo_ref, gh_ref, ot_ref, lse_ref, out_ref,
                       ka_ref, kt_ref, va_ref, dk_ref, dv_ref):
    g = pl.program_id(0)
    nb = pl.num_programs(0)
    i = nb - 1 - g
    width = heads * d

    @pl.when(g == 0)
    def _():
        dk_ref[...] = jnp.zeros_like(dk_ref)
        dv_ref[...] = jnp.zeros_like(dv_ref)
        lanes = lax.broadcasted_iota(jnp.int32, (bq, 128), 1)
        def fill(b, c):
            first = pl.multiple_of(b * bq, bq)
            fill_keys(qkv_ref, ka_ref, heads, d, slope_fn(heads, total_heads), first, bq)
            rows = pl.ds(first, bq)
            kt_ref[b] = (qkv_ref[rows, width:2 * width].astype(F32) * (1.0 / d ** 0.5)).astype(BF).T
            for h in range(heads):
                tile = head_tile(qkv_ref, rows, 2 * width, h, d)
                va_ref[h, rows, :] = jnp.where(lanes < d, tile, jnp.where(lanes < d + 3, 1.0, 0.0)).astype(BF)
            return c
        lax.fori_loop(0, nb, fill, 0)

    rows_i = pl.ds(pl.multiple_of(i * bq, bq), bq)
    grad_o = dot(gh_ref[...], wo_ref[...], NT).astype(BF)
    grad_t = grad_o.T
    q_nat = qkv_ref[rows_i, 0:width]
    qt = q_nat.T
    lanes = lax.broadcasted_iota(jnp.int32, (bq, 128), 1)
    queries, grads, q_pair, g_pair = [], [], [], []
    for h in range(heads):
        hs = slice(h * d, (h + 1) * d)
        delta = jnp.sum(grad_t[hs].astype(F32) * ot_ref[hs, :], axis=0, keepdims=True)
        queries.append(jnp.concatenate(
            [qt[hs], stack_rows((128 - d, bq), (1.0, 1.0, 1.0) + three(-lse_ref[0, h:h + 1, :]))], axis=0))
        grads.append(jnp.concatenate([grad_t[hs], stack_rows((128 - d, bq), three(-delta))], axis=0))
        pair = slice((h // 2) * 128, (h // 2) * 128 + 128)
        own = (lanes < d) if h % 2 == 0 else (lanes >= d)
        q_pair.append(jnp.where(own, q_nat[:, pair].astype(F32), 0.0).astype(BF))
        g_pair.append(jnp.where(own, grad_o[:, pair].astype(F32), 0.0).astype(BF))

    def block(j, carry, last):
        out = []
        kr = pl.ds(pl.multiple_of(j * bq, bq), bq)
        for h in range(heads):
            s = dot(ka_ref[h, kr, :], queries[h])
            if last:
                s = causal(s, bq, bq)
            p = jnp.exp(s)
            gs = (p * dot(va_ref[h, kr, :], grads[h])).astype(BF)
            pair = slice((h // 2) * 128, (h // 2) * 128 + 128)
            dv_ref[kr, pair] += dot(p.astype(BF), g_pair[h])
            dk_ref[kr, pair] += dot(gs, q_pair[h])
            out.append(carry[h] + dot(kt_ref[j, h * d:(h + 1) * d, :], gs))
        return tuple(out)

    carry = lax.fori_loop(0, i, lambda j, c: block(j, c, False), (jnp.zeros((d, bq), F32),) * heads)
    carry = block(i, carry, True)
    out_ref[:, 0:width] = jnp.concatenate(carry, axis=0).T.astype(BF)
    out_ref[:, width:2 * width] = dk_ref[rows_i, :].astype(BF)
    out_ref[:, 2 * width:] = dv_ref[rows_i, :].astype(BF)


def attend_back(qkv, wo, gh, ot, lse, heads, d, total_heads, bq=512):
    n, width = qkv.shape[0], heads * d
    bq = min(bq, n)
    nb = n // bq
    feats = wo.shape[1]
    back = lambda i: nb - 1 - i
    return pl.pallas_call(
        functools.partial(attend_back_kernel, heads, d, total_heads, bq),
        grid=(nb,),
        in_specs=[pl.BlockSpec(qkv.shape, lambda i: (0, 0)), pl.BlockSpec(wo.shape, lambda i: (0, 0)),
                  pl.BlockSpec((bq, feats), lambda i: (back(i), 0)), pl.BlockSpec((width, bq), lambda i: (0, back(i))),
                  pl.BlockSpec((1, heads, bq), lambda i: (back(i), 0, 0))],
        out_specs=pl.BlockSpec((bq, 3 * width), lambda i: (back(i), 0)),
        out_shape=jax.ShapeDtypeStruct((n, 3 * width), BF),
        scratch_shapes=[pltpu.VMEM((heads, n, 128), BF), pltpu.VMEM((nb, width, bq), BF),
                        pltpu.VMEM((heads, n, 128), BF), pltpu.VMEM((n, width), F32), pltpu.VMEM((n, width), F32)],
        compiler_params=pltpu.CompilerParams(vmem_limit_bytes=56 * 2**20),
        name="attend_back",
    )(qkv, wo, gh, ot, lse)


def normalize(values):
    centred = values - jnp.mean(values, axis=-1, keepdims=True)
    inverse = lax.rsqrt(jnp.mean(centred * centred, axis=-1, keepdims=True) + NORM_EPSILON)
    return (centred * inverse, inverse)


def normalize_back(incoming, normed, inverse, gain):
    scaled = incoming * gain
    return inverse * (
        scaled
        - jnp.mean(scaled, axis=-1, keepdims=True)
        - normed * jnp.mean(scaled * normed, axis=-1, keepdims=True)
    )


def over_rows(left, right):
    return lax.dot_general(
        left, right, (((0,), (0,)), ((), ())), preferred_element_type=jnp.float32
    )


def against_rows(left, right):
    return lax.dot_general(
        left, right, (((1,), (1,)), ((), ())), preferred_element_type=jnp.float32
    )


def gelu_tanh(values):
    return jax.nn.gelu(values, approximate=True)


def adam_step(master, moment, variance, gradient, rate, decay):
    moment_new = BETA_FIRST * moment + (1.0 - BETA_FIRST) * gradient
    variance_new = BETA_SECOND * variance + (1.0 - BETA_SECOND) * gradient * gradient
    moment_hat = moment_new / (1.0 - BETA_FIRST**STEP)
    variance_hat = variance_new / (1.0 - BETA_SECOND**STEP)
    master_new = master - rate * (
        moment_hat / (jnp.sqrt(variance_hat) + ADAM_EPSILON) + decay * master
    )
    return (master_new, moment_new, variance_new)


def on_device(
    tokens,
    cotangent,
    lengths,
    joint_weight,
    output_weight,
    widen_weight,
    narrow_weight,
    shared_vectors,
    split_vectors,
    joint_first,
    joint_second,
    output_first,
    output_second,
    widen_first,
    widen_second,
    narrow_first,
    narrow_second,
    shared_first,
    shared_second,
    split_first,
    split_second,
):
    gathered = (
        lax.all_gather(by_kind(joint_weight.astype(jnp.bfloat16)), "dp", axis=0, tiled=True),
        lax.all_gather(output_weight.astype(jnp.bfloat16), "dp", axis=1, tiled=True),
        lax.all_gather(widen_weight.astype(jnp.bfloat16), "dp", axis=0, tiled=True),
        lax.all_gather(narrow_weight.astype(jnp.bfloat16), "dp", axis=1, tiled=True),
        lax.all_gather(shared_vectors.astype(jnp.bfloat16), "dp", axis=1, tiled=True),
        lax.all_gather(split_vectors.astype(jnp.bfloat16), "dp", axis=1, tiled=True),
    )
    joint_work, output_work, widen_work, narrow_work, shared_work, split_work = gathered
    shared_float = shared_work.astype(jnp.float32)
    split_float = split_work.astype(jnp.float32)[0]
    head_size = D // HEADS
    head_cols = output_work.shape[0]
    local_heads = head_cols // head_size
    tensor_rank = lax.axis_index("tensor")
    widen_bias = split_float[2 * head_cols :]
    total_rows = tokens.shape[0]
    positions = jnp.arange(total_rows, dtype=jnp.int32)
    live_rows = (positions < lengths[0]).astype(jnp.float32)[:, None]
    scale = 1.0 / math.sqrt(head_size)
    qkv_bias = jnp.concatenate([split_float[:head_cols], jnp.zeros((head_cols,), F32), split_float[head_cols : 2 * head_cols]])
    qkv_scale = jnp.concatenate([jnp.full((head_cols,), scale, F32), jnp.ones((2 * head_cols,), F32)])

    inputs = tokens.astype(jnp.float32)
    normed_one, inverse_one = normalize(inputs)
    attn_input = (normed_one * shared_float[0] + shared_float[1]).astype(jnp.bfloat16)
    joint = jnp.dot(attn_input, joint_work, preferred_element_type=jnp.float32)
    qkv = ((joint + qkv_bias) * qkv_scale).astype(BF)
    attn_part, heads_out, lse = attend(qkv, output_work, local_heads, head_size, HEADS)
    attn_sum = lax.psum(attn_part, "tensor").astype(jnp.float32)
    hidden_one = inputs + attn_sum + shared_float[4]
    normed_two, inverse_two = normalize(hidden_one)
    mlp_input = (normed_two * shared_float[2] + shared_float[3]).astype(jnp.bfloat16)
    widened = jnp.dot(mlp_input, widen_work, preferred_element_type=jnp.float32) + widen_bias
    activated, gelu_pull = jax.vjp(gelu_tanh, widened)
    activated_low = activated.astype(jnp.bfloat16)
    mlp_sum = lax.psum(
        jnp.dot(activated_low, narrow_work, preferred_element_type=jnp.float32).astype(
            jnp.bfloat16
        ),
        "tensor",
    ).astype(jnp.float32)
    result = hidden_one + mlp_sum + shared_float[5]
    layer_output = (result * live_rows).astype(jnp.bfloat16)
    grad_out = cotangent.astype(jnp.float32) * live_rows
    grad_out_low = grad_out.astype(jnp.bfloat16)
    grad_narrow = over_rows(activated_low, grad_out_low)
    grad_widened = gelu_pull(against_rows(grad_out_low, narrow_work))[0].astype(jnp.bfloat16)
    grad_widen = over_rows(mlp_input, grad_widened)
    grad_mlp_in = lax.psum(
        against_rows(grad_widened, widen_work).astype(jnp.bfloat16), "tensor"
    ).astype(jnp.float32)
    grad_hidden = grad_out + normalize_back(grad_mlp_in, normed_two, inverse_two, shared_float[2])
    grad_hidden_low = grad_hidden.astype(jnp.bfloat16)
    grad_output = jnp.dot(heads_out.astype(BF), grad_hidden_low, preferred_element_type=F32)
    grad_joint_act = attend_back(
        qkv, output_work, grad_hidden_low, heads_out, lse, local_heads, head_size, HEADS
    )
    grad_qkv_bias = jnp.sum(grad_joint_act, axis=0, dtype=jnp.float32)
    grad_query_bias = grad_qkv_bias[:head_cols]
    grad_value_bias = grad_qkv_bias[2 * head_cols :]
    grad_joint = over_rows(attn_input, grad_joint_act)
    grad_attn_in = lax.psum(
        against_rows(grad_joint_act, joint_work).astype(jnp.bfloat16), "tensor"
    ).astype(jnp.float32)
    input_grad = (
        grad_hidden + normalize_back(grad_attn_in, normed_one, inverse_one, shared_float[0])
    ).astype(jnp.bfloat16)
    grad_shared = jnp.stack(
        [
            jnp.sum(grad_attn_in * normed_one, axis=0),
            jnp.sum(grad_attn_in, axis=0),
            jnp.sum(grad_mlp_in * normed_two, axis=0),
            jnp.sum(grad_mlp_in, axis=0),
            jnp.sum(grad_hidden, axis=0),
            jnp.sum(grad_out, axis=0),
        ]
    )
    grad_split = jnp.concatenate(
        [grad_query_bias, grad_value_bias, jnp.sum(grad_widened, axis=0, dtype=jnp.float32)]
    )[None]
    joint_sum, output_sum, widen_sum, narrow_sum, shared_sum, split_sum = (
        lax.psum_scatter(grad_joint.astype(BF), "dp", scatter_dimension=0, tiled=True),
        lax.psum_scatter(grad_output.astype(BF), "dp", scatter_dimension=1, tiled=True),
        lax.psum_scatter(grad_widen.astype(BF), "dp", scatter_dimension=0, tiled=True),
        lax.psum_scatter(grad_narrow.astype(BF), "dp", scatter_dimension=1, tiled=True),
        lax.psum_scatter(grad_shared, "dp", scatter_dimension=1, tiled=True),
        lax.psum_scatter(grad_split, "dp", scatter_dimension=1, tiled=True),
    )
    joint_sum, output_sum, widen_sum, narrow_sum = (
        by_head(joint_sum.astype(F32)), output_sum.astype(F32), widen_sum.astype(F32), narrow_sum.astype(F32)
    )
    local_square = jnp.sum(joint_sum * joint_sum) + jnp.sum(output_sum * output_sum)
    local_square = local_square + jnp.sum(widen_sum * widen_sum) + jnp.sum(narrow_sum * narrow_sum)
    local_square = local_square + jnp.sum(split_sum * split_sum)
    local_square = local_square + jnp.where(
        tensor_rank == 0, jnp.sum(shared_sum * shared_sum), jnp.float32(0.0)
    )
    total_square = lax.psum(local_square, ("dp", "tensor"))
    grad_norm = jnp.sqrt(total_square)
    factor = jnp.minimum(1.0, CLIP_LIMIT / (grad_norm + 1e-06))
    joint_new = adam_step(
        joint_weight, joint_first, joint_second, factor * joint_sum, MATRIX_RATE, MATRIX_DECAY
    )
    output_new = adam_step(
        output_weight, output_first, output_second, factor * output_sum, OUTPUT_RATE, MATRIX_DECAY
    )
    widen_new = adam_step(
        widen_weight, widen_first, widen_second, factor * widen_sum, MATRIX_RATE, MATRIX_DECAY
    )
    narrow_new = adam_step(
        narrow_weight, narrow_first, narrow_second, factor * narrow_sum, MATRIX_RATE, MATRIX_DECAY
    )
    shared_new = adam_step(
        shared_vectors, shared_first, shared_second, factor * shared_sum, VECTOR_RATE, 0.0
    )
    split_new = adam_step(
        split_vectors, split_first, split_second, factor * split_sum, VECTOR_RATE, 0.0
    )
    return (
        layer_output,
        input_grad,
        grad_norm,
        joint_new[0],
        joint_new[1],
        joint_new[2],
        output_new[0],
        output_new[1],
        output_new[2],
        widen_new[0],
        widen_new[1],
        widen_new[2],
        narrow_new[0],
        narrow_new[1],
        narrow_new[2],
        shared_new[0],
        shared_new[1],
        shared_new[2],
        split_new[0],
        split_new[1],
        split_new[2],
    )


def solution(mesh):
    in_specs = (
        P("dp", None),
        P("dp", None),
        P("dp"),
        P("dp", "tensor"),
        P("tensor", "dp"),
        P("dp", "tensor"),
        P("tensor", "dp"),
        P(None, "dp"),
        P("tensor", "dp"),
        P("dp", "tensor"),
        P("dp", "tensor"),
        P("tensor", "dp"),
        P("tensor", "dp"),
        P("dp", "tensor"),
        P("dp", "tensor"),
        P("tensor", "dp"),
        P("tensor", "dp"),
        P(None, "dp"),
        P(None, "dp"),
        P("tensor", "dp"),
        P("tensor", "dp"),
    )
    out_specs = (
        P("dp", None),
        P("dp", None),
        P(),
        P("dp", "tensor"),
        P("dp", "tensor"),
        P("dp", "tensor"),
        P("tensor", "dp"),
        P("tensor", "dp"),
        P("tensor", "dp"),
        P("dp", "tensor"),
        P("dp", "tensor"),
        P("dp", "tensor"),
        P("tensor", "dp"),
        P("tensor", "dp"),
        P("tensor", "dp"),
        P(None, "dp"),
        P(None, "dp"),
        P(None, "dp"),
        P("tensor", "dp"),
        P("tensor", "dp"),
        P("tensor", "dp"),
    )
    return jax.shard_map(
        on_device, mesh=mesh, in_specs=in_specs, out_specs=out_specs, check_vma=False
    )
```

```python
import functools
import math

import jax
import jax.numpy as jnp
from jax import lax
from jax.experimental import pallas as pl
from jax.experimental.pallas import tpu as pltpu
from jax.sharding import PartitionSpec as P

F32, BF = jnp.float32, jnp.bfloat16

D = 1024
HEADS = 16
STEP = 10


NORM_EPSILON = 1e-05
CLIP_LIMIT = 1.0
BETA_FIRST = 0.9
BETA_SECOND = 0.95
ADAM_EPSILON = 1e-08
MATRIX_RATE = 0.05
OUTPUT_RATE = 0.2
VECTOR_RATE = 0.6
MATRIX_DECAY = 0.1


def by_kind(values):
    rows, cols = values.shape
    size = D // HEADS
    return jnp.swapaxes(values.reshape(rows, cols // (3 * size), 3, size), 1, 2).reshape(rows, cols)


def by_head(values):
    rows, cols = values.shape
    size = D // HEADS
    return jnp.swapaxes(values.reshape(rows, 3, cols // (3 * size), size), 1, 2).reshape(rows, cols)


NN = (((1,), (0,)), ((), ()))
NT = (((1,), (1,)), ((), ()))
TN = (((0,), (0,)), ((), ()))
LOW = -1e30


def dot(left, right, dims=NN):
    return lax.dot_general(left, right, dims, preferred_element_type=F32)


def three(values):
    high = values.astype(BF).astype(F32)
    rest = values - high
    middle = rest.astype(BF).astype(F32)
    return high, middle, rest - middle


def stack_rows(shape, rows):
    ids = lax.broadcasted_iota(jnp.int32, shape, 0)
    out = jnp.zeros(shape, F32)
    for at, row in enumerate(rows):
        out = jnp.where(ids == at, row, out)
    return out.astype(BF)


def head_tile(ref, rows, col, head, d):
    lane = col + (head // 2) * 128
    tile = ref[rows, lane:lane + 128].astype(F32)
    if head % 2:
        tile = pltpu.roll(tile, 64, 1)
    return tile


def fill_keys(qkv_ref, ka_ref, heads, d, slope_of, first, count):
    rows = pl.ds(first, count)
    lanes = lax.broadcasted_iota(jnp.int32, (count, 128), 1)
    position = (lax.broadcasted_iota(jnp.int32, (count, 128), 0) + first).astype(F32)
    for head in range(heads):
        high, middle, low = three(position * slope_of(head))
        tile = head_tile(qkv_ref, rows, heads * d, head, d)
        for at, part in enumerate((high, middle, low, 1.0, 1.0, 1.0)):
            tile = jnp.where(lanes == d + at, part, tile)
        ka_ref[head, rows, :] = jnp.where(lanes < d + 6, tile, 0.0).astype(BF)


def causal(scores, bk, bq):
    kid = lax.broadcasted_iota(jnp.int32, (bk, bq), 0)
    qid = lax.broadcasted_iota(jnp.int32, (bk, bq), 1)
    return jnp.where(kid <= qid, scores, LOW)


def slope_fn(heads, total_heads):
    rank = lax.axis_index("tensor")
    def slope_of(head):
        index = jnp.full((1, 128), rank * heads + head + 1, jnp.int32).astype(F32)
        return jnp.exp2(index * (-8.0 / total_heads))
    return slope_of


def attend_kernel(heads, d, total_heads, bq, qkv_ref, wo_ref, part_ref, ot_ref, lse_ref, ka_ref, vt_ref):
    i = pl.program_id(0)
    blocks = pl.num_programs(0)
    width = heads * d

    rows_i = pl.ds(pl.multiple_of(i * bq, bq), bq)
    fill_keys(qkv_ref, ka_ref, heads, d, slope_fn(heads, total_heads), pl.multiple_of(i * bq, bq), bq)
    vt_ref[i] = qkv_ref[rows_i, 2 * width:3 * width].T
    qt = qkv_ref[rows_i, 0:width].T
    ones = stack_rows((128 - d, bq), (1.0, 1.0, 1.0))
    queries = [jnp.concatenate([qt[h * d:(h + 1) * d], ones], axis=0) for h in range(heads)]

    def block(j, carry, last):
        out = []
        kr = pl.ds(pl.multiple_of(j * bq, bq), bq)
        for h in range(heads):
            m, l, acc = carry[h]
            s = dot(ka_ref[h, kr, :], queries[h])
            if last:
                s = causal(s, bq, bq)
            top = jnp.maximum(m, jnp.max(s, axis=0, keepdims=True))
            p = jnp.exp(s - top)
            scale = jnp.exp(m - top)
            l = l * scale + jnp.sum(p, axis=0, keepdims=True)
            acc = acc * scale + dot(vt_ref[j, h * d:(h + 1) * d, :], p.astype(BF))
            out.append((top, l, acc))
        return tuple(out)

    start = (jnp.full((1, bq), LOW, F32), jnp.zeros((1, bq), F32), jnp.zeros((d, bq), F32))
    carry = lax.fori_loop(0, i, lambda j, c: block(j, c, False), (start,) * heads)
    carry = block(i, carry, True)
    for h in range(heads):
        m, l, acc = carry[h]
        ot_ref[h * d:(h + 1) * d, :] = acc / l
        lse_ref[0, h:h + 1, :] = m + jnp.log(l)
    part_ref[...] = dot(ot_ref[...].astype(BF).T, wo_ref[...], NT).astype(BF)


def attend(qkv, wo, heads, d, total_heads, bq=512):
    n, width = qkv.shape[0], heads * d
    bq = min(bq, n)
    nb = n // bq
    feats = wo.shape[0]
    return pl.pallas_call(
        functools.partial(attend_kernel, heads, d, total_heads, bq),
        grid=(nb,),
        in_specs=[pl.BlockSpec(qkv.shape, lambda i: (0, 0)), pl.BlockSpec(wo.shape, lambda i: (0, 0))],
        out_specs=[pl.BlockSpec((bq, feats), lambda i: (i, 0)), pl.BlockSpec((width, bq), lambda i: (0, i)),
                   pl.BlockSpec((1, heads, bq), lambda i: (i, 0, 0))],
        out_shape=[jax.ShapeDtypeStruct((n, feats), BF), jax.ShapeDtypeStruct((width, n), F32),
                   jax.ShapeDtypeStruct((nb, heads, bq), F32)],
        scratch_shapes=[pltpu.VMEM((heads, n, 128), BF), pltpu.VMEM((nb, width, bq), BF)],
        compiler_params=pltpu.CompilerParams(vmem_limit_bytes=48 * 2**20),
        name="attend",
    )(qkv, wo)


def attend_back_kernel(heads, d, total_heads, bq, qkv_ref, wo_ref, gh_ref, ot_ref, lse_ref, out_ref,
                       ka_ref, kt_ref, va_ref, dk_ref, dv_ref):
    g = pl.program_id(0)
    nb = pl.num_programs(0)
    i = nb - 1 - g
    width = heads * d

    @pl.when(g == 0)
    def _():
        dk_ref[...] = jnp.zeros_like(dk_ref)
        dv_ref[...] = jnp.zeros_like(dv_ref)
        lanes = lax.broadcasted_iota(jnp.int32, (bq, 128), 1)
        def fill(b, c):
            first = pl.multiple_of(b * bq, bq)
            fill_keys(qkv_ref, ka_ref, heads, d, slope_fn(heads, total_heads), first, bq)
            rows = pl.ds(first, bq)
            kt_ref[b] = (qkv_ref[rows, width:2 * width].astype(F32) * (1.0 / d ** 0.5)).astype(BF).T
            for h in range(heads):
                tile = head_tile(qkv_ref, rows, 2 * width, h, d)
                va_ref[h, rows, :] = jnp.where(lanes < d, tile, jnp.where(lanes < d + 3, 1.0, 0.0)).astype(BF)
            return c
        lax.fori_loop(0, nb, fill, 0)

    rows_i = pl.ds(pl.multiple_of(i * bq, bq), bq)
    grad_o = dot(gh_ref[...], wo_ref[...]).astype(BF)
    grad_t = grad_o.T
    q_nat = qkv_ref[rows_i, 0:width]
    qt = q_nat.T
    lanes = lax.broadcasted_iota(jnp.int32, (bq, 128), 1)
    queries, grads, q_pair, g_pair = [], [], [], []
    for h in range(heads):
        hs = slice(h * d, (h + 1) * d)
        delta = jnp.sum(grad_t[hs].astype(F32) * ot_ref[hs, :], axis=0, keepdims=True)
        queries.append(jnp.concatenate(
            [qt[hs], stack_rows((128 - d, bq), (1.0, 1.0, 1.0) + three(-lse_ref[0, h:h + 1, :]))], axis=0))
        grads.append(jnp.concatenate([grad_t[hs], stack_rows((128 - d, bq), three(-delta))], axis=0))
        pair = slice((h // 2) * 128, (h // 2) * 128 + 128)
        own = (lanes < d) if h % 2 == 0 else (lanes >= d)
        q_pair.append(jnp.where(own, q_nat[:, pair].astype(F32), 0.0).astype(BF))
        g_pair.append(jnp.where(own, grad_o[:, pair].astype(F32), 0.0).astype(BF))

    def block(j, carry, last):
        out = []
        kr = pl.ds(pl.multiple_of(j * bq, bq), bq)
        for h in range(heads):
            s = dot(ka_ref[h, kr, :], queries[h])
            if last:
                s = causal(s, bq, bq)
            p = jnp.exp(s)
            gs = (p * dot(va_ref[h, kr, :], grads[h])).astype(BF)
            pair = slice((h // 2) * 128, (h // 2) * 128 + 128)
            dv_ref[kr, pair] += dot(p.astype(BF), g_pair[h])
            dk_ref[kr, pair] += dot(gs, q_pair[h])
            out.append(carry[h] + dot(kt_ref[j, h * d:(h + 1) * d, :], gs))
        return tuple(out)

    carry = lax.fori_loop(0, i, lambda j, c: block(j, c, False), (jnp.zeros((d, bq), F32),) * heads)
    carry = block(i, carry, True)
    out_ref[:, 0:width] = jnp.concatenate(carry, axis=0).T.astype(BF)
    out_ref[:, width:2 * width] = dk_ref[rows_i, :].astype(BF)
    out_ref[:, 2 * width:] = dv_ref[rows_i, :].astype(BF)


def attend_back(qkv, wo, gh, ot, lse, heads, d, total_heads, bq=512):
    n, width = qkv.shape[0], heads * d
    bq = min(bq, n)
    nb = n // bq
    feats = wo.shape[0]
    back = lambda i: nb - 1 - i
    return pl.pallas_call(
        functools.partial(attend_back_kernel, heads, d, total_heads, bq),
        grid=(nb,),
        in_specs=[pl.BlockSpec(qkv.shape, lambda i: (0, 0)), pl.BlockSpec(wo.shape, lambda i: (0, 0)),
                  pl.BlockSpec((bq, feats), lambda i: (back(i), 0)), pl.BlockSpec((width, bq), lambda i: (0, back(i))),
                  pl.BlockSpec((1, heads, bq), lambda i: (back(i), 0, 0))],
        out_specs=pl.BlockSpec((bq, 3 * width), lambda i: (back(i), 0)),
        out_shape=jax.ShapeDtypeStruct((n, 3 * width), BF),
        scratch_shapes=[pltpu.VMEM((heads, n, 128), BF), pltpu.VMEM((nb, width, bq), BF),
                        pltpu.VMEM((heads, n, 128), BF), pltpu.VMEM((n, width), F32), pltpu.VMEM((n, width), F32)],
        compiler_params=pltpu.CompilerParams(vmem_limit_bytes=56 * 2**20),
        name="attend_back",
    )(qkv, wo, gh, ot, lse)


def at_dp(index):
    return {"dp": index}


def at_tensor(index):
    return {"tensor": index}


def remote(src, dst, send, recv, where):
    return pltpu.make_async_remote_copy(
        src_ref=src, dst_ref=dst, send_sem=send, recv_sem=recv, device_id=where, device_id_type=pl.DeviceIdType.MESH
    )


def greet(n_dp, n_tensor):
    me, rank = lax.axis_index("dp"), lax.axis_index("tensor")
    barrier = pltpu.get_barrier_semaphore()

    def along_dp(k, c):
        pl.semaphore_signal(barrier, inc=1, device_id=at_dp(lax.rem(me + k, n_dp)), device_id_type=pl.DeviceIdType.MESH)
        return c

    lax.fori_loop(1, n_dp, along_dp, 0)
    for k in range(1, n_tensor):
        pl.semaphore_signal(
            barrier, inc=1, device_id=at_tensor(lax.rem(rank + k, n_tensor)), device_id_type=pl.DeviceIdType.MESH
        )
    pl.semaphore_wait(barrier, n_dp + n_tensor - 2)


def gather_kernel(n_dp, n_tensor, cuts, shard_ref, vec_ref, out_ref, vecs_ref, own_sem, xs, xr, zs, zr, vs, vr):
    me = lax.axis_index("dp")
    lines = n_dp // 2
    z, x = me // 2, lax.rem(me, 2)
    other = at_dp(z * 2 + 1 - x)
    rows = shard_ref.shape[0]

    def place(index, cut):
        first, count = cut
        return out_ref.at[pl.ds(pl.multiple_of(index * rows, rows), rows), pl.ds(first, count)]

    def own(cut):
        first, count = cut
        return shard_ref.at[:, pl.ds(first, count)]

    def to_x(s, zz, src):
        return remote(src, place(zz * 2 + x, cuts[s]), xs.at[s, zz], xr.at[s, zz], other)

    def to_z(s, k):
        return remote(own(cuts[s]), place(me, cuts[s]), zs.at[s, k], zr.at[s, z], at_dp(lax.rem(z + k, lines) * 2 + x))

    def from_z(s, zz):
        spot = place(zz * 2 + x, cuts[s])
        return remote(spot, spot, zs.at[s, 0], zr.at[s, zz], other)

    def vec_to(k):
        return remote(vec_ref, vecs_ref.at[me], vs.at[k], vr.at[me], at_dp(lax.rem(me + k, n_dp)))

    def vec_from(source):
        return remote(vec_ref, vecs_ref.at[source], vs.at[0], vr.at[source], other)

    mine = pltpu.make_async_copy(shard_ref, out_ref.at[pl.ds(pl.multiple_of(me * rows, rows), rows)], own_sem.at[0])
    mine.start()
    mine_vec = pltpu.make_async_copy(vec_ref, vecs_ref.at[me], own_sem.at[1])
    mine_vec.start()
    greet(n_dp, n_tensor)
    count = len(cuts)

    def loop(body, first, last):
        lax.fori_loop(first, last, lambda k, c: (body(k), c)[1], 0)

    loop(lambda k: vec_to(k).start(), 1, n_dp)

    def begin(s):
        loop(lambda k: to_z(s, k).start(), 1, lines)
        to_x(s, z, own(cuts[s])).start()

    def forward(s):
        def step(k):
            zz = lax.rem(z + k, lines)
            from_z(s, zz).wait_recv()
            to_x(s, zz, place(zz * 2 + x, cuts[s])).start()
        loop(step, 1, lines)

    def sent(s):
        loop(lambda k: to_z(s, k).wait_send(), 1, lines)
        loop(lambda zz: to_x(s, zz, own(cuts[s])).wait_send(), 0, lines)

    for s in range(count):
        begin(s)
        if s:
            forward(s - 1)
    forward(count - 1)
    for s in range(count):
        sent(s)
        loop(lambda zz: to_x(s, zz, own(cuts[s])).wait_recv(), 0, lines)
    loop(lambda k: vec_to(k).wait_send(), 1, n_dp)
    loop(lambda k: vec_from(lax.rem(me + k, n_dp)).wait_recv(), 1, n_dp)
    mine.wait()
    mine_vec.wait()


def gather_weights(shard, vec, n_dp, n_tensor, cuts, collective_id):
    rows, cols = shard.shape
    lines, count = n_dp // 2, len(cuts)
    anywhere = pl.BlockSpec(memory_space=pl.ANY)
    vmem = pl.BlockSpec(memory_space=pltpu.VMEM)
    dma = pltpu.SemaphoreType.DMA
    return pl.pallas_call(
        functools.partial(gather_kernel, n_dp, n_tensor, cuts),
        in_specs=[anywhere, vmem],
        out_specs=[anywhere, vmem],
        out_shape=[jax.ShapeDtypeStruct((n_dp * rows, cols), BF), jax.ShapeDtypeStruct((n_dp,) + vec.shape, BF)],
        scratch_shapes=[dma((2,))] + [dma((count, lines))] * 4 + [dma((n_dp,))] * 2,
        compiler_params=pltpu.CompilerParams(collective_id=collective_id, has_side_effects=True),
        name="gather_weights",
    )(shard, vec)


def scatter_kernel(n_dp, n_tensor, parts, ahead, g_ref, vec_ref, total_ref, vec_out, square_out,
                   x_buf, z_buf, v_buf, q_buf, t_buf, xs, xr, zs, zr, vs, vr, qs, qr, ts, tr):
    me, rank = lax.axis_index("dp"), lax.axis_index("tensor")
    lines = n_dp // 2
    z, x = me // 2, lax.rem(me, 2)
    rows, cols = total_ref.shape
    wide = cols // parts
    items = parts * lines

    def loop(body, first, last):
        lax.fori_loop(first, last, lambda k, c: (body(k), c)[1], 0)

    def chunk(dest, part):
        return (pl.ds(pl.multiple_of(dest * rows, rows), rows), pl.ds(pl.multiple_of(part * wide, wide), wide))

    def which(item):
        return item // lines, lax.rem(z + 1 + lax.rem(item, lines), lines)

    def to_x(item):
        part, dz = which(item)
        return remote(g_ref.at[chunk(dz * 2 + 1 - x, part)], x_buf.at[part, dz], xs.at[part, dz], xr.at[part, dz],
                      at_dp(z * 2 + 1 - x))

    def to_z(part, dz):
        return remote(x_buf.at[part, dz], z_buf.at[part, z], zs.at[part, dz], zr.at[part, z], at_dp(dz * 2 + x))

    def from_z(part, zz):
        return remote(z_buf.at[part, zz], z_buf.at[part, zz], zs.at[part, zz], zr.at[part, zz], at_dp(zz * 2 + x))

    def vec_to(k):
        dest = lax.rem(me + k, n_dp)
        return remote(vec_ref.at[dest], v_buf.at[me], vs.at[k], vr.at[me], at_dp(dest))

    def square_to(k):
        return remote(q_buf.at[me], q_buf.at[me], qs.at[k], qr.at[me], at_dp(lax.rem(me + k, n_dp)))

    def tensor_to(k):
        return remote(t_buf.at[rank], t_buf.at[rank], ts.at[k], tr.at[rank], at_tensor(lax.rem(rank + k, n_tensor)))

    greet(n_dp, n_tensor)
    for item in range(min(ahead, items)):
        to_x(item).start()
    loop(lambda k: vec_to(k).start(), 1, n_dp)

    def step(item):
        part, dz = which(item)
        to_x(item).wait()
        if items > ahead:
            @pl.when(item + ahead < items)
            def _():
                to_x(item + ahead).start()
        summed = x_buf[part, dz].astype(F32) + g_ref[chunk(dz * 2 + x, part)].astype(F32)

        @pl.when(dz != z)
        def _():
            x_buf[part, dz] = summed.astype(BF)
            to_z(part, dz).start()

        @pl.when(dz == z)
        def _():
            total_ref[:, pl.ds(pl.multiple_of(part * wide, wide), wide)] = summed

    loop(step, 0, items)

    def finish(part):
        def add(k):
            zz = lax.rem(z + k, lines)
            from_z(part, zz).wait_recv()
            total_ref[:, pl.ds(pl.multiple_of(part * wide, wide), wide)] += z_buf[part, zz].astype(F32)
            to_z(part, zz).wait_send()
        loop(add, 1, lines)

    loop(finish, 0, parts)

    v_buf[me] = vec_ref[me]
    def vec_arrived(k):
        source = lax.rem(me + k, n_dp)
        remote(v_buf.at[source], v_buf.at[source], vs.at[0], vr.at[source], at_dp(source)).wait_recv()
        vec_to(k).wait_send()
    loop(vec_arrived, 1, n_dp)
    vec_total = lax.fori_loop(0, n_dp, lambda k, acc: acc + v_buf[k], jnp.zeros(vec_out.shape, F32))
    vec_out[...] = vec_total

    counted = lax.broadcasted_iota(jnp.int32, vec_out.shape, 0) >= jnp.where(rank == 0, 0, 6)
    vec_kept = jnp.where(counted, vec_total, 0.0)
    square = jnp.sum(total_ref[...] * total_ref[...]) + jnp.sum(vec_kept * vec_kept)
    q_buf[me] = jnp.full(q_buf.shape[1:], square, F32)
    loop(lambda k: square_to(k).start(), 1, n_dp)
    def square_arrived(k):
        source = lax.rem(me + k, n_dp)
        remote(q_buf.at[source], q_buf.at[source], qs.at[0], qr.at[source], at_dp(source)).wait_recv()
        square_to(k).wait_send()
    loop(square_arrived, 1, n_dp)
    t_buf[rank] = lax.fori_loop(0, n_dp, lambda k, acc: acc + q_buf[k], jnp.zeros(q_buf.shape[1:], F32))
    for k in range(1, n_tensor):
        tensor_to(k).start()
    for k in range(1, n_tensor):
        source = lax.rem(rank + k, n_tensor)
        remote(t_buf.at[source], t_buf.at[source], ts.at[0], tr.at[source], at_tensor(source)).wait_recv()
        tensor_to(k).wait_send()
    square_out[...] = lax.fori_loop(0, n_tensor, lambda k, acc: acc + t_buf[k], jnp.zeros(q_buf.shape[1:], F32))


def scatter_gradients(grads, vec, n_dp, n_tensor, collective_id, parts=4, ahead=3):
    rows, cols = grads.shape[0] // n_dp, grads.shape[1]
    lines = n_dp // 2
    vmem = pl.BlockSpec(memory_space=pltpu.VMEM)
    dma = pltpu.SemaphoreType.DMA
    wide = cols // parts
    tile = (8, 128)
    return pl.pallas_call(
        functools.partial(scatter_kernel, n_dp, n_tensor, parts, ahead),
        in_specs=[vmem, vmem],
        out_specs=[vmem, vmem, vmem],
        out_shape=[jax.ShapeDtypeStruct((rows, cols), F32), jax.ShapeDtypeStruct(vec.shape[1:], F32),
                   jax.ShapeDtypeStruct(tile, F32)],
        scratch_shapes=[pltpu.VMEM((parts, lines, rows, wide), BF), pltpu.VMEM((parts, lines, rows, wide), BF),
                        pltpu.VMEM(vec.shape, F32), pltpu.VMEM((n_dp,) + tile, F32), pltpu.VMEM((n_tensor,) + tile, F32)]
        + [dma((parts, lines))] * 4 + [dma((n_dp,))] * 4 + [dma((n_tensor,))] * 2,
        compiler_params=pltpu.CompilerParams(collective_id=collective_id, has_side_effects=True, vmem_limit_bytes=48 * 2**20),
        name="scatter_gradients",
    )(grads, vec)


def normalize(values):
    centred = values - jnp.mean(values, axis=-1, keepdims=True)
    inverse = lax.rsqrt(jnp.mean(centred * centred, axis=-1, keepdims=True) + NORM_EPSILON)
    return (centred * inverse, inverse)


def normalize_back(incoming, normed, inverse, gain):
    scaled = incoming * gain
    return inverse * (
        scaled
        - jnp.mean(scaled, axis=-1, keepdims=True)
        - normed * jnp.mean(scaled * normed, axis=-1, keepdims=True)
    )


def over_rows(left, right):
    return lax.dot_general(
        left, right, (((0,), (0,)), ((), ())), preferred_element_type=jnp.float32
    )


def against_rows(left, right):
    return lax.dot_general(
        left, right, (((1,), (1,)), ((), ())), preferred_element_type=jnp.float32
    )


def gelu_tanh(values):
    return jax.nn.gelu(values, approximate=True)


def adam_step(master, moment, variance, gradient, rate, decay):
    moment_new = BETA_FIRST * moment + (1.0 - BETA_FIRST) * gradient
    variance_new = BETA_SECOND * variance + (1.0 - BETA_SECOND) * gradient * gradient
    moment_hat = moment_new / (1.0 - BETA_FIRST**STEP)
    variance_hat = variance_new / (1.0 - BETA_SECOND**STEP)
    master_new = master - rate * (
        moment_hat / (jnp.sqrt(variance_hat) + ADAM_EPSILON) + decay * master
    )
    return (master_new, moment_new, variance_new)


def on_device(
    tokens,
    cotangent,
    lengths,
    joint_weight,
    output_weight,
    widen_weight,
    narrow_weight,
    shared_vectors,
    split_vectors,
    joint_first,
    joint_second,
    output_first,
    output_second,
    widen_first,
    widen_second,
    narrow_first,
    narrow_second,
    shared_first,
    shared_second,
    split_first,
    split_second,
):
    n_dp, n_tensor = lax.axis_size("dp"), lax.axis_size("tensor")
    sizes = (joint_weight.shape[1], widen_weight.shape[1], output_weight.shape[0], narrow_weight.shape[0])
    starts = (0, sizes[0], sizes[0] + sizes[1], sum(sizes[:3]), sum(sizes))
    spans = [slice(first, last) for first, last in zip(starts[:-1], starts[1:])]
    shard = jnp.concatenate(
        [by_kind(joint_weight), widen_weight, output_weight.T, narrow_weight.T], axis=1
    ).astype(BF)
    shared_cols, split_cols = shared_vectors.shape[1], split_vectors.shape[1]
    vec_cols = -(-max(shared_cols, split_cols) // 128) * 128
    vec_shard = jnp.concatenate(
        [
            jnp.pad(shared_vectors, ((0, 0), (0, vec_cols - shared_cols))),
            jnp.pad(split_vectors, ((0, 9), (0, vec_cols - split_cols))),
        ],
        axis=0,
    ).astype(BF)
    cuts = tuple((first, last - first) for first, last in zip(starts[:-1], starts[1:]))
    work, vecs = gather_weights(shard, vec_shard, n_dp, n_tensor, cuts, 0)
    joint_work, widen_work, output_t, narrow_t = [work[:, span] for span in spans]
    shared_float = jnp.swapaxes(vecs[:, :6, :shared_cols], 0, 1).reshape(6, D).astype(F32)
    split_float = vecs[:, 6, :split_cols].reshape(-1).astype(F32)
    head_size = D // HEADS
    head_cols = sizes[2]
    local_heads = head_cols // head_size
    tensor_rank = lax.axis_index("tensor")
    widen_bias = split_float[2 * head_cols :]
    total_rows = tokens.shape[0]
    positions = jnp.arange(total_rows, dtype=jnp.int32)
    live_rows = (positions < lengths[0]).astype(jnp.float32)[:, None]
    scale = 1.0 / math.sqrt(head_size)
    qkv_bias = jnp.concatenate([split_float[:head_cols], jnp.zeros((head_cols,), F32), split_float[head_cols : 2 * head_cols]])
    qkv_scale = jnp.concatenate([jnp.full((head_cols,), scale, F32), jnp.ones((2 * head_cols,), F32)])

    inputs = tokens.astype(jnp.float32)
    normed_one, inverse_one = normalize(inputs)
    attn_input = (normed_one * shared_float[0] + shared_float[1]).astype(jnp.bfloat16)
    joint = jnp.dot(attn_input, joint_work, preferred_element_type=jnp.float32)
    qkv = ((joint + qkv_bias) * qkv_scale).astype(BF)
    attn_part, heads_out, lse = attend(qkv, output_t, local_heads, head_size, HEADS)
    attn_sum = lax.psum(attn_part, "tensor").astype(jnp.float32)
    hidden_one = inputs + attn_sum + shared_float[4]
    normed_two, inverse_two = normalize(hidden_one)
    mlp_input = (normed_two * shared_float[2] + shared_float[3]).astype(jnp.bfloat16)
    widened = jnp.dot(mlp_input, widen_work, preferred_element_type=jnp.float32) + widen_bias
    activated, gelu_pull = jax.vjp(gelu_tanh, widened)
    activated_low = activated.astype(jnp.bfloat16)
    mlp_sum = lax.psum(
        against_rows(activated_low, narrow_t).astype(
            jnp.bfloat16
        ),
        "tensor",
    ).astype(jnp.float32)
    result = hidden_one + mlp_sum + shared_float[5]
    layer_output = (result * live_rows).astype(jnp.bfloat16)
    grad_out = cotangent.astype(jnp.float32) * live_rows
    grad_out_low = grad_out.astype(jnp.bfloat16)
    grad_narrow = over_rows(grad_out_low, activated_low)
    grad_widened = gelu_pull(jnp.dot(grad_out_low, narrow_t, preferred_element_type=F32))[0].astype(jnp.bfloat16)
    grad_widen = over_rows(mlp_input, grad_widened)
    grad_mlp_in = lax.psum(
        against_rows(grad_widened, widen_work).astype(jnp.bfloat16), "tensor"
    ).astype(jnp.float32)
    grad_hidden = grad_out + normalize_back(grad_mlp_in, normed_two, inverse_two, shared_float[2])
    grad_hidden_low = grad_hidden.astype(jnp.bfloat16)
    grad_output = lax.dot_general(
        grad_hidden_low, heads_out.astype(BF), (((0,), (1,)), ((), ())), preferred_element_type=F32
    )
    grad_joint_act = attend_back(
        qkv, output_t, grad_hidden_low, heads_out, lse, local_heads, head_size, HEADS
    )
    grad_qkv_bias = jnp.sum(grad_joint_act, axis=0, dtype=jnp.float32)
    grad_query_bias = grad_qkv_bias[:head_cols]
    grad_value_bias = grad_qkv_bias[2 * head_cols :]
    grad_joint = over_rows(attn_input, grad_joint_act)
    grad_attn_in = lax.psum(
        against_rows(grad_joint_act, joint_work).astype(jnp.bfloat16), "tensor"
    ).astype(jnp.float32)
    input_grad = (
        grad_hidden + normalize_back(grad_attn_in, normed_one, inverse_one, shared_float[0])
    ).astype(jnp.bfloat16)
    grad_shared = jnp.stack(
        [
            jnp.sum(grad_attn_in * normed_one, axis=0),
            jnp.sum(grad_attn_in, axis=0),
            jnp.sum(grad_mlp_in * normed_two, axis=0),
            jnp.sum(grad_mlp_in, axis=0),
            jnp.sum(grad_hidden, axis=0),
            jnp.sum(grad_out, axis=0),
        ]
    )
    grad_split = jnp.concatenate(
        [grad_query_bias, grad_value_bias, jnp.sum(grad_widened, axis=0, dtype=jnp.float32)]
    )
    grads = jnp.concatenate(
        [part.astype(BF) for part in (grad_joint, grad_widen, grad_output, grad_narrow)], axis=1
    )
    grad_vecs = jnp.concatenate(
        [
            jnp.pad(
                jnp.swapaxes(grad_shared.reshape(6, n_dp, shared_cols), 0, 1),
                ((0, 0), (0, 0), (0, vec_cols - shared_cols)),
            ),
            jnp.pad(grad_split.reshape(n_dp, 1, split_cols), ((0, 0), (0, 1), (0, vec_cols - split_cols))),
        ],
        axis=1,
    )
    grad_sum, vec_sum, square = scatter_gradients(grads, grad_vecs, n_dp, n_tensor, 1)
    joint_sum = by_head(grad_sum[:, spans[0]])
    widen_sum = grad_sum[:, spans[1]]
    output_sum = grad_sum[:, spans[2]].T
    narrow_sum = grad_sum[:, spans[3]].T
    shared_sum = vec_sum[:6, :shared_cols]
    split_sum = vec_sum[6:7, :split_cols]
    grad_norm = jnp.sqrt(square[0, 0])
    factor = jnp.minimum(1.0, CLIP_LIMIT / (grad_norm + 1e-06))
    joint_new = adam_step(
        joint_weight, joint_first, joint_second, factor * joint_sum, MATRIX_RATE, MATRIX_DECAY
    )
    output_new = adam_step(
        output_weight, output_first, output_second, factor * output_sum, OUTPUT_RATE, MATRIX_DECAY
    )
    widen_new = adam_step(
        widen_weight, widen_first, widen_second, factor * widen_sum, MATRIX_RATE, MATRIX_DECAY
    )
    narrow_new = adam_step(
        narrow_weight, narrow_first, narrow_second, factor * narrow_sum, MATRIX_RATE, MATRIX_DECAY
    )
    shared_new = adam_step(
        shared_vectors, shared_first, shared_second, factor * shared_sum, VECTOR_RATE, 0.0
    )
    split_new = adam_step(
        split_vectors, split_first, split_second, factor * split_sum, VECTOR_RATE, 0.0
    )
    return (
        layer_output,
        input_grad,
        grad_norm,
        joint_new[0],
        joint_new[1],
        joint_new[2],
        output_new[0],
        output_new[1],
        output_new[2],
        widen_new[0],
        widen_new[1],
        widen_new[2],
        narrow_new[0],
        narrow_new[1],
        narrow_new[2],
        shared_new[0],
        shared_new[1],
        shared_new[2],
        split_new[0],
        split_new[1],
        split_new[2],
    )


def solution(mesh):
    in_specs = (
        P("dp", None),
        P("dp", None),
        P("dp"),
        P("dp", "tensor"),
        P("tensor", "dp"),
        P("dp", "tensor"),
        P("tensor", "dp"),
        P(None, "dp"),
        P("tensor", "dp"),
        P("dp", "tensor"),
        P("dp", "tensor"),
        P("tensor", "dp"),
        P("tensor", "dp"),
        P("dp", "tensor"),
        P("dp", "tensor"),
        P("tensor", "dp"),
        P("tensor", "dp"),
        P(None, "dp"),
        P(None, "dp"),
        P("tensor", "dp"),
        P("tensor", "dp"),
    )
    out_specs = (
        P("dp", None),
        P("dp", None),
        P(),
        P("dp", "tensor"),
        P("dp", "tensor"),
        P("dp", "tensor"),
        P("tensor", "dp"),
        P("tensor", "dp"),
        P("tensor", "dp"),
        P("dp", "tensor"),
        P("dp", "tensor"),
        P("dp", "tensor"),
        P("tensor", "dp"),
        P("tensor", "dp"),
        P("tensor", "dp"),
        P(None, "dp"),
        P(None, "dp"),
        P(None, "dp"),
        P("tensor", "dp"),
        P("tensor", "dp"),
        P("tensor", "dp"),
    )
    return jax.shard_map(
        on_device, mesh=mesh, in_specs=in_specs, out_specs=out_specs, check_vma=False
    )
```

```python
import functools
import math

import jax
import jax.numpy as jnp
from jax import lax
from jax.experimental import pallas as pl
from jax.experimental.pallas import tpu as pltpu
from jax.sharding import PartitionSpec as P

F32, BF = jnp.float32, jnp.bfloat16

D = 1024
HEADS = 16
STEP = 10


NORM_EPSILON = 1e-05
CLIP_LIMIT = 1.0
BETA_FIRST = 0.9
BETA_SECOND = 0.95
ADAM_EPSILON = 1e-08
MATRIX_RATE = 0.05
OUTPUT_RATE = 0.2
VECTOR_RATE = 0.6
MATRIX_DECAY = 0.1


def by_kind(values):
    rows, cols = values.shape
    size = D // HEADS
    return jnp.swapaxes(values.reshape(rows, cols // (3 * size), 3, size), 1, 2).reshape(rows, cols)


def by_head(values):
    rows, cols = values.shape
    size = D // HEADS
    return jnp.swapaxes(values.reshape(rows, 3, cols // (3 * size), size), 1, 2).reshape(rows, cols)


NN = (((1,), (0,)), ((), ()))
NT = (((1,), (1,)), ((), ()))
TN = (((0,), (0,)), ((), ()))
LOW = -1e30


def dot(left, right, dims=NN):
    return lax.dot_general(left, right, dims, preferred_element_type=F32)


def three(values):
    high = values.astype(BF).astype(F32)
    rest = values - high
    middle = rest.astype(BF).astype(F32)
    return high, middle, rest - middle


def stack_rows(shape, rows):
    ids = lax.broadcasted_iota(jnp.int32, shape, 0)
    out = jnp.zeros(shape, F32)
    for at, row in enumerate(rows):
        out = jnp.where(ids == at, row, out)
    return out.astype(BF)


def head_tile(ref, rows, col, head, d):
    lane = col + (head // 2) * 128
    tile = ref[rows, lane:lane + 128].astype(F32)
    if head % 2:
        tile = pltpu.roll(tile, 64, 1)
    return tile


def fill_keys(qkv_ref, ka_ref, heads, d, slope_of, first, count):
    rows = pl.ds(first, count)
    lanes = lax.broadcasted_iota(jnp.int32, (count, 128), 1)
    position = (lax.broadcasted_iota(jnp.int32, (count, 128), 0) + first).astype(F32)
    for head in range(heads):
        high, middle, low = three(position * slope_of(head))
        tile = head_tile(qkv_ref, rows, heads * d, head, d)
        for at, part in enumerate((high, middle, low, 1.0, 1.0, 1.0)):
            tile = jnp.where(lanes == d + at, part, tile)
        ka_ref[head, rows, :] = jnp.where(lanes < d + 6, tile, 0.0).astype(BF)


def causal(scores, bk, bq):
    kid = lax.broadcasted_iota(jnp.int32, (bk, bq), 0)
    qid = lax.broadcasted_iota(jnp.int32, (bk, bq), 1)
    return jnp.where(kid <= qid, scores, LOW)


def slope_fn(heads, total_heads):
    rank = lax.axis_index("tensor")
    def slope_of(head):
        index = jnp.full((1, 128), rank * heads + head + 1, jnp.int32).astype(F32)
        return jnp.exp2(index * (-8.0 / total_heads))
    return slope_of


def at_dp(index):
    return {"dp": index}


def at_tensor(index):
    return {"tensor": index}


def remote(src, dst, send, recv, where):
    return pltpu.make_async_remote_copy(
        src_ref=src, dst_ref=dst, send_sem=send, recv_sem=recv, device_id=where, device_id_type=pl.DeviceIdType.MESH
    )


def greet(n_dp, n_tensor):
    me, rank = lax.axis_index("dp"), lax.axis_index("tensor")
    barrier = pltpu.get_barrier_semaphore()

    def along_dp(k, c):
        pl.semaphore_signal(barrier, inc=1, device_id=at_dp(lax.rem(me + k, n_dp)), device_id_type=pl.DeviceIdType.MESH)
        return c

    lax.fori_loop(1, n_dp, along_dp, 0)
    for k in range(1, n_tensor):
        pl.semaphore_signal(
            barrier, inc=1, device_id=at_tensor(lax.rem(rank + k, n_tensor)), device_id_type=pl.DeviceIdType.MESH
        )
    pl.semaphore_wait(barrier, n_dp + n_tensor - 2)


def gather_kernel(n_dp, n_tensor, cuts, shard_ref, vec_ref, out_ref, vecs_ref, own_sem, xs, xr, zs, zr, vs, vr):
    me = lax.axis_index("dp")
    lines = n_dp // 2
    z, x = me // 2, lax.rem(me, 2)
    other = at_dp(z * 2 + 1 - x)
    rows = shard_ref.shape[0]

    def place(index, cut):
        first, count = cut
        return out_ref.at[pl.ds(pl.multiple_of(index * rows, rows), rows), pl.ds(first, count)]

    def own(cut):
        first, count = cut
        return shard_ref.at[:, pl.ds(first, count)]

    def to_x(s, zz, src):
        return remote(src, place(zz * 2 + x, cuts[s]), xs.at[s, zz], xr.at[s, zz], other)

    def to_z(s, k):
        return remote(own(cuts[s]), place(me, cuts[s]), zs.at[s, k], zr.at[s, z], at_dp(lax.rem(z + k, lines) * 2 + x))

    def from_z(s, zz):
        spot = place(zz * 2 + x, cuts[s])
        return remote(spot, spot, zs.at[s, 0], zr.at[s, zz], other)

    def vec_to(k):
        return remote(vec_ref, vecs_ref.at[me], vs.at[k], vr.at[me], at_dp(lax.rem(me + k, n_dp)))

    def vec_from(source):
        return remote(vec_ref, vecs_ref.at[source], vs.at[0], vr.at[source], other)

    mine = pltpu.make_async_copy(shard_ref, out_ref.at[pl.ds(pl.multiple_of(me * rows, rows), rows)], own_sem.at[0])
    mine.start()
    mine_vec = pltpu.make_async_copy(vec_ref, vecs_ref.at[me], own_sem.at[1])
    mine_vec.start()
    greet(n_dp, n_tensor)
    count = len(cuts)

    def loop(body, first, last):
        lax.fori_loop(first, last, lambda k, c: (body(k), c)[1], 0)

    loop(lambda k: vec_to(k).start(), 1, n_dp)

    def begin(s):
        loop(lambda k: to_z(s, k).start(), 1, lines)
        to_x(s, z, own(cuts[s])).start()

    def forward(s):
        def step(k):
            zz = lax.rem(z + k, lines)
            from_z(s, zz).wait_recv()
            to_x(s, zz, place(zz * 2 + x, cuts[s])).start()
        loop(step, 1, lines)

    def sent(s):
        loop(lambda k: to_z(s, k).wait_send(), 1, lines)
        loop(lambda zz: to_x(s, zz, own(cuts[s])).wait_send(), 0, lines)

    for s in range(count):
        begin(s)
        if s:
            forward(s - 1)
    forward(count - 1)
    for s in range(count):
        sent(s)
        loop(lambda zz: to_x(s, zz, own(cuts[s])).wait_recv(), 0, lines)
    loop(lambda k: vec_to(k).wait_send(), 1, n_dp)
    loop(lambda k: vec_from(lax.rem(me + k, n_dp)).wait_recv(), 1, n_dp)
    mine.wait()
    mine_vec.wait()


def gather_weights(shard, vec, n_dp, n_tensor, cuts, collective_id):
    rows, cols = shard.shape
    lines, count = n_dp // 2, len(cuts)
    anywhere = pl.BlockSpec(memory_space=pl.ANY)
    vmem = pl.BlockSpec(memory_space=pltpu.VMEM)
    dma = pltpu.SemaphoreType.DMA
    return pl.pallas_call(
        functools.partial(gather_kernel, n_dp, n_tensor, cuts),
        in_specs=[anywhere, vmem],
        out_specs=[anywhere, vmem],
        out_shape=[jax.ShapeDtypeStruct((n_dp * rows, cols), BF), jax.ShapeDtypeStruct((n_dp,) + vec.shape, BF)],
        scratch_shapes=[dma((2,))] + [dma((count, lines))] * 4 + [dma((n_dp,))] * 2,
        compiler_params=pltpu.CompilerParams(collective_id=collective_id, has_side_effects=True),
        name="gather_weights",
    )(shard, vec)


def over(body, first, last):
    lax.fori_loop(first, last, lambda k, c: (body(k), c)[1], 0)


def greet_tensor(n_tensor):
    rank = lax.axis_index("tensor")
    barrier = pltpu.get_barrier_semaphore()
    for k in range(1, n_tensor):
        pl.semaphore_signal(
            barrier, inc=1, device_id=at_tensor(lax.rem(rank + k, n_tensor)), device_id_type=pl.DeviceIdType.MESH
        )
    pl.semaphore_wait(barrier, n_tensor - 1)


class Place:
    def __init__(self):
        rank = lax.axis_index("tensor")
        self.far, self.near = rank // 2, lax.rem(rank, 2)
        self.near_device = at_tensor(self.far * 2 + 1 - self.near)
        self.far_device = at_tensor((1 - self.far) * 2 + self.near)


class BlockSum:
    def __init__(self, place, quarter, part, near_buf, send_buf, far_buf, sems):
        self.place, self.quarter, self.part = place, quarter, part
        self.near_buf, self.send_buf, self.far_buf = near_buf, send_buf, far_buf
        self.sems = sems

    def rows(self, near, far):
        first = (near * 2 + far) * self.quarter
        return pl.ds(pl.multiple_of(first, self.quarter), self.quarter)

    def half(self, near):
        first = near * 2 * self.quarter
        return pl.ds(pl.multiple_of(first, self.quarter), 2 * self.quarter)

    def to_near(self, b):
        return remote(self.part.at[b, self.half(1 - self.place.near)], self.near_buf.at[b],
                      self.sems.at[0, b], self.sems.at[1, b], self.place.near_device)

    def to_far(self, b):
        return remote(self.send_buf.at[b], self.far_buf.at[b], self.sems.at[2, b], self.sems.at[3, b],
                      self.place.far_device)

    def own(self, b, far):
        return self.part[b, self.rows(self.place.near, far)].astype(F32)

    def begin(self, b):
        self.to_near(b).start()

    def pass_on(self, b):
        far = self.place.far
        self.to_near(b).wait_recv()
        taken = self.near_buf[b, self.rows(0, 1 - far)].astype(F32)
        self.send_buf[b] = (self.own(b, 1 - far) + taken).astype(BF)
        self.to_far(b).start()

    def total(self, b):
        far = self.place.far
        self.to_far(b).wait_recv()
        return self.own(b, far) + self.near_buf[b, self.rows(0, far)].astype(F32) + self.far_buf[b].astype(F32)

    def finish(self, b):
        self.to_near(b).wait_send()
        self.to_far(b).wait_send()


class HalfSum(BlockSum):
    def __init__(self, place, quarter, whole, block, part, near_buf, send_buf, far_buf, sems):
        super().__init__(place, quarter, part, near_buf, send_buf, far_buf, sems)
        self.whole, self.block = whole, block

    def from_block(self, b, near):
        first = b * self.block + near * 2 * self.quarter
        return self.whole.at[pl.ds(pl.multiple_of(first, self.quarter), 2 * self.quarter)]

    def to_near(self, b):
        return remote(self.from_block(b, 1 - self.place.near), self.near_buf.at[b],
                      self.sems.at[0, b], self.sems.at[1, b], self.place.near_device)

    def load(self, b):
        return pltpu.make_async_copy(self.from_block(b, self.place.near), self.part.at[b], self.sems.at[4, b])

    def own(self, b, far):
        return self.part[b, self.rows(0, far)].astype(F32)

    def begin(self, b):
        self.to_near(b).start()
        self.load(b).start()

    def pass_on(self, b):
        self.load(b).wait()
        super().pass_on(b)


class BlockSpread:
    def __init__(self, place, quarter, own, out, sems):
        self.place, self.quarter, self.own, self.out, self.sems = place, quarter, own, out, sems

    def spot(self, b, near, far):
        first = (b * 4 + near * 2 + far) * self.quarter
        return self.out.at[pl.ds(pl.multiple_of(first, self.quarter), self.quarter)]

    def mine(self, b):
        return self.spot(b, self.place.near, self.place.far)

    def to_far(self, b):
        return remote(self.own.at[b], self.mine(b), self.sems.at[0, b], self.sems.at[1, b], self.place.far_device)

    def to_near(self, b):
        return remote(self.own.at[b], self.mine(b), self.sems.at[2, b], self.sems.at[3, b], self.place.near_device)

    def arrival(self, near, far, b, at):
        spot = self.spot(b, near, far)
        return remote(spot, spot, self.sems.at[at - 1, b], self.sems.at[at, b], self.place.near_device)

    def pass_far(self, b):
        spot = self.spot(b, self.place.near, 1 - self.place.far)
        return remote(spot, spot, self.sems.at[4, b], self.sems.at[5, b], self.place.near_device)

    def keep(self, b):
        return pltpu.make_async_copy(self.own.at[b], self.mine(b), self.sems.at[6, b])

    def begin(self, b):
        self.to_far(b).start()
        self.to_near(b).start()
        self.keep(b).start()

    def relay(self, b):
        self.arrival(self.place.near, 1 - self.place.far, b, 1).wait_recv()
        self.pass_far(b).start()

    def finish(self, b):
        self.to_far(b).wait_send()
        self.to_near(b).wait_send()
        self.pass_far(b).wait_send()
        self.keep(b).wait()
        self.arrival(1 - self.place.near, self.place.far, b, 3).wait_recv()
        self.arrival(1 - self.place.near, 1 - self.place.far, b, 5).wait_recv()


def normalize(values):
    centred = values - jnp.mean(values, axis=-1, keepdims=True)
    inverse = lax.rsqrt(jnp.mean(centred * centred, axis=-1, keepdims=True) + NORM_EPSILON)
    return (centred * inverse, inverse)


def normalize_back(incoming, normed, inverse, gain):
    scaled = incoming * gain
    return inverse * (
        scaled
        - jnp.mean(scaled, axis=-1, keepdims=True)
        - normed * jnp.mean(scaled * normed, axis=-1, keepdims=True)
    )


def column_sum(values):
    return jnp.sum(values, axis=0, keepdims=True)


def params(collective_id, megabytes):
    return pltpu.CompilerParams(
        collective_id=collective_id, has_side_effects=True, vmem_limit_bytes=megabytes * 2**20
    )


ANYWHERE = pl.BlockSpec(memory_space=pl.ANY)


def whole(array):
    return pl.BlockSpec(array.shape, lambda i: (0,) * array.ndim)


def attend_kernel(heads, d, total_heads, bq, nb, n_tensor, qkv_ref, wo_ref, tok_ref, vec_ref, ot_ref, lse_ref, h1_ref,
                  c_ref, ka_ref, vt_ref, part_ref, near_buf, send_buf, far_buf, own_buf, sum_sems, spread_sems):
    i = pl.program_id(0)
    width = heads * d
    place = Place()
    quarter = bq // 4
    summing = BlockSum(place, quarter, part_ref, near_buf, send_buf, far_buf, sum_sems)
    spread = BlockSpread(place, quarter, own_buf, c_ref, spread_sems)

    @pl.when(i == 0)
    def _():
        greet_tensor(n_tensor)

    def norm_block(b):
        hidden = tok_ref[b].astype(F32) + summing.total(b) + vec_ref[4:5, :]
        h1_ref[b] = hidden
        normed, _ = normalize(hidden)
        own_buf[b] = (normed * vec_ref[2:3, :] + vec_ref[3:4, :]).astype(BF)
        spread.begin(b)

    rows_i = pl.ds(pl.multiple_of(i * bq, bq), bq)
    fill_keys(qkv_ref, ka_ref, heads, d, slope_fn(heads, total_heads), pl.multiple_of(i * bq, bq), bq)
    vt_ref[i] = qkv_ref[rows_i, 2 * width:3 * width].T
    qt = qkv_ref[rows_i, 0:width].T
    ones = stack_rows((128 - d, bq), (1.0, 1.0, 1.0))
    queries = [jnp.concatenate([qt[h * d:(h + 1) * d], ones], axis=0) for h in range(heads)]

    def block(j, carry, last):
        out = []
        kr = pl.ds(pl.multiple_of(j * bq, bq), bq)
        for h in range(heads):
            m, l, acc = carry[h]
            s = dot(ka_ref[h, kr, :], queries[h])
            if last:
                s = causal(s, bq, bq)
            top = jnp.maximum(m, jnp.max(s, axis=0, keepdims=True))
            p = jnp.exp(s - top)
            scale = jnp.exp(m - top)
            l = l * scale + jnp.sum(p, axis=0, keepdims=True)
            acc = acc * scale + dot(vt_ref[j, h * d:(h + 1) * d, :], p.astype(BF))
            out.append((top, l, acc))
        return tuple(out)

    start = (jnp.full((1, bq), LOW, F32), jnp.zeros((1, bq), F32), jnp.zeros((d, bq), F32))
    carry = lax.fori_loop(0, i, lambda j, c: block(j, c, False), (start,) * heads)

    @pl.when(i >= 1)
    def _():
        summing.pass_on(i - 1)

    @pl.when(i >= 2)
    def _():
        norm_block(i - 2)

    @pl.when(i >= 3)
    def _():
        spread.relay(i - 3)

    carry = block(i, carry, True)
    for h in range(heads):
        m, l, acc = carry[h]
        ot_ref[h * d:(h + 1) * d, :] = acc / l
        lse_ref[0, h:h + 1, :] = m + jnp.log(l)
    part_ref[i] = dot(ot_ref[...].astype(BF).T, wo_ref[...], NT).astype(BF)
    summing.begin(i)

    @pl.when(i == nb - 1)
    def _():
        summing.pass_on(nb - 1)
        if nb >= 2:
            norm_block(nb - 2)
        if nb >= 3:
            spread.relay(nb - 3)
        norm_block(nb - 1)
        if nb >= 2:
            spread.relay(nb - 2)
        spread.relay(nb - 1)

        def close(b):
            summing.finish(b)
            spread.finish(b)

        over(close, 0, nb)


def sum_scratch(nb, quarter, feats):
    return [pltpu.VMEM((nb, 2 * quarter, feats), BF), pltpu.VMEM((nb, quarter, feats), BF),
            pltpu.VMEM((nb, quarter, feats), BF)]


def attend(qkv, wo, tok_own, vec, heads, d, total_heads, bq, n_tensor, collective_id):
    n, width = qkv.shape[0], heads * d
    nb = n // bq
    feats = wo.shape[0]
    quarter = bq // 4
    own = (nb, quarter, feats)
    dma = pltpu.SemaphoreType.DMA
    return pl.pallas_call(
        functools.partial(attend_kernel, heads, d, total_heads, bq, nb, n_tensor),
        grid=(nb,),
        in_specs=[whole(qkv), whole(wo), whole(tok_own), whole(vec)],
        out_specs=[pl.BlockSpec((width, bq), lambda i: (0, i)), pl.BlockSpec((1, heads, bq), lambda i: (i, 0, 0)),
                   pl.BlockSpec(own, lambda i: (0, 0, 0)), ANYWHERE],
        out_shape=[jax.ShapeDtypeStruct((width, n), F32), jax.ShapeDtypeStruct((nb, heads, bq), F32),
                   jax.ShapeDtypeStruct(own, F32), jax.ShapeDtypeStruct((n, feats), BF)],
        scratch_shapes=[pltpu.VMEM((heads, n, 128), BF), pltpu.VMEM((nb, width, bq), BF),
                        pltpu.VMEM((nb, bq, feats), BF)] + sum_scratch(nb, quarter, feats)
        + [pltpu.VMEM(own, BF), dma((4, nb)), dma((7, nb))],
        compiler_params=params(collective_id, 56),
        name="attend",
    )(qkv, wo, tok_own, vec)


def feed_kernel(bq, nb, n_tensor, hidden_step, len_ref, c_ref, cot_ref, w1_ref, w2_ref, bias_ref, h1_ref, vec_ref,
                mlp_ref, gw1_ref, gw2_ref, gh1_ref, low_ref, gvec_ref, gbias_ref,
                acc1, acc2, gown_buf, hid_buf, slope_buf, gu_buf, part_ref, near_buf, send_buf, far_buf, own_buf,
                sum_sems, spread_sems):
    g = pl.program_id(0)
    i = nb - 1 - g
    place = Place()
    quarter = bq // 4
    summing = BlockSum(place, quarter, part_ref, near_buf, send_buf, far_buf, sum_sems)
    spread = BlockSpread(place, quarter, own_buf, low_ref, spread_sems)
    hidden = w1_ref.shape[1]

    @pl.when(g == 0)
    def _():
        greet_tensor(n_tensor)
        acc1[...] = jnp.zeros_like(acc1)
        acc2[...] = jnp.zeros_like(acc2)
        gvec_ref[...] = jnp.zeros_like(gvec_ref)
        gbias_ref[...] = jnp.zeros_like(gbias_ref)

    def norm_block(b):
        grad_c = summing.total(b)
        normed, inverse = normalize(h1_ref[b])
        grad_out = gown_buf[b].astype(F32)
        grad_h = grad_out + normalize_back(grad_c, normed, inverse, vec_ref[2:3, :])
        gh1_ref[b] = grad_h
        own_buf[b] = grad_h.astype(BF)
        spread.begin(b)
        gvec_ref[0:1, :] += column_sum(grad_c * normed)
        gvec_ref[1:2, :] += column_sum(grad_c)
        gvec_ref[2:3, :] += column_sum(grad_h)
        gvec_ref[3:4, :] += column_sum(grad_out)

    c = c_ref[...]
    row_ids = lax.broadcasted_iota(jnp.int32, (bq, 128), 0) + i * bq
    live = jnp.where(row_ids < len_ref[0], 1.0, 0.0).astype(BF)
    grad_out = cot_ref[...] * jnp.concatenate([live] * (cot_ref.shape[1] // 128), axis=1)
    cot_ref_rows = pl.ds(pl.multiple_of((place.near * 2 + place.far) * quarter, quarter), quarter)
    own_ids = lax.broadcasted_iota(jnp.int32, (quarter, 128), 0) + (place.near * 2 + place.far) * quarter + i * bq
    own_live = jnp.where(own_ids < len_ref[0], 1.0, 0.0).astype(BF)
    gown_buf[i] = cot_ref[cot_ref_rows, :] * jnp.concatenate([own_live] * (cot_ref.shape[1] // 128), axis=1)

    root = math.sqrt(2.0 / math.pi)
    for first in range(0, hidden, hidden_step):
        cols = slice(first, first + hidden_step)
        u = dot(c, w1_ref[:, cols]) + bias_ref[:, cols]
        square = u * u
        bent = jnp.tanh(root * (u + 0.044715 * (square * u)))
        half = 0.5 * (1.0 + bent)
        hid = (u * half).astype(BF)
        hid_buf[:, cols] = hid
        slope = half + 0.5 * u * (1.0 - bent * bent) * (root * (1.0 + 3 * 0.044715 * square))
        grad_u = (dot(grad_out, w2_ref[:, cols]) * slope).astype(BF)
        gu_buf[:, cols] = grad_u
        gbias_ref[:, cols] += column_sum(grad_u.astype(F32))
    part_ref[i] = dot(gu_buf[...], w1_ref[...], NT).astype(BF)
    summing.begin(i)
    mlp_ref[...] = dot(hid_buf[...], w2_ref[...], NT).astype(BF)

    @pl.when(g >= 1)
    def _():
        norm_block(i + 1)

    summing.pass_on(i)

    @pl.when(g >= 2)
    def _():
        spread.relay(i + 2)

    acc1[...] += dot(c, gu_buf[...], TN)
    acc2[...] += dot(grad_out, hid_buf[...], TN)

    @pl.when(g == nb - 1)
    def _():
        norm_block(0)
        gw1_ref[...] = acc1[...].astype(BF)
        gw2_ref[...] = acc2[...].astype(BF)
        if nb >= 2:
            spread.relay(1)
        spread.relay(0)

        def close(b):
            summing.finish(b)
            spread.finish(b)

        over(close, 0, nb)


def feed(lengths, c, cot, w1, w2, bias, h1, vec, bq, n_tensor, collective_id):
    n, feats = c.shape
    hidden = w1.shape[1]
    nb = n // bq
    quarter = bq // 4
    own = (nb, quarter, feats)
    dma = pltpu.SemaphoreType.DMA
    back = pl.BlockSpec((bq, feats), lambda i: (nb - 1 - i, 0))
    fixed = lambda shape: pl.BlockSpec(shape, lambda i: (0,) * len(shape))
    return pl.pallas_call(
        functools.partial(feed_kernel, bq, nb, n_tensor, 256),
        grid=(nb,),
        in_specs=[pl.BlockSpec(memory_space=pltpu.SMEM), back, back, whole(w1), whole(w2), whole(bias), whole(h1), whole(vec)],
        out_specs=[back, fixed((feats, hidden)), fixed((feats, hidden)), fixed(own), ANYWHERE, fixed((8, feats)),
                   fixed((1, hidden))],
        out_shape=[jax.ShapeDtypeStruct((n, feats), BF), jax.ShapeDtypeStruct((feats, hidden), BF),
                   jax.ShapeDtypeStruct((feats, hidden), BF), jax.ShapeDtypeStruct(own, F32),
                   jax.ShapeDtypeStruct((n, feats), BF), jax.ShapeDtypeStruct((8, feats), F32),
                   jax.ShapeDtypeStruct((1, hidden), F32)],
        scratch_shapes=[pltpu.VMEM((feats, hidden), F32), pltpu.VMEM((feats, hidden), F32), pltpu.VMEM(own, BF),
                        pltpu.VMEM((bq, hidden), BF), pltpu.VMEM((8, 128), F32), pltpu.VMEM((bq, hidden), BF),
                        pltpu.VMEM((nb, bq, feats), BF)] + sum_scratch(nb, quarter, feats)
        + [pltpu.VMEM(own, BF), dma((4, nb)), dma((7, nb))],
        compiler_params=params(collective_id, 62),
        name="feed",
    )(lengths, c, cot, w1, w2, bias, h1, vec)


def attend_back_kernel(heads, d, total_heads, bq, nb, n_tensor, len_ref, qkv_ref, wo_ref, wj_ref, gh_ref, a_ref, ot_ref,
                       lse_ref, tok_ref, gh1_ref, h1_ref, vec_ref, mlp_ref,
                       gj_ref, go_ref, in_ref, lay_ref, gvec_ref, gbias_ref,
                       ka_ref, kt_ref, va_ref, dk_ref, dv_ref, gqkv_buf, accj, acco,
                       part_ref, near_buf, send_buf, far_buf, half_buf, near2_buf, send2_buf, far2_buf,
                       sum_sems, sum2_sems):
    g = pl.program_id(0)
    i = nb - 1 - g
    width = heads * d
    place = Place()
    quarter = bq // 4
    summing = BlockSum(place, quarter, part_ref, near_buf, send_buf, far_buf, sum_sems)
    second = HalfSum(place, quarter, mlp_ref, bq, half_buf, near2_buf, send2_buf, far2_buf, sum2_sems)

    def layer_block(b):
        first = (b * 4 + place.near * 2 + place.far) * quarter
        ids = lax.broadcasted_iota(jnp.int32, (quarter, 1), 0) + first
        result = h1_ref[b] + second.total(b) + vec_ref[5:6, :]
        lay_ref[b] = jnp.where(ids < len_ref[0], result, 0.0).astype(BF)

    def norm_block(b):
        grad_a = summing.total(b)
        normed, inverse = normalize(tok_ref[b].astype(F32))
        in_ref[b] = (gh1_ref[b] + normalize_back(grad_a, normed, inverse, vec_ref[0:1, :])).astype(BF)
        gvec_ref[0:1, :] += column_sum(grad_a * normed)
        gvec_ref[1:2, :] += column_sum(grad_a)

    @pl.when(g == 0)
    def _():
        greet_tensor(n_tensor)
        over(second.begin, 0, nb)
        for ref in (dk_ref, dv_ref, accj, acco, gvec_ref, gbias_ref):
            ref[...] = jnp.zeros_like(ref)
        lanes = lax.broadcasted_iota(jnp.int32, (bq, 128), 1)

        def fill(b):
            first = pl.multiple_of(b * bq, bq)
            fill_keys(qkv_ref, ka_ref, heads, d, slope_fn(heads, total_heads), first, bq)
            rows = pl.ds(first, bq)
            kt_ref[b] = (qkv_ref[rows, width:2 * width].astype(F32) * (1.0 / d**0.5)).astype(BF).T
            for h in range(heads):
                tile = head_tile(qkv_ref, rows, 2 * width, h, d)
                va_ref[h, rows, :] = jnp.where(lanes < d, tile, jnp.where(lanes < d + 3, 1.0, 0.0)).astype(BF)

        over(fill, 0, nb)
        over(second.pass_on, 0, nb)

    rows_i = pl.ds(pl.multiple_of(i * bq, bq), bq)
    grad_o = dot(gh_ref[...], wo_ref[...]).astype(BF)
    grad_t = grad_o.T
    q_nat = qkv_ref[rows_i, 0:width]
    qt = q_nat.T
    lanes = lax.broadcasted_iota(jnp.int32, (bq, 128), 1)
    queries, grads, q_pair, g_pair = [], [], [], []
    for h in range(heads):
        hs = slice(h * d, (h + 1) * d)
        delta = jnp.sum(grad_t[hs].astype(F32) * ot_ref[hs, :], axis=0, keepdims=True)
        queries.append(jnp.concatenate(
            [qt[hs], stack_rows((128 - d, bq), (1.0, 1.0, 1.0) + three(-lse_ref[0, h:h + 1, :]))], axis=0))
        grads.append(jnp.concatenate([grad_t[hs], stack_rows((128 - d, bq), three(-delta))], axis=0))
        pair = slice((h // 2) * 128, (h // 2) * 128 + 128)
        mine = (lanes < d) if h % 2 == 0 else (lanes >= d)
        q_pair.append(jnp.where(mine, q_nat[:, pair].astype(F32), 0.0).astype(BF))
        g_pair.append(jnp.where(mine, grad_o[:, pair].astype(F32), 0.0).astype(BF))

    def block(j, carry, last):
        out = []
        kr = pl.ds(pl.multiple_of(j * bq, bq), bq)
        for h in range(heads):
            s = dot(ka_ref[h, kr, :], queries[h])
            if last:
                s = causal(s, bq, bq)
            p = jnp.exp(s)
            gs = (p * dot(va_ref[h, kr, :], grads[h])).astype(BF)
            pair = slice((h // 2) * 128, (h // 2) * 128 + 128)
            dv_ref[kr, pair] += dot(p.astype(BF), g_pair[h])
            dk_ref[kr, pair] += dot(gs, q_pair[h])
            out.append(carry[h] + dot(kt_ref[j, h * d:(h + 1) * d, :], gs))
        return tuple(out)

    carry = lax.fori_loop(0, i, lambda j, c: block(j, c, False), (jnp.zeros((d, bq), F32),) * heads)

    @pl.when(g >= 1)
    def _():
        summing.pass_on(i + 1)

    @pl.when(g >= 2)
    def _():
        norm_block(i + 2)

    carry = block(i, carry, True)
    gqkv_buf[:, 0:width] = jnp.concatenate(carry, axis=0).T.astype(BF)
    gqkv_buf[:, width:2 * width] = dk_ref[rows_i, :].astype(BF)
    gqkv_buf[:, 2 * width:] = dv_ref[rows_i, :].astype(BF)
    part_ref[i] = dot(gqkv_buf[...], wj_ref[...], NT).astype(BF)
    summing.begin(i)
    gbias_ref[...] += column_sum(gqkv_buf[...].astype(F32))
    acco[...] += dot(ot_ref[...].astype(BF), gh_ref[...])
    accj[...] += dot(a_ref[...], gqkv_buf[...], TN)
    layer_block(i)

    @pl.when(g == nb - 1)
    def _():
        summing.pass_on(0)
        if nb >= 2:
            norm_block(1)
        gj_ref[...] = accj[...].astype(BF)
        go_ref[...] = acco[...].T.astype(BF)
        norm_block(0)

        def close(b):
            summing.finish(b)
            second.finish(b)

        over(close, 0, nb)


def attend_back(lengths, qkv, wo, wj, gh, a, ot, lse, tok_own, gh1, h1, vec, mlp, heads, d, total_heads, bq, n_tensor,
                collective_id):
    n, width = qkv.shape[0], heads * d
    nb = n // bq
    feats = wo.shape[0]
    quarter = bq // 4
    own = (nb, quarter, feats)
    back = lambda i: nb - 1 - i
    dma = pltpu.SemaphoreType.DMA
    fixed = lambda shape: pl.BlockSpec(shape, lambda i: (0,) * len(shape))
    rows = pl.BlockSpec((bq, feats), lambda i: (back(i), 0))
    vm = pltpu.VMEM
    return pl.pallas_call(
        functools.partial(attend_back_kernel, heads, d, total_heads, bq, nb, n_tensor),
        grid=(nb,),
        in_specs=[pl.BlockSpec(memory_space=pltpu.SMEM), whole(qkv), whole(wo), whole(wj), rows, rows,
                  pl.BlockSpec((width, bq), lambda i: (0, back(i))),
                  pl.BlockSpec((1, heads, bq), lambda i: (back(i), 0, 0)),
                  whole(tok_own), whole(gh1), whole(h1), whole(vec), ANYWHERE],
        out_specs=[fixed((feats, 3 * width)), fixed((feats, width)), fixed(own), fixed(own), fixed((8, feats)),
                   fixed((1, 3 * width))],
        out_shape=[jax.ShapeDtypeStruct((feats, 3 * width), BF), jax.ShapeDtypeStruct((feats, width), BF),
                   jax.ShapeDtypeStruct(own, BF), jax.ShapeDtypeStruct(own, BF),
                   jax.ShapeDtypeStruct((8, feats), F32), jax.ShapeDtypeStruct((1, 3 * width), F32)],
        scratch_shapes=[vm((heads, n, 128), BF), vm((nb, width, bq), BF), vm((heads, n, 128), BF), vm((n, width), F32),
                        vm((n, width), F32), vm((bq, 3 * width), BF), vm((feats, 3 * width), F32), vm((width, feats), F32),
                        vm((nb, bq, feats), BF)] + sum_scratch(nb, quarter, feats)
        + [vm((nb, 2 * quarter, feats), BF)] + sum_scratch(nb, quarter, feats)
        + [dma((4, nb)), dma((5, nb))],
        compiler_params=params(collective_id, 62),
        name="attend_back",
    )(lengths, qkv, wo, wj, gh, a, ot, lse, tok_own, gh1, h1, vec, mlp)


class Scatter:
    def __init__(self, lines, rows, source, first, cols, x_buf, z_buf, total, at, sems, part):
        me = lax.axis_index("dp")
        self.z, self.x = me // 2, lax.rem(me, 2)
        self.lines, self.rows, self.source = lines, rows, source
        self.cols, self.total_cols = pl.ds(first, cols), pl.ds(at, cols)
        self.x_buf, self.z_buf, self.total, self.sems, self.part = x_buf, z_buf, total, sems, part

    def dest(self, k):
        return lax.rem(self.z + 1 + k, self.lines)

    def chunk(self, device):
        return (pl.ds(pl.multiple_of(device * self.rows, self.rows), self.rows), self.cols)

    def sem(self, kind, index):
        return self.sems.at[kind, self.part, index]

    def to_x(self, dz):
        return remote(self.source.at[self.chunk(dz * 2 + 1 - self.x)], self.x_buf.at[dz], self.sem(0, dz),
                      self.sem(1, dz), at_dp(self.z * 2 + 1 - self.x))

    def to_z(self, dz):
        return remote(self.x_buf.at[dz], self.z_buf.at[self.z], self.sem(2, dz), self.sem(3, self.z),
                      at_dp(dz * 2 + self.x))

    def from_z(self, zz):
        return remote(self.z_buf.at[zz], self.z_buf.at[zz], self.sem(2, zz), self.sem(3, zz), at_dp(zz * 2 + self.x))

    def begin(self):
        over(lambda k: self.to_x(self.dest(k)).start(), 0, self.lines)

    def summed(self, dz):
        self.to_x(dz).wait()
        return self.x_buf[dz].astype(F32) + self.source[self.chunk(dz * 2 + self.x)].astype(F32)

    def pass_on(self):
        def step(k):
            dz = self.dest(k)
            self.x_buf[dz] = self.summed(dz).astype(BF)
            self.to_z(dz).start()

        over(step, 0, self.lines - 1)
        self.total[:, self.total_cols] = self.summed(self.z)

    def finish(self):
        def add(k):
            zz = lax.rem(self.z + k, self.lines)
            self.from_z(zz).wait_recv()
            self.total[:, self.total_cols] += self.z_buf[zz].astype(F32)
            self.to_z(zz).wait_send()

        over(add, 1, self.lines)


def scatter_kernel(n_dp, n_tensor, pieces, nb, quarter, *refs):
    arrays = max(index for index, _, _, _ in pieces) + 1
    sources, refs = refs[:arrays], refs[arrays:]
    (vec_ref, in_own, lay_own, total_ref, vec_out, square_out, in_out, lay_out), refs = refs[:8], refs[8:]
    x_bufs, refs = refs[:len(pieces)], refs[len(pieces):]
    z_bufs, refs = refs[:len(pieces)], refs[len(pieces):]
    v_buf, s_buf, q_buf, t_buf, sems, in_sems, lay_sems, vs, vr, ss, sr, qs, qr, ts, tr = refs
    me, rank = lax.axis_index("dp"), lax.axis_index("tensor")
    lines = n_dp // 2
    rows = total_ref.shape[0]
    place = Place()
    spreads = (BlockSpread(place, quarter, lay_own, lay_out, lay_sems),
               BlockSpread(place, quarter, in_own, in_out, in_sems))
    parts = [
        Scatter(lines, rows, sources[index], first, cols, x_bufs[p], z_bufs[p], total_ref, at, sems, p)
        for p, (index, first, cols, at) in enumerate(pieces)
    ]

    def vec_to(k):
        dest = lax.rem(me + k, n_dp)
        return remote(vec_ref.at[dest], v_buf.at[me], vs.at[k], vr.at[me], at_dp(dest))

    def sum_to(k):
        return remote(s_buf.at[rank], s_buf.at[rank], ss.at[k], sr.at[rank], at_tensor(lax.rem(rank + k, n_tensor)))

    def square_to(k):
        return remote(q_buf.at[me], q_buf.at[me], qs.at[k], qr.at[me], at_dp(lax.rem(me + k, n_dp)))

    def tensor_to(k):
        return remote(t_buf.at[rank], t_buf.at[rank], ts.at[k], tr.at[rank], at_tensor(lax.rem(rank + k, n_tensor)))

    def arrived(buf, source, send, recv, where):
        remote(buf.at[source], buf.at[source], send.at[0], recv.at[source], where).wait_recv()

    greet(n_dp, n_tensor)
    parts[0].begin()
    over(lambda k: vec_to(k).start(), 1, n_dp)
    v_buf[me] = vec_ref[me]
    for spread in spreads:
        over(spread.begin, 0, nb)
    for p, part in enumerate(parts):
        if p + 1 < len(parts):
            parts[p + 1].begin()
        part.pass_on()
        if p == 0:
            def vec_arrived(k):
                source = lax.rem(me + k, n_dp)
                arrived(v_buf, source, vs, vr, at_dp(source))
                vec_to(k).wait_send()

            over(vec_arrived, 1, n_dp)
            s_buf[rank] = lax.fori_loop(0, n_dp, lambda k, acc: acc + v_buf[k], jnp.zeros(vec_out.shape, F32))
            for k in range(1, n_tensor):
                sum_to(k).start()
    for k in range(1, n_tensor):
        source = lax.rem(rank + k, n_tensor)
        arrived(s_buf, source, ss, sr, at_tensor(source))
        sum_to(k).wait_send()
    shared_total = lax.fori_loop(0, n_tensor, lambda k, acc: acc + s_buf[k], jnp.zeros(vec_out.shape, F32))
    row_ids = lax.broadcasted_iota(jnp.int32, vec_out.shape, 0)
    vec_total = jnp.where(row_ids < 6, shared_total, s_buf[rank])
    vec_out[...] = vec_total
    vec_kept = jnp.where(row_ids >= jnp.where(rank == 0, 0, 6), vec_total, 0.0)
    for part in parts:
        part.finish()
    square = jnp.sum(total_ref[...] * total_ref[...]) + jnp.sum(vec_kept * vec_kept)
    q_buf[me] = jnp.full(q_buf.shape[1:], square, F32)
    over(lambda k: square_to(k).start(), 1, n_dp)

    def square_arrived(k):
        source = lax.rem(me + k, n_dp)
        arrived(q_buf, source, qs, qr, at_dp(source))
        square_to(k).wait_send()

    over(square_arrived, 1, n_dp)
    t_buf[rank] = lax.fori_loop(0, n_dp, lambda k, acc: acc + q_buf[k], jnp.zeros(q_buf.shape[1:], F32))
    for k in range(1, n_tensor):
        tensor_to(k).start()
    for spread in spreads:
        over(spread.relay, 0, nb)
    for k in range(1, n_tensor):
        source = lax.rem(rank + k, n_tensor)
        arrived(t_buf, source, ts, tr, at_tensor(source))
        tensor_to(k).wait_send()
    square_out[...] = lax.fori_loop(0, n_tensor, lambda k, acc: acc + t_buf[k], jnp.zeros(q_buf.shape[1:], F32))
    for spread in spreads:
        over(spread.finish, 0, nb)


def scatter_gradients(grads, vec, in_own, lay_own, n_dp, n_tensor, collective_id, step=512):
    rows = grads[0].shape[0] // n_dp
    lines = n_dp // 2
    pieces, at = [], 0
    for index, grad in enumerate(grads):
        cols = grad.shape[1]
        cut = step if cols % step == 0 else cols
        for first in range(0, cols, cut):
            pieces.append((index, first, cut, at))
            at += cut
    nb, quarter, feats = in_own.shape
    vmem = pl.BlockSpec(memory_space=pltpu.VMEM)
    dma = pltpu.SemaphoreType.DMA
    tile = (8, 128)
    full = jax.ShapeDtypeStruct((nb * quarter * n_tensor, feats), BF)
    bufs = [pltpu.VMEM((lines, rows, cols), BF) for _, _, cols, _ in pieces]
    return pl.pallas_call(
        functools.partial(scatter_kernel, n_dp, n_tensor, pieces, nb, quarter),
        in_specs=[vmem] * (len(grads) + 1) + [ANYWHERE] * 2,
        out_specs=[vmem, vmem, vmem, ANYWHERE, ANYWHERE],
        out_shape=[jax.ShapeDtypeStruct((rows, at), F32), jax.ShapeDtypeStruct(vec.shape[1:], F32),
                   jax.ShapeDtypeStruct(tile, F32), full, full],
        scratch_shapes=bufs + bufs + [pltpu.VMEM(vec.shape, F32), pltpu.VMEM((n_tensor,) + vec.shape[1:], F32),
                                      pltpu.VMEM((n_dp,) + tile, F32), pltpu.VMEM((n_tensor,) + tile, F32)]
        + [dma((4, len(pieces), lines)), dma((7, nb)), dma((7, nb))] + [dma((n_dp,))] * 2 + [dma((n_tensor,))] * 2
        + [dma((n_dp,))] * 2 + [dma((n_tensor,))] * 2,
        compiler_params=params(collective_id, 48),
        name="scatter_gradients",
    )(*grads, vec, in_own, lay_own)


def adam_step(master, moment, variance, gradient, rate, decay):
    moment_new = BETA_FIRST * moment + (1.0 - BETA_FIRST) * gradient
    variance_new = BETA_SECOND * variance + (1.0 - BETA_SECOND) * gradient * gradient
    moment_hat = moment_new / (1.0 - BETA_FIRST**STEP)
    variance_hat = variance_new / (1.0 - BETA_SECOND**STEP)
    master_new = master - rate * (
        moment_hat / (jnp.sqrt(variance_hat) + ADAM_EPSILON) + decay * master
    )
    return (master_new, moment_new, variance_new)


def on_device(
    tokens,
    cotangent,
    lengths,
    joint_weight,
    output_weight,
    widen_weight,
    narrow_weight,
    shared_vectors,
    split_vectors,
    joint_first,
    joint_second,
    output_first,
    output_second,
    widen_first,
    widen_second,
    narrow_first,
    narrow_second,
    shared_first,
    shared_second,
    split_first,
    split_second,
):
    n_dp, n_tensor = lax.axis_size("dp"), lax.axis_size("tensor")
    sizes = (joint_weight.shape[1], widen_weight.shape[1], output_weight.shape[0], narrow_weight.shape[0])
    starts = (0, sizes[0], sizes[0] + sizes[1], sum(sizes[:3]), sum(sizes))
    spans = [slice(first, last) for first, last in zip(starts[:-1], starts[1:])]
    shard = jnp.concatenate(
        [by_kind(joint_weight), widen_weight, output_weight.T, narrow_weight.T], axis=1
    ).astype(BF)
    shared_cols, split_cols = shared_vectors.shape[1], split_vectors.shape[1]
    vec_cols = -(-max(shared_cols, split_cols) // 128) * 128
    vec_shard = jnp.concatenate(
        [
            jnp.pad(shared_vectors, ((0, 0), (0, vec_cols - shared_cols))),
            jnp.pad(split_vectors, ((0, 9), (0, vec_cols - split_cols))),
        ],
        axis=0,
    ).astype(BF)
    cuts = tuple((first, last - first) for first, last in zip(starts[:-1], starts[1:]))
    work, vecs = gather_weights(shard, vec_shard, n_dp, n_tensor, cuts, 0)
    joint_work, widen_work, output_t, narrow_t = [work[:, span] for span in spans]
    shared_float = jnp.swapaxes(vecs[:, :6, :shared_cols], 0, 1).reshape(6, D).astype(F32)
    split_float = vecs[:, 6, :split_cols].reshape(-1).astype(F32)
    vec = jnp.pad(shared_float, ((0, 2), (0, 0)))
    head_size = D // HEADS
    head_cols = sizes[2]
    local_heads = head_cols // head_size
    tensor_rank = lax.axis_index("tensor")
    widen_bias = split_float[2 * head_cols :]
    total_rows = tokens.shape[0]
    block = min(512, total_rows)
    blocks, quarter = total_rows // block, block // 4
    slot = lax.rem(tensor_rank, 2) * 2 + tensor_rank // 2
    own_tokens = lax.dynamic_index_in_dim(tokens.reshape(blocks, 4, quarter, D), slot, 1, keepdims=False)
    scale = 1.0 / math.sqrt(head_size)
    qkv_bias = jnp.concatenate([split_float[:head_cols], jnp.zeros((head_cols,), F32), split_float[head_cols : 2 * head_cols]])
    qkv_scale = jnp.concatenate([jnp.full((head_cols,), scale, F32), jnp.ones((2 * head_cols,), F32)])

    normed_one, _ = normalize(tokens.astype(F32))
    attn_input = (normed_one * shared_float[0] + shared_float[1]).astype(BF)
    qkv = ((jnp.dot(attn_input, joint_work, preferred_element_type=F32) + qkv_bias) * qkv_scale).astype(BF)
    heads_out, lse, hidden_one, mlp_input = attend(
        qkv, output_t, own_tokens, vec, local_heads, head_size, HEADS, block, n_tensor, 1
    )
    mlp_part, grad_widen, grad_narrow, grad_hidden, grad_hidden_low, feed_vec, widen_bias_grad = feed(
        lengths, mlp_input, cotangent, widen_work, narrow_t, widen_bias[None], hidden_one, vec, block, n_tensor, 2
    )
    grad_joint, grad_output, input_own, layer_own, attend_vec, qkv_bias_grad = attend_back(
        lengths, qkv, output_t, joint_work, grad_hidden_low, attn_input, heads_out, lse, own_tokens, grad_hidden,
        hidden_one, vec, mlp_part, local_heads, head_size, HEADS, block, n_tensor, 3,
    )
    grad_shared = jnp.concatenate([attend_vec[:2], feed_vec[:4]], axis=0)
    grad_split = jnp.concatenate(
        [qkv_bias_grad[0, :head_cols], qkv_bias_grad[0, 2 * head_cols :], widen_bias_grad[0]]
    )
    grad_vecs = jnp.concatenate(
        [
            jnp.pad(
                jnp.swapaxes(grad_shared.reshape(6, n_dp, shared_cols), 0, 1),
                ((0, 0), (0, 0), (0, vec_cols - shared_cols)),
            ),
            jnp.pad(grad_split.reshape(n_dp, 1, split_cols), ((0, 0), (0, 1), (0, vec_cols - split_cols))),
        ],
        axis=1,
    )
    grad_sum, vec_sum, square, input_grad, layer_output = scatter_gradients(
        (grad_joint, grad_widen, grad_output, grad_narrow), grad_vecs, input_own, layer_own, n_dp, n_tensor, 4
    )
    joint_sum = by_head(grad_sum[:, spans[0]])
    widen_sum = grad_sum[:, spans[1]]
    output_sum = grad_sum[:, spans[2]].T
    narrow_sum = grad_sum[:, spans[3]].T
    shared_sum = vec_sum[:6, :shared_cols]
    split_sum = vec_sum[6:7, :split_cols]
    grad_norm = jnp.sqrt(square[0, 0])
    factor = jnp.minimum(1.0, CLIP_LIMIT / (grad_norm + 1e-06))
    joint_new = adam_step(
        joint_weight, joint_first, joint_second, factor * joint_sum, MATRIX_RATE, MATRIX_DECAY
    )
    output_new = adam_step(
        output_weight, output_first, output_second, factor * output_sum, OUTPUT_RATE, MATRIX_DECAY
    )
    widen_new = adam_step(
        widen_weight, widen_first, widen_second, factor * widen_sum, MATRIX_RATE, MATRIX_DECAY
    )
    narrow_new = adam_step(
        narrow_weight, narrow_first, narrow_second, factor * narrow_sum, MATRIX_RATE, MATRIX_DECAY
    )
    shared_new = adam_step(
        shared_vectors, shared_first, shared_second, factor * shared_sum, VECTOR_RATE, 0.0
    )
    split_new = adam_step(
        split_vectors, split_first, split_second, factor * split_sum, VECTOR_RATE, 0.0
    )
    return (
        layer_output,
        input_grad,
        grad_norm,
        joint_new[0],
        joint_new[1],
        joint_new[2],
        output_new[0],
        output_new[1],
        output_new[2],
        widen_new[0],
        widen_new[1],
        widen_new[2],
        narrow_new[0],
        narrow_new[1],
        narrow_new[2],
        shared_new[0],
        shared_new[1],
        shared_new[2],
        split_new[0],
        split_new[1],
        split_new[2],
    )


def solution(mesh):
    in_specs = (
        P("dp", None),
        P("dp", None),
        P("dp"),
        P("dp", "tensor"),
        P("tensor", "dp"),
        P("dp", "tensor"),
        P("tensor", "dp"),
        P(None, "dp"),
        P("tensor", "dp"),
        P("dp", "tensor"),
        P("dp", "tensor"),
        P("tensor", "dp"),
        P("tensor", "dp"),
        P("dp", "tensor"),
        P("dp", "tensor"),
        P("tensor", "dp"),
        P("tensor", "dp"),
        P(None, "dp"),
        P(None, "dp"),
        P("tensor", "dp"),
        P("tensor", "dp"),
    )
    out_specs = (
        P("dp", None),
        P("dp", None),
        P(),
        P("dp", "tensor"),
        P("dp", "tensor"),
        P("dp", "tensor"),
        P("tensor", "dp"),
        P("tensor", "dp"),
        P("tensor", "dp"),
        P("dp", "tensor"),
        P("dp", "tensor"),
        P("dp", "tensor"),
        P("tensor", "dp"),
        P("tensor", "dp"),
        P("tensor", "dp"),
        P(None, "dp"),
        P(None, "dp"),
        P(None, "dp"),
        P("tensor", "dp"),
        P("tensor", "dp"),
        P("tensor", "dp"),
    )
    return jax.shard_map(
        on_device, mesh=mesh, in_specs=in_specs, out_specs=out_specs, check_vma=False
    )
```

```python
import functools
import math

import jax
import jax.numpy as jnp
from jax import lax
from jax.experimental import pallas as pl
from jax.experimental.pallas import tpu as pltpu
from jax.sharding import PartitionSpec as P

F32, BF = jnp.float32, jnp.bfloat16

D = 1024
HEADS = 16
STEP = 10


NORM_EPSILON = 1e-05
CLIP_LIMIT = 1.0
BETA_FIRST = 0.9
BETA_SECOND = 0.95
ADAM_EPSILON = 1e-08
MATRIX_RATE = 0.05
OUTPUT_RATE = 0.2
VECTOR_RATE = 0.6
MATRIX_DECAY = 0.1


def by_kind(values):
    rows, cols = values.shape
    size = D // HEADS
    return jnp.swapaxes(values.reshape(rows, cols // (3 * size), 3, size), 1, 2).reshape(rows, cols)


NN = (((1,), (0,)), ((), ()))
NT = (((1,), (1,)), ((), ()))
TN = (((0,), (0,)), ((), ()))
LOW = -1e30


def dot(left, right, dims=NN):
    return lax.dot_general(left, right, dims, preferred_element_type=F32)


def three(values):
    high = values.astype(BF).astype(F32)
    rest = values - high
    middle = rest.astype(BF).astype(F32)
    return high, middle, rest - middle


def stack_rows(shape, rows):
    ids = lax.broadcasted_iota(jnp.int32, shape, 0)
    out = jnp.zeros(shape, F32)
    for at, row in enumerate(rows):
        out = jnp.where(ids == at, row, out)
    return out.astype(BF)


def head_tile(ref, rows, col, head, d):
    lane = col + (head // 2) * 128
    tile = ref[rows, lane:lane + 128].astype(F32)
    if head % 2:
        tile = pltpu.roll(tile, 64, 1)
    return tile


def fill_keys(qkv_ref, ka_ref, heads, d, slope_of, first, count):
    rows = pl.ds(first, count)
    lanes = lax.broadcasted_iota(jnp.int32, (count, 128), 1)
    position = (lax.broadcasted_iota(jnp.int32, (count, 128), 0) + first).astype(F32)
    for head in range(heads):
        high, middle, low = three(position * slope_of(head))
        tile = head_tile(qkv_ref, rows, heads * d, head, d)
        for at, part in enumerate((high, middle, low, 1.0, 1.0, 1.0)):
            tile = jnp.where(lanes == d + at, part, tile)
        ka_ref[head, rows, :] = jnp.where(lanes < d + 6, tile, 0.0).astype(BF)


def causal(scores, bk, bq):
    kid = lax.broadcasted_iota(jnp.int32, (bk, bq), 0)
    qid = lax.broadcasted_iota(jnp.int32, (bk, bq), 1)
    return jnp.where(kid <= qid, scores, LOW)


def slope_fn(heads, total_heads):
    rank = lax.axis_index("tensor")
    def slope_of(head):
        index = jnp.full((1, 128), rank * heads + head + 1, jnp.int32).astype(F32)
        return jnp.exp2(index * (-8.0 / total_heads))
    return slope_of


def at_dp(index):
    return {"dp": index}


def at_tensor(index):
    return {"tensor": index}


def remote(src, dst, send, recv, where):
    return pltpu.make_async_remote_copy(
        src_ref=src, dst_ref=dst, send_sem=send, recv_sem=recv, device_id=where, device_id_type=pl.DeviceIdType.MESH
    )


def greet(n_dp, n_tensor):
    me, rank = lax.axis_index("dp"), lax.axis_index("tensor")
    barrier = pltpu.get_barrier_semaphore()

    def along_dp(k, c):
        pl.semaphore_signal(barrier, inc=1, device_id=at_dp(lax.rem(me + k, n_dp)), device_id_type=pl.DeviceIdType.MESH)
        return c

    lax.fori_loop(1, n_dp, along_dp, 0)
    for k in range(1, n_tensor):
        pl.semaphore_signal(
            barrier, inc=1, device_id=at_tensor(lax.rem(rank + k, n_tensor)), device_id_type=pl.DeviceIdType.MESH
        )
    pl.semaphore_wait(barrier, n_dp + n_tensor - 2)


def over(body, first, last):
    lax.fori_loop(first, last, lambda k, c: (body(k), c)[1], 0)


def greet_tensor(n_tensor):
    rank = lax.axis_index("tensor")
    barrier = pltpu.get_barrier_semaphore()
    for k in range(1, n_tensor):
        pl.semaphore_signal(
            barrier, inc=1, device_id=at_tensor(lax.rem(rank + k, n_tensor)), device_id_type=pl.DeviceIdType.MESH
        )
    pl.semaphore_wait(barrier, n_tensor - 1)


class Gather:
    def __init__(self, lines, rows, pieces, sems):
        me = lax.axis_index("dp")
        self.me, self.z, self.x = me, me // 2, lax.rem(me, 2)
        self.lines, self.rows, self.pieces, self.sems = lines, rows, pieces, sems
        self.other = at_dp(self.z * 2 + 1 - self.x)

    def own(self, s):
        shard, first, _, cols = self.pieces[s][:4]
        return shard.at[:, pl.ds(first, cols)]

    def spot(self, s, device):
        _, _, first, cols, out = self.pieces[s]
        return out.at[pl.ds(pl.multiple_of(device * self.rows, self.rows), self.rows), pl.ds(first, cols)]

    def to_x(self, s, zz, src):
        return remote(src, self.spot(s, zz * 2 + self.x), self.sems.at[0, s, zz], self.sems.at[1, s, zz], self.other)

    def from_x(self, s, zz):
        spot = self.spot(s, zz * 2 + 1 - self.x)
        return remote(spot, spot, self.sems.at[0, s, zz], self.sems.at[1, s, zz], self.other)

    def to_z(self, s, k):
        target = lax.rem(self.z + k, self.lines) * 2 + self.x
        return remote(self.own(s), self.spot(s, self.me), self.sems.at[2, s, k], self.sems.at[3, s, self.z], at_dp(target))

    def from_z(self, s, zz):
        spot = self.spot(s, zz * 2 + self.x)
        return remote(spot, spot, self.sems.at[2, s, 0], self.sems.at[3, s, zz], self.other)

    def keep(self, s):
        return pltpu.make_async_copy(self.own(s), self.spot(s, self.me), self.sems.at[2, s, 0])

    def begin(self, s):
        over(lambda k: self.to_z(s, k).start(), 1, self.lines)
        self.to_x(s, self.z, self.own(s)).start()
        self.keep(s).start()

    def forward(self, s):
        def step(k):
            zz = lax.rem(self.z + k, self.lines)
            self.from_z(s, zz).wait_recv()
            self.to_x(s, zz, self.spot(s, zz * 2 + self.x)).start()

        over(step, 1, self.lines)

    def finish(self, s):
        self.keep(s).wait()
        over(lambda k: self.to_z(s, k).wait_send(), 1, self.lines)
        over(lambda zz: self.to_x(s, zz, self.own(s)).wait_send(), 0, self.lines)
        over(lambda zz: self.from_x(s, zz).wait_recv(), 0, self.lines)


class Place:
    def __init__(self):
        rank = lax.axis_index("tensor")
        self.far, self.near = rank // 2, lax.rem(rank, 2)
        self.near_device = at_tensor(self.far * 2 + 1 - self.near)
        self.far_device = at_tensor((1 - self.far) * 2 + self.near)


class BlockSum:
    def __init__(self, place, quarter, part, near_buf, send_buf, far_buf, sems):
        self.place, self.quarter, self.part = place, quarter, part
        self.near_buf, self.send_buf, self.far_buf = near_buf, send_buf, far_buf
        self.sems = sems

    def rows(self, near, far):
        first = (near * 2 + far) * self.quarter
        return pl.ds(pl.multiple_of(first, self.quarter), self.quarter)

    def half(self, near):
        first = near * 2 * self.quarter
        return pl.ds(pl.multiple_of(first, self.quarter), 2 * self.quarter)

    def to_near(self, b):
        return remote(self.part.at[b, self.half(1 - self.place.near)], self.near_buf.at[b],
                      self.sems.at[0, b], self.sems.at[1, b], self.place.near_device)

    def to_far(self, b):
        return remote(self.send_buf.at[b], self.far_buf.at[b], self.sems.at[2, b], self.sems.at[3, b],
                      self.place.far_device)

    def own(self, b, far):
        return self.part[b, self.rows(self.place.near, far)].astype(F32)

    def begin(self, b):
        self.to_near(b).start()

    def pass_on(self, b):
        far = self.place.far
        self.to_near(b).wait_recv()
        taken = self.near_buf[b, self.rows(0, 1 - far)].astype(F32)
        self.send_buf[b] = (self.own(b, 1 - far) + taken).astype(BF)
        self.to_far(b).start()

    def total(self, b):
        far = self.place.far
        self.to_far(b).wait_recv()
        return self.own(b, far) + self.near_buf[b, self.rows(0, far)].astype(F32) + self.far_buf[b].astype(F32)

    def finish(self, b):
        self.to_near(b).wait_send()
        self.to_far(b).wait_send()


class HalfSum(BlockSum):
    def __init__(self, place, quarter, whole, block, part, near_buf, send_buf, far_buf, sems):
        super().__init__(place, quarter, part, near_buf, send_buf, far_buf, sems)
        self.whole, self.block = whole, block

    def from_block(self, b, near):
        first = b * self.block + near * 2 * self.quarter
        return self.whole.at[pl.ds(pl.multiple_of(first, self.quarter), 2 * self.quarter)]

    def to_near(self, b):
        return remote(self.from_block(b, 1 - self.place.near), self.near_buf.at[b],
                      self.sems.at[0, b], self.sems.at[1, b], self.place.near_device)

    def load(self, b):
        return pltpu.make_async_copy(self.from_block(b, self.place.near), self.part.at[b], self.sems.at[4, b])

    def own(self, b, far):
        return self.part[b, self.rows(0, far)].astype(F32)

    def begin(self, b):
        self.to_near(b).start()
        self.load(b).start()

    def pass_on(self, b):
        self.load(b).wait()
        super().pass_on(b)


class BlockSpread:
    def __init__(self, place, quarter, own, out, sems):
        self.place, self.quarter, self.own, self.out, self.sems = place, quarter, own, out, sems

    def spot(self, b, near, far):
        first = (b * 4 + near * 2 + far) * self.quarter
        return self.out.at[pl.ds(pl.multiple_of(first, self.quarter), self.quarter)]

    def mine(self, b):
        return self.spot(b, self.place.near, self.place.far)

    def to_far(self, b):
        return remote(self.own.at[b], self.mine(b), self.sems.at[0, b], self.sems.at[1, b], self.place.far_device)

    def to_near(self, b):
        return remote(self.own.at[b], self.mine(b), self.sems.at[2, b], self.sems.at[3, b], self.place.near_device)

    def arrival(self, near, far, b, at):
        spot = self.spot(b, near, far)
        return remote(spot, spot, self.sems.at[at - 1, b], self.sems.at[at, b], self.place.near_device)

    def pass_far(self, b):
        spot = self.spot(b, self.place.near, 1 - self.place.far)
        return remote(spot, spot, self.sems.at[4, b], self.sems.at[5, b], self.place.near_device)

    def keep(self, b):
        return pltpu.make_async_copy(self.own.at[b], self.mine(b), self.sems.at[6, b])

    def begin(self, b):
        self.to_far(b).start()
        self.to_near(b).start()
        self.keep(b).start()

    def relay(self, b):
        self.arrival(self.place.near, 1 - self.place.far, b, 1).wait_recv()
        self.pass_far(b).start()

    def finish(self, b):
        self.to_far(b).wait_send()
        self.to_near(b).wait_send()
        self.pass_far(b).wait_send()
        self.keep(b).wait()
        self.arrival(1 - self.place.near, self.place.far, b, 3).wait_recv()
        self.arrival(1 - self.place.near, 1 - self.place.far, b, 5).wait_recv()


def normalize(values):
    centred = values - jnp.mean(values, axis=-1, keepdims=True)
    inverse = lax.rsqrt(jnp.mean(centred * centred, axis=-1, keepdims=True) + NORM_EPSILON)
    return (centred * inverse, inverse)


def normalize_back(incoming, normed, inverse, gain):
    scaled = incoming * gain
    return inverse * (
        scaled
        - jnp.mean(scaled, axis=-1, keepdims=True)
        - normed * jnp.mean(scaled * normed, axis=-1, keepdims=True)
    )


def column_sum(values):
    return jnp.sum(values, axis=0, keepdims=True)


def params(collective_id, megabytes):
    return pltpu.CompilerParams(
        collective_id=collective_id, has_side_effects=True, vmem_limit_bytes=megabytes * 2**20
    )


ANYWHERE = pl.BlockSpec(memory_space=pl.ANY)


def fixed(shape):
    return pl.BlockSpec(shape, lambda i: (0,) * len(shape), pipeline_mode=pl.Buffered(1))


def whole(array):
    return fixed(array.shape)


def project_kernel(n_dp, n_tensor, chunk, scale, tok_ref, shard_ref, vec_ref, a_ref, qkv_ref, wj_ref, wo_ref, vec_out,
                   a_buf, vec_buf, sems, a_sem, vs, vr):
    me = lax.axis_index("dp")
    rows = shard_ref.shape[0]
    joint, width = wj_ref.shape[1], wo_ref.shape[1]
    pieces = [(shard_ref, 0, 0, joint, wj_ref), (shard_ref, joint, 0, width, wo_ref)]
    gather = Gather(n_dp // 2, rows, pieces, sems)
    n = tok_ref.shape[0]

    def vec_to(k):
        return remote(vec_ref, vec_buf.at[me], vs.at[k], vr.at[me], at_dp(lax.rem(me + k, n_dp)))

    def vec_from(k):
        source = lax.rem(me + k, n_dp)
        return remote(vec_buf.at[source], vec_buf.at[source], vs.at[k], vr.at[source], at_dp(source))

    greet(n_dp, n_tensor)
    over(lambda k: vec_to(k).start(), 1, n_dp)
    gather.begin(0)
    gather.begin(1)
    vec_buf[me] = vec_ref[...]
    over(lambda k: vec_from(k).wait_recv(), 1, n_dp)
    vec_out[...] = lax.fori_loop(0, n_dp, lambda k, acc: acc + vec_buf[k].astype(F32), jnp.zeros(vec_out.shape, F32))
    feats = tok_ref.shape[1]

    def store(c):
        span = pl.ds(pl.multiple_of(c * chunk, chunk), chunk)
        return pltpu.make_async_copy(a_buf.at[span], a_ref.at[span], a_sem.at[c])

    def norm(c):
        span = pl.ds(pl.multiple_of(c * chunk, chunk), chunk)
        normed, _ = normalize(tok_ref[span, :].astype(F32))
        a_buf[span, :] = (normed * vec_out[0:1, :feats] + vec_out[1:2, :feats]).astype(BF)
        store(c).start()

    over(norm, 0, n // chunk)
    gather.forward(0)
    gather.forward(1)
    gather.finish(0)

    def project(c):
        span = pl.ds(pl.multiple_of(c * chunk, chunk), chunk)
        out = dot(a_buf[span, :], wj_ref[...])
        qkv_ref[span, 0:width] = ((out[:, 0:width] + vec_out[6:7, 0:width]) * scale).astype(BF)
        qkv_ref[span, width:2 * width] = out[:, width:2 * width].astype(BF)
        qkv_ref[span, 2 * width:] = (out[:, 2 * width:] + vec_out[6:7, width:2 * width]).astype(BF)

    over(project, 0, n // chunk)
    gather.finish(1)
    over(lambda c: store(c).wait(), 0, n // chunk)
    over(lambda k: vec_to(k).wait_send(), 1, n_dp)


def project(tokens, shard, vec, joint, width, scale, n_dp, n_tensor, collective_id, chunk=256):
    n, feats = tokens.shape
    chunk = min(chunk, n)
    vmem = pl.BlockSpec(memory_space=pltpu.VMEM)
    dma = pltpu.SemaphoreType.DMA
    return pl.pallas_call(
        functools.partial(project_kernel, n_dp, n_tensor, chunk, scale),
        in_specs=[vmem, vmem, vmem],
        out_specs=[ANYWHERE, vmem, vmem, vmem, vmem],
        out_shape=[jax.ShapeDtypeStruct((n, feats), BF), jax.ShapeDtypeStruct((n, joint), BF),
                   jax.ShapeDtypeStruct((feats, joint), BF), jax.ShapeDtypeStruct((feats, width), BF),
                   jax.ShapeDtypeStruct(vec.shape, F32)],
        scratch_shapes=[pltpu.VMEM((n, feats), BF), pltpu.VMEM((n_dp,) + vec.shape, BF), dma((4, 2, n_dp // 2)),
                        dma((n // chunk,)), dma((n_dp,)), dma((n_dp,))],
        compiler_params=params(collective_id, 48),
        name="project",
    )(tokens, shard, vec)


def attend_kernel(heads, d, total_heads, bq, nb, n_dp, n_tensor, cuts, qkv_ref, wo_ref, tok_ref, vec_ref, shard_ref,
                  ot_ref, lse_ref, h1_ref, c_ref, work_ref, ka_ref, vt_ref, part_ref, near_buf, send_buf, far_buf, own_buf, sum_sems, spread_sems,
                  gather_sems):
    i = pl.program_id(0)
    width = heads * d
    place = Place()
    pieces = [(shard_ref, first, first, cols, work_ref) for first, cols in cuts]
    gather = Gather(n_dp // 2, shard_ref.shape[0], pieces, gather_sems)
    feats = wo_ref.shape[0]
    quarter = bq // 4
    summing = BlockSum(place, quarter, part_ref, near_buf, send_buf, far_buf, sum_sems)
    spread = BlockSpread(place, quarter, own_buf, c_ref, spread_sems)

    @pl.when(i == 0)
    def _():
        greet(n_dp, n_tensor)
        for s in range(len(cuts)):
            gather.begin(s)

    def norm_block(b):
        hidden = tok_ref[b].astype(F32) + summing.total(b) + vec_ref[4:5, :feats]
        h1_ref[b] = hidden
        normed, _ = normalize(hidden)
        own_buf[b] = (normed * vec_ref[2:3, :feats] + vec_ref[3:4, :feats]).astype(BF)
        spread.begin(b)

    rows_i = pl.ds(pl.multiple_of(i * bq, bq), bq)
    fill_keys(qkv_ref, ka_ref, heads, d, slope_fn(heads, total_heads), pl.multiple_of(i * bq, bq), bq)
    vt_ref[i] = qkv_ref[rows_i, 2 * width:3 * width].T
    qt = qkv_ref[rows_i, 0:width].T
    ones = stack_rows((128 - d, bq), (1.0, 1.0, 1.0))
    queries = [jnp.concatenate([qt[h * d:(h + 1) * d], ones], axis=0) for h in range(heads)]

    def block(j, carry, last):
        out = []
        kr = pl.ds(pl.multiple_of(j * bq, bq), bq)
        for h in range(heads):
            m, l, acc = carry[h]
            s = dot(ka_ref[h, kr, :], queries[h])
            if last:
                s = causal(s, bq, bq)
            top = jnp.maximum(m, jnp.max(s, axis=0, keepdims=True))
            p = jnp.exp(s - top)
            scale = jnp.exp(m - top)
            l = l * scale + jnp.sum(p, axis=0, keepdims=True)
            acc = acc * scale + dot(vt_ref[j, h * d:(h + 1) * d, :], p.astype(BF))
            out.append((top, l, acc))
        return tuple(out)

    start = (jnp.full((1, bq), LOW, F32), jnp.zeros((1, bq), F32), jnp.zeros((d, bq), F32))
    carry = lax.fori_loop(0, i, lambda j, c: block(j, c, False), (start,) * heads)

    @pl.when(i >= 1)
    def _():
        summing.pass_on(i - 1)

    @pl.when(i >= 2)
    def _():
        norm_block(i - 2)

    @pl.when(i >= 3)
    def _():
        spread.relay(i - 3)

    carry = block(i, carry, True)
    for h in range(heads):
        m, l, acc = carry[h]
        ot_ref[h * d:(h + 1) * d, :] = acc / l
        lse_ref[0, h:h + 1, :] = m + jnp.log(l)
    part_ref[i] = dot(ot_ref[...].astype(BF).T, wo_ref[...], NT).astype(BF)
    summing.begin(i)

    @pl.when(i == nb - 2)
    def _():
        gather.forward(0)

    @pl.when(i == nb - 1)
    def _():
        summing.pass_on(nb - 1)
        gather.forward(1)
        if nb >= 2:
            norm_block(nb - 2)
        if nb >= 3:
            spread.relay(nb - 3)
        norm_block(nb - 1)
        if nb >= 2:
            spread.relay(nb - 2)
        gather.forward(2)
        spread.relay(nb - 1)
        for s in range(3, len(cuts)):
            gather.forward(s)
        for s in range(len(cuts)):
            gather.finish(s)

        def close(b):
            summing.finish(b)
            spread.finish(b)

        over(close, 0, nb)


def sum_scratch(nb, quarter, feats):
    return [pltpu.VMEM((nb, 2 * quarter, feats), BF), pltpu.VMEM((nb, quarter, feats), BF),
            pltpu.VMEM((nb, quarter, feats), BF)]


def attend(qkv, wo, tok_own, vec, shard, cuts, heads, d, total_heads, bq, n_dp, n_tensor, collective_id):
    n, width = qkv.shape[0], heads * d
    nb = n // bq
    feats = wo.shape[0]
    quarter = bq // 4
    own = (nb, quarter, feats)
    dma = pltpu.SemaphoreType.DMA
    return pl.pallas_call(
        functools.partial(attend_kernel, heads, d, total_heads, bq, nb, n_dp, n_tensor, cuts),
        grid=(nb,),
        in_specs=[whole(qkv), whole(wo), whole(tok_own), whole(vec), ANYWHERE],
        out_specs=[pl.BlockSpec((width, bq), lambda i: (0, i)), pl.BlockSpec((1, heads, bq), lambda i: (i, 0, 0)),
                   fixed(own), ANYWHERE, ANYWHERE],
        out_shape=[jax.ShapeDtypeStruct((width, n), F32), jax.ShapeDtypeStruct((nb, heads, bq), F32),
                   jax.ShapeDtypeStruct(own, F32), jax.ShapeDtypeStruct((n, feats), BF),
                   jax.ShapeDtypeStruct((n_dp * shard.shape[0], shard.shape[1]), BF)],
        scratch_shapes=[pltpu.VMEM((heads, n, 128), BF), pltpu.VMEM((nb, width, bq), BF),
                        pltpu.VMEM((nb, bq, feats), BF)] + sum_scratch(nb, quarter, feats)
        + [pltpu.VMEM(own, BF), dma((4, nb)), dma((7, nb)), dma((4, len(cuts), n_dp // 2))],
        compiler_params=params(collective_id, 56),
        name="attend",
    )(qkv, wo, tok_own, vec, shard)


def feed_kernel(bq, nb, n_tensor, hidden_step, bias_at, len_ref, c_ref, cot_ref, w1_ref, w2_ref, h1_ref, vec_ref,
                mlp_ref, gw1_ref, gw2_ref, gh1_ref, low_ref, gvec_ref, gbias_ref,
                acc1, acc2, gown_buf, hid_buf, gu_buf, part_ref, near_buf, send_buf, far_buf, own_buf,
                sum_sems, spread_sems):
    g = pl.program_id(0)
    i = nb - 1 - g
    place = Place()
    quarter = bq // 4
    summing = BlockSum(place, quarter, part_ref, near_buf, send_buf, far_buf, sum_sems)
    spread = BlockSpread(place, quarter, own_buf, low_ref, spread_sems)
    hidden = w1_ref.shape[1]

    @pl.when(g == 0)
    def _():
        greet_tensor(n_tensor)
        acc1[...] = jnp.zeros_like(acc1)
        acc2[...] = jnp.zeros_like(acc2)
        gvec_ref[...] = jnp.zeros_like(gvec_ref)
        gbias_ref[...] = jnp.zeros_like(gbias_ref)

    def norm_block(b):
        grad_c = summing.total(b)
        normed, inverse = normalize(h1_ref[b])
        grad_out = gown_buf[b].astype(F32)
        grad_h = grad_out + normalize_back(grad_c, normed, inverse, vec_ref[2:3, :h1_ref.shape[2]])
        gh1_ref[b] = grad_h
        own_buf[b] = grad_h.astype(BF)
        spread.begin(b)
        gvec_ref[0:1, :] += column_sum(grad_c * normed)
        gvec_ref[1:2, :] += column_sum(grad_c)
        gvec_ref[2:3, :] += column_sum(grad_h)
        gvec_ref[3:4, :] += column_sum(grad_out)

    c = c_ref[...]
    row_ids = lax.broadcasted_iota(jnp.int32, (bq, 128), 0) + i * bq
    live = jnp.where(row_ids < len_ref[0], 1.0, 0.0).astype(BF)
    grad_out = cot_ref[...] * jnp.concatenate([live] * (cot_ref.shape[1] // 128), axis=1)
    cot_ref_rows = pl.ds(pl.multiple_of((place.near * 2 + place.far) * quarter, quarter), quarter)
    own_ids = lax.broadcasted_iota(jnp.int32, (quarter, 128), 0) + (place.near * 2 + place.far) * quarter + i * bq
    own_live = jnp.where(own_ids < len_ref[0], 1.0, 0.0).astype(BF)
    gown_buf[i] = cot_ref[cot_ref_rows, :] * jnp.concatenate([own_live] * (cot_ref.shape[1] // 128), axis=1)

    root = math.sqrt(2.0 / math.pi)
    for first in range(0, hidden, hidden_step):
        cols = slice(first, first + hidden_step)
        u = dot(c, w1_ref[:, cols]) + vec_ref[6:7, bias_at + first:bias_at + first + hidden_step]
        square = u * u
        bent = jnp.tanh(root * (u + 0.044715 * (square * u)))
        half = 0.5 * (1.0 + bent)
        hid = (u * half).astype(BF)
        hid_buf[:, cols] = hid
        slope = half + 0.5 * u * (1.0 - bent * bent) * (root * (1.0 + 3 * 0.044715 * square))
        grad_u = (dot(grad_out, w2_ref[:, cols]) * slope).astype(BF)
        gu_buf[:, cols] = grad_u
        gbias_ref[:, cols] += column_sum(grad_u.astype(F32))
    part_ref[i] = dot(gu_buf[...], w1_ref[...], NT).astype(BF)
    summing.begin(i)
    mlp_ref[...] = dot(hid_buf[...], w2_ref[...], NT).astype(BF)

    @pl.when(g >= 1)
    def _():
        norm_block(i + 1)

    summing.pass_on(i)

    @pl.when(g >= 2)
    def _():
        spread.relay(i + 2)

    acc1[...] += dot(c, gu_buf[...], TN)
    acc2[...] += dot(grad_out, hid_buf[...], TN)

    @pl.when(g == nb - 1)
    def _():
        norm_block(0)
        gw1_ref[...] = acc1[...].astype(BF)
        gw2_ref[...] = acc2[...].astype(BF)
        if nb >= 2:
            spread.relay(1)
        spread.relay(0)

        def close(b):
            summing.finish(b)
            spread.finish(b)

        over(close, 0, nb)


def feed(lengths, c, cot, work, bias_at, h1, vec, bq, n_tensor, collective_id):
    n, feats = c.shape
    hidden = work.shape[1] // 2
    nb = n // bq
    quarter = bq // 4
    own = (nb, quarter, feats)
    dma = pltpu.SemaphoreType.DMA
    back = pl.BlockSpec((bq, feats), lambda i: (nb - 1 - i, 0))
    return pl.pallas_call(
        functools.partial(feed_kernel, bq, nb, n_tensor, 256, bias_at),
        grid=(nb,),
        in_specs=[pl.BlockSpec(memory_space=pltpu.SMEM), back, back,
                  pl.BlockSpec((feats, hidden), lambda i: (0, 0), pipeline_mode=pl.Buffered(1)),
                  pl.BlockSpec((feats, hidden), lambda i: (0, 1), pipeline_mode=pl.Buffered(1)), whole(h1), whole(vec)],
        out_specs=[back, fixed((feats, hidden)), fixed((feats, hidden)), fixed(own), ANYWHERE, fixed((8, feats)),
                   fixed((1, hidden))],
        out_shape=[jax.ShapeDtypeStruct((n, feats), BF), jax.ShapeDtypeStruct((feats, hidden), BF),
                   jax.ShapeDtypeStruct((feats, hidden), BF), jax.ShapeDtypeStruct(own, F32),
                   jax.ShapeDtypeStruct((n, feats), BF), jax.ShapeDtypeStruct((8, feats), F32),
                   jax.ShapeDtypeStruct((1, hidden), F32)],
        scratch_shapes=[pltpu.VMEM((feats, hidden), F32), pltpu.VMEM((feats, hidden), F32), pltpu.VMEM(own, BF),
                        pltpu.VMEM((bq, hidden), BF), pltpu.VMEM((bq, hidden), BF),
                        pltpu.VMEM((nb, bq, feats), BF)] + sum_scratch(nb, quarter, feats)
        + [pltpu.VMEM(own, BF), dma((4, nb)), dma((7, nb))],
        compiler_params=params(collective_id, 62),
        name="feed",
    )(lengths, c, cot, work, work, h1, vec)


def attend_back_kernel(heads, d, total_heads, bq, nb, n_dp, n_tensor, cuts, len_ref, qkv_ref, wo_ref, wj_ref, gh_ref, a_ref, ot_ref,
                       lse_ref, tok_ref, gh1_ref, h1_ref, vec_ref, mlp_ref, gw1_ref, gw2_ref,
                       gj_ref, go_ref, in_ref, lay_ref, gvec_ref, gbias_ref, total_ref,
                       ka_ref, kt_ref, va_ref, dk_ref, dv_ref, gqkv_buf, accj, acco,
                       part_ref, near_buf, send_buf, far_buf, half_buf, near2_buf, send2_buf, far2_buf,
                       lay_buf, x_buf, z_buf, sum_sems, sum2_sems, lay_sems, scatter_sems):
    g = pl.program_id(0)
    i = nb - 1 - g
    width = heads * d
    place = Place()
    quarter = bq // 4
    summing = BlockSum(place, quarter, part_ref, near_buf, send_buf, far_buf, sum_sems)
    second = HalfSum(place, quarter, mlp_ref, bq, half_buf, near2_buf, send2_buf, far2_buf, sum2_sems)

    spread = BlockSpread(place, quarter, lay_buf, lay_ref, lay_sems)
    feats = wo_ref.shape[0]
    parts = [
        Scatter(n_dp // 2, total_ref.shape[0], (gw1_ref, gw2_ref)[index], first, cols, x_buf.at[p], z_buf.at[p], total_ref,
                at, scatter_sems, p)
        for p, (index, first, cols, at) in enumerate(cuts)
    ]

    def layer_block(b):
        first = (b * 4 + place.near * 2 + place.far) * quarter
        ids = lax.broadcasted_iota(jnp.int32, (quarter, 1), 0) + first
        result = h1_ref[b] + second.total(b) + vec_ref[5:6, :feats]
        lay_buf[b] = jnp.where(ids < len_ref[0], result, 0.0).astype(BF)
        spread.begin(b)

    def norm_block(b):
        grad_a = summing.total(b)
        normed, inverse = normalize(tok_ref[b].astype(F32))
        in_ref[b] = (gh1_ref[b] + normalize_back(grad_a, normed, inverse, vec_ref[0:1, :feats])).astype(BF)
        gvec_ref[0:1, :] += column_sum(grad_a * normed)
        gvec_ref[1:2, :] += column_sum(grad_a)

    @pl.when(g == 0)
    def _():
        greet(n_dp, n_tensor)
        over(second.begin, 0, nb)
        parts[0].begin()
        parts[1].begin()
        for ref in (dk_ref, dv_ref, accj, acco, gvec_ref, gbias_ref):
            ref[...] = jnp.zeros_like(ref)
        lanes = lax.broadcasted_iota(jnp.int32, (bq, 128), 1)

        def fill(b):
            first = pl.multiple_of(b * bq, bq)
            fill_keys(qkv_ref, ka_ref, heads, d, slope_fn(heads, total_heads), first, bq)
            rows = pl.ds(first, bq)
            kt_ref[b] = (qkv_ref[rows, width:2 * width].astype(F32) * (1.0 / d**0.5)).astype(BF).T
            for h in range(heads):
                tile = head_tile(qkv_ref, rows, 2 * width, h, d)
                va_ref[h, rows, :] = jnp.where(lanes < d, tile, jnp.where(lanes < d + 3, 1.0, 0.0)).astype(BF)

        over(fill, 0, nb)
        over(second.pass_on, 0, nb)

    rows_i = pl.ds(pl.multiple_of(i * bq, bq), bq)
    grad_o = dot(gh_ref[...], wo_ref[...]).astype(BF)
    grad_t = grad_o.T
    q_nat = qkv_ref[rows_i, 0:width]
    qt = q_nat.T
    lanes = lax.broadcasted_iota(jnp.int32, (bq, 128), 1)
    queries, grads, q_pair, g_pair = [], [], [], []
    for h in range(heads):
        hs = slice(h * d, (h + 1) * d)
        delta = jnp.sum(grad_t[hs].astype(F32) * ot_ref[hs, :], axis=0, keepdims=True)
        queries.append(jnp.concatenate(
            [qt[hs], stack_rows((128 - d, bq), (1.0, 1.0, 1.0) + three(-lse_ref[0, h:h + 1, :]))], axis=0))
        grads.append(jnp.concatenate([grad_t[hs], stack_rows((128 - d, bq), three(-delta))], axis=0))
        pair = slice((h // 2) * 128, (h // 2) * 128 + 128)
        mine = (lanes < d) if h % 2 == 0 else (lanes >= d)
        q_pair.append(jnp.where(mine, q_nat[:, pair].astype(F32), 0.0).astype(BF))
        g_pair.append(jnp.where(mine, grad_o[:, pair].astype(F32), 0.0).astype(BF))

    def block(j, carry, last):
        out = []
        kr = pl.ds(pl.multiple_of(j * bq, bq), bq)
        for h in range(heads):
            s = dot(ka_ref[h, kr, :], queries[h])
            if last:
                s = causal(s, bq, bq)
            p = jnp.exp(s)
            gs = (p * dot(va_ref[h, kr, :], grads[h])).astype(BF)
            pair = slice((h // 2) * 128, (h // 2) * 128 + 128)
            dv_ref[kr, pair] += dot(p.astype(BF), g_pair[h])
            dk_ref[kr, pair] += dot(gs, q_pair[h])
            out.append(carry[h] + dot(kt_ref[j, h * d:(h + 1) * d, :], gs))
        return tuple(out)

    carry = lax.fori_loop(0, i, lambda j, c: block(j, c, False), (jnp.zeros((d, bq), F32),) * heads)

    @pl.when(g >= 1)
    def _():
        summing.pass_on(i + 1)

    @pl.when(g >= 2)
    def _():
        norm_block(i + 2)

    @pl.when(g == 0)
    def _():
        parts[0].pass_on()
        parts[2].begin()
        layer_block(nb - 1)

    @pl.when(g == 1)
    def _():
        parts[2].pass_on()
        spread.relay(i + 1)

    carry = block(i, carry, True)
    gqkv_buf[:, 0:width] = jnp.concatenate(carry, axis=0).T.astype(BF)
    gqkv_buf[:, width:2 * width] = dk_ref[rows_i, :].astype(BF)
    gqkv_buf[:, 2 * width:] = dv_ref[rows_i, :].astype(BF)
    part_ref[i] = dot(gqkv_buf[...], wj_ref[...], NT).astype(BF)
    summing.begin(i)
    gbias_ref[...] += column_sum(gqkv_buf[...].astype(F32))
    acco[...] += dot(ot_ref[...].astype(BF), gh_ref[...])
    accj[...] += dot(a_ref[...], gqkv_buf[...], TN)

    @pl.when(g == 0)
    def _():
        parts[1].pass_on()
        parts[3].begin()
        for b in range(nb - 2, -1, -1):
            layer_block(b)

    @pl.when(g == 1)
    def _():
        parts[3].pass_on()
        for b in range(nb - 2, -1, -1):
            spread.relay(b)

    @pl.when(g == nb - 1)
    def _():
        summing.pass_on(0)
        if nb >= 2:
            norm_block(1)
        gj_ref[...] = accj[...].astype(BF)
        go_ref[...] = acco[...].T.astype(BF)
        norm_block(0)

        def close(b):
            summing.finish(b)
            second.finish(b)
            spread.finish(b)

        for part in parts:
            part.finish()

        over(close, 0, nb)


def attend_back(lengths, qkv, wo, wj, gh, a, ot, lse, tok_own, gh1, h1, vec, mlp, gw1, gw2, heads, d, total_heads, bq,
                n_dp, n_tensor, collective_id):
    n, width = qkv.shape[0], heads * d
    nb = n // bq
    feats = wo.shape[0]
    quarter = bq // 4
    own = (nb, quarter, feats)
    back = lambda i: nb - 1 - i
    dma = pltpu.SemaphoreType.DMA
    hidden = gw1.shape[1]
    step = hidden // 2
    cuts = [(index, first, step, index * hidden + first) for index in range(2) for first in range(0, hidden, step)]
    shard = feats // n_dp
    rows = pl.BlockSpec((bq, feats), lambda i: (back(i), 0))
    vm = pltpu.VMEM
    return pl.pallas_call(
        functools.partial(attend_back_kernel, heads, d, total_heads, bq, nb, n_dp, n_tensor, cuts),
        grid=(nb,),
        in_specs=[pl.BlockSpec(memory_space=pltpu.SMEM), whole(qkv), whole(wo), whole(wj), rows, rows,
                  pl.BlockSpec((width, bq), lambda i: (0, back(i))),
                  pl.BlockSpec((1, heads, bq), lambda i: (back(i), 0, 0)),
                  whole(tok_own), whole(gh1), whole(h1), whole(vec), ANYWHERE, whole(gw1), whole(gw2)],
        out_specs=[fixed((feats, 3 * width)), fixed((feats, width)), fixed(own), ANYWHERE, fixed((8, feats)),
                   fixed((1, 3 * width)), fixed((shard, 2 * hidden))],
        out_shape=[jax.ShapeDtypeStruct((feats, 3 * width), BF), jax.ShapeDtypeStruct((feats, width), BF),
                   jax.ShapeDtypeStruct(own, BF), jax.ShapeDtypeStruct((n, feats), BF),
                   jax.ShapeDtypeStruct((8, feats), F32), jax.ShapeDtypeStruct((1, 3 * width), F32),
                   jax.ShapeDtypeStruct((shard, 2 * hidden), F32)],
        scratch_shapes=[vm((heads, n, 128), BF), vm((nb, width, bq), BF), vm((heads, n, 128), BF), vm((n, width), F32),
                        vm((n, width), F32), vm((bq, 3 * width), BF), vm((feats, 3 * width), F32), vm((width, feats), F32),
                        vm((nb, bq, feats), BF)] + sum_scratch(nb, quarter, feats)
        + [vm((nb, 2 * quarter, feats), BF)] + sum_scratch(nb, quarter, feats)
        + [vm(own, BF), vm((len(cuts), n_dp // 2, shard, step), BF), vm((len(cuts), n_dp // 2, shard, step), BF)]
        + [dma((4, nb)), dma((5, nb)), dma((7, nb)), dma((4, len(cuts), n_dp // 2))],
        compiler_params=params(collective_id, 63),
        name="attend_back",
    )(lengths, qkv, wo, wj, gh, a, ot, lse, tok_own, gh1, h1, vec, mlp, gw1, gw2)


class Scatter:
    def __init__(self, lines, rows, source, first, cols, x_buf, z_buf, total, at, sems, part):
        me = lax.axis_index("dp")
        self.z, self.x = me // 2, lax.rem(me, 2)
        self.lines, self.rows, self.source = lines, rows, source
        self.cols, self.total_cols = pl.ds(first, cols), pl.ds(at, cols)
        self.x_buf, self.z_buf, self.total, self.sems, self.part = x_buf, z_buf, total, sems, part

    def dest(self, k):
        return lax.rem(self.z + 1 + k, self.lines)

    def chunk(self, device):
        return (pl.ds(pl.multiple_of(device * self.rows, self.rows), self.rows), self.cols)

    def sem(self, kind, index):
        return self.sems.at[kind, self.part, index]

    def to_x(self, dz):
        return remote(self.source.at[self.chunk(dz * 2 + 1 - self.x)], self.x_buf.at[dz], self.sem(0, dz),
                      self.sem(1, dz), at_dp(self.z * 2 + 1 - self.x))

    def to_z(self, dz):
        return remote(self.x_buf.at[dz], self.z_buf.at[self.z], self.sem(2, dz), self.sem(3, self.z),
                      at_dp(dz * 2 + self.x))

    def from_z(self, zz):
        return remote(self.z_buf.at[zz], self.z_buf.at[zz], self.sem(2, zz), self.sem(3, zz), at_dp(zz * 2 + self.x))

    def begin(self):
        over(lambda k: self.to_x(self.dest(k)).start(), 0, self.lines)

    def summed(self, dz):
        self.to_x(dz).wait()
        return self.x_buf[dz].astype(F32) + self.source[self.chunk(dz * 2 + self.x)].astype(F32)

    def pass_on(self):
        def step(k):
            dz = self.dest(k)
            self.x_buf[dz] = self.summed(dz).astype(BF)
            self.to_z(dz).start()

        over(step, 0, self.lines - 1)
        self.total[:, self.total_cols] = self.summed(self.z)

    def finish(self):
        def add(k):
            zz = lax.rem(self.z + k, self.lines)
            self.from_z(zz).wait_recv()
            self.total[:, self.total_cols] += self.z_buf[zz].astype(F32)
            self.to_z(zz).wait_send()

        over(add, 1, self.lines)


def scatter_kernel(n_dp, n_tensor, pieces, nb, quarter, *refs):
    arrays = max(index for index, _, _, _ in pieces) + 1
    sources, refs = refs[:arrays], refs[arrays:]
    (vec_ref, in_own, done_ref, total_ref, vec_out, square_out, in_out), refs = refs[:7], refs[7:]
    x_bufs, refs = refs[:len(pieces)], refs[len(pieces):]
    z_bufs, refs = refs[:len(pieces)], refs[len(pieces):]
    v_buf, s_buf, q_buf, t_buf, sems, in_sems, vs, vr, ss, sr, qs, qr, ts, tr = refs
    me, rank = lax.axis_index("dp"), lax.axis_index("tensor")
    lines = n_dp // 2
    rows = total_ref.shape[0]
    place = Place()
    spreads = (BlockSpread(place, quarter, in_own, in_out, in_sems),)
    parts = [
        Scatter(lines, rows, sources[index], first, cols, x_bufs[p], z_bufs[p], total_ref, at, sems, p)
        for p, (index, first, cols, at) in enumerate(pieces)
    ]

    def vec_to(k):
        dest = lax.rem(me + k, n_dp)
        return remote(vec_ref.at[dest], v_buf.at[me], vs.at[k], vr.at[me], at_dp(dest))

    def sum_to(k):
        return remote(s_buf.at[rank], s_buf.at[rank], ss.at[k], sr.at[rank], at_tensor(lax.rem(rank + k, n_tensor)))

    def square_to(k):
        return remote(q_buf.at[me], q_buf.at[me], qs.at[k], qr.at[me], at_dp(lax.rem(me + k, n_dp)))

    def tensor_to(k):
        return remote(t_buf.at[rank], t_buf.at[rank], ts.at[k], tr.at[rank], at_tensor(lax.rem(rank + k, n_tensor)))

    def arrived(buf, source, send, recv, where):
        remote(buf.at[source], buf.at[source], send.at[0], recv.at[source], where).wait_recv()

    greet(n_dp, n_tensor)
    parts[0].begin()
    over(lambda k: vec_to(k).start(), 1, n_dp)
    v_buf[me] = vec_ref[me]
    for spread in spreads:
        over(spread.begin, 0, nb)
    for p, part in enumerate(parts):
        if p + 1 < len(parts):
            parts[p + 1].begin()
        part.pass_on()
        if p == 0:
            def vec_arrived(k):
                source = lax.rem(me + k, n_dp)
                arrived(v_buf, source, vs, vr, at_dp(source))
                vec_to(k).wait_send()

            over(vec_arrived, 1, n_dp)
            s_buf[rank] = lax.fori_loop(0, n_dp, lambda k, acc: acc + v_buf[k], jnp.zeros(vec_out.shape, F32))
            for k in range(1, n_tensor):
                sum_to(k).start()
    for k in range(1, n_tensor):
        source = lax.rem(rank + k, n_tensor)
        arrived(s_buf, source, ss, sr, at_tensor(source))
        sum_to(k).wait_send()
    shared_total = lax.fori_loop(0, n_tensor, lambda k, acc: acc + s_buf[k], jnp.zeros(vec_out.shape, F32))
    row_ids = lax.broadcasted_iota(jnp.int32, vec_out.shape, 0)
    vec_total = jnp.where(row_ids < 6, shared_total, s_buf[rank])
    vec_out[...] = vec_total
    vec_kept = jnp.where(row_ids >= jnp.where(rank == 0, 0, 6), vec_total, 0.0)
    done_square = jnp.sum(done_ref[...] * done_ref[...])
    for part in parts:
        part.finish()
    square = done_square + jnp.sum(total_ref[...] * total_ref[...]) + jnp.sum(vec_kept * vec_kept)
    q_buf[me] = jnp.full(q_buf.shape[1:], square, F32)
    over(lambda k: square_to(k).start(), 1, n_dp)

    def square_arrived(k):
        source = lax.rem(me + k, n_dp)
        arrived(q_buf, source, qs, qr, at_dp(source))
        square_to(k).wait_send()

    over(square_arrived, 1, n_dp)
    t_buf[rank] = lax.fori_loop(0, n_dp, lambda k, acc: acc + q_buf[k], jnp.zeros(q_buf.shape[1:], F32))
    for k in range(1, n_tensor):
        tensor_to(k).start()
    for spread in spreads:
        over(spread.relay, 0, nb)
    for k in range(1, n_tensor):
        source = lax.rem(rank + k, n_tensor)
        arrived(t_buf, source, ts, tr, at_tensor(source))
        tensor_to(k).wait_send()
    square_out[...] = lax.fori_loop(0, n_tensor, lambda k, acc: acc + t_buf[k], jnp.zeros(q_buf.shape[1:], F32))
    for spread in spreads:
        over(spread.finish, 0, nb)


def scatter_gradients(grads, vec, in_own, done, n_dp, n_tensor, collective_id, step=256):
    rows = grads[0].shape[0] // n_dp
    lines = n_dp // 2
    pieces, at = [], 0
    for index, grad in enumerate(grads):
        cols = grad.shape[1]
        cut = step if cols % step == 0 else cols
        for first in range(0, cols, cut):
            pieces.append((index, first, cut, at))
            at += cut
    nb, quarter, feats = in_own.shape
    vmem = pl.BlockSpec(memory_space=pltpu.VMEM)
    dma = pltpu.SemaphoreType.DMA
    tile = (8, 128)
    full = jax.ShapeDtypeStruct((nb * quarter * n_tensor, feats), BF)
    bufs = [pltpu.VMEM((lines, rows, cols), BF) for _, _, cols, _ in pieces]
    return pl.pallas_call(
        functools.partial(scatter_kernel, n_dp, n_tensor, pieces, nb, quarter),
        in_specs=[vmem] * (len(grads) + 1) + [ANYWHERE, vmem],
        out_specs=[vmem, vmem, vmem, ANYWHERE],
        out_shape=[jax.ShapeDtypeStruct((rows, at), F32), jax.ShapeDtypeStruct(vec.shape[1:], F32),
                   jax.ShapeDtypeStruct(tile, F32), full],
        scratch_shapes=bufs + bufs + [pltpu.VMEM(vec.shape, F32), pltpu.VMEM((n_tensor,) + vec.shape[1:], F32),
                                      pltpu.VMEM((n_dp,) + tile, F32), pltpu.VMEM((n_tensor,) + tile, F32)]
        + [dma((4, len(pieces), lines)), dma((7, nb))] + [dma((n_dp,))] * 2 + [dma((n_tensor,))] * 2
        + [dma((n_dp,))] * 2 + [dma((n_tensor,))] * 2,
        compiler_params=params(collective_id, 48),
        name="scatter_gradients",
    )(*grads, vec, in_own, done)


def adam_step(master, moment, variance, gradient, rate, decay):
    moment_new = BETA_FIRST * moment + (1.0 - BETA_FIRST) * gradient
    variance_new = BETA_SECOND * variance + (1.0 - BETA_SECOND) * gradient * gradient
    moment_hat = moment_new / (1.0 - BETA_FIRST**STEP)
    variance_hat = variance_new / (1.0 - BETA_SECOND**STEP)
    master_new = master - rate * (
        moment_hat / (jnp.sqrt(variance_hat) + ADAM_EPSILON) + decay * master
    )
    return (master_new, moment_new, variance_new)


def update_kernel(head_size, turned, square_ref, near_ref, done_ref, vec_ref, *refs):
    ins, outs = refs[:18], refs[18:]
    norm = jnp.sqrt(square_ref[0:1, 0:1])
    factor = jnp.minimum(1.0, CLIP_LIMIT / (norm + 1e-06))

    def step(at, gradient, rate, decay, cols=slice(None)):
        new = adam_step(*[ref[:, cols] for ref in ins[3 * at:3 * at + 3]], factor * gradient, rate, decay)
        for ref, value in zip(outs[3 * at:3 * at + 3], new):
            ref[:, cols] = value

    joint, hidden = ins[0].shape[1], ins[6].shape[1]
    heads = joint // (3 * head_size)

    def source(piece):
        head, kind = piece // 3, piece % 3
        first = (kind * heads + head) * head_size
        return near_ref[:, first:first + head_size]

    for piece in range(0, joint // head_size, 2):
        cols = slice(piece * head_size, (piece + 2) * head_size)
        step(0, jnp.concatenate([source(piece), source(piece + 1)], axis=1), MATRIX_RATE, MATRIX_DECAY, cols)
    output, narrow = near_ref[:, joint:], done_ref[:, hidden:]
    if turned:
        output, narrow = output.T, narrow.T
        step(1, output, OUTPUT_RATE, MATRIX_DECAY)
        step(3, narrow, MATRIX_RATE, MATRIX_DECAY)
    step(2, done_ref[:, :hidden], MATRIX_RATE, MATRIX_DECAY)
    step(4, vec_ref[0:6, :ins[12].shape[1]], VECTOR_RATE, 0.0)
    step(5, vec_ref[6:7, :ins[15].shape[1]], VECTOR_RATE, 0.0)


def update(square, near, done, vec, states, head_size):
    vmem = pl.BlockSpec(memory_space=pltpu.VMEM)
    return pl.pallas_call(
        functools.partial(update_kernel, head_size, True),
        in_specs=[vmem] * (4 + len(states)),
        out_specs=[vmem] * len(states),
        out_shape=[jax.ShapeDtypeStruct(state.shape, F32) for state in states],
        compiler_params=pltpu.CompilerParams(vmem_limit_bytes=48 * 2**20),
        name="update",
    )(square, near, done, vec, *states)


def on_device(
    tokens,
    cotangent,
    lengths,
    joint_weight,
    output_weight,
    widen_weight,
    narrow_weight,
    shared_vectors,
    split_vectors,
    joint_first,
    joint_second,
    output_first,
    output_second,
    widen_first,
    widen_second,
    narrow_first,
    narrow_second,
    shared_first,
    shared_second,
    split_first,
    split_second,
):
    n_dp, n_tensor = lax.axis_size("dp"), lax.axis_size("tensor")
    me, tensor_rank = lax.axis_index("dp"), lax.axis_index("tensor")
    joint_cols, head_cols, hidden = joint_weight.shape[1], output_weight.shape[0], widen_weight.shape[1]
    near_shard = jnp.concatenate([by_kind(joint_weight), output_weight.T], axis=1).astype(BF)
    far_shard = jnp.concatenate([widen_weight, narrow_weight.T], axis=1).astype(BF)
    shared_cols, split_cols = shared_vectors.shape[1], split_vectors.shape[1]
    vec_shard = jnp.zeros((16, n_dp * max(shared_cols, split_cols)), BF)
    vec_shard = lax.dynamic_update_slice(vec_shard, shared_vectors.astype(BF), (0, me * shared_cols))
    vec_shard = lax.dynamic_update_slice(vec_shard, split_vectors.astype(BF), (6, me * split_cols))
    head_size = D // HEADS
    local_heads = head_cols // head_size
    total_rows = tokens.shape[0]
    block = min(512, total_rows)
    blocks, quarter = total_rows // block, block // 4
    slot = lax.rem(tensor_rank, 2) * 2 + tensor_rank // 2
    own_tokens = lax.dynamic_index_in_dim(tokens.reshape(blocks, 4, quarter, D), slot, 1, keepdims=False)

    attn_input, qkv, joint_work, output_t, vec = project(
        tokens, near_shard, vec_shard, joint_cols, head_cols, 1.0 / math.sqrt(head_size), n_dp, n_tensor, 0
    )
    step = hidden // 2
    cuts = ((0, step), (step, step), (2 * step, step), (3 * step, step // 2), (3 * step + step // 2, step // 2))
    heads_out, lse, hidden_one, mlp_input, far_work = attend(
        qkv, output_t, own_tokens, vec, far_shard, cuts, local_heads, head_size, HEADS, block, n_dp, n_tensor, 1
    )
    mlp_part, grad_widen, grad_narrow, grad_hidden, grad_hidden_low, feed_vec, widen_bias_grad = feed(
        lengths, mlp_input, cotangent, far_work, 2 * head_cols, hidden_one, vec, block, n_tensor, 2
    )
    grad_joint, grad_output, input_own, layer_output, attend_vec, qkv_bias_grad, far_sum = attend_back(
        lengths, qkv, output_t, joint_work, grad_hidden_low, attn_input, heads_out, lse, own_tokens, grad_hidden,
        hidden_one, vec, mlp_part, grad_widen, grad_narrow, local_heads, head_size, HEADS, block, n_dp, n_tensor, 3,
    )
    vec_cols = -(-max(shared_cols, split_cols) // 128) * 128
    grad_shared = jnp.concatenate([attend_vec[:2], feed_vec[:4]], axis=0)
    grad_split = jnp.concatenate(
        [qkv_bias_grad[0, :head_cols], qkv_bias_grad[0, 2 * head_cols :], widen_bias_grad[0]]
    )
    grad_vecs = jnp.concatenate(
        [
            jnp.pad(
                jnp.swapaxes(grad_shared.reshape(6, n_dp, shared_cols), 0, 1),
                ((0, 0), (0, 0), (0, vec_cols - shared_cols)),
            ),
            jnp.pad(grad_split.reshape(n_dp, 1, split_cols), ((0, 0), (0, 1), (0, vec_cols - split_cols))),
        ],
        axis=1,
    )
    near_sum, vec_sum, square, input_grad = scatter_gradients(
        (grad_joint, grad_output), grad_vecs, input_own, far_sum, n_dp, n_tensor, 4
    )
    states = (
        joint_weight, joint_first, joint_second, output_weight, output_first, output_second,
        widen_weight, widen_first, widen_second, narrow_weight, narrow_first, narrow_second,
        shared_vectors, shared_first, shared_second, split_vectors, split_first, split_second,
    )
    updated = update(square, near_sum, far_sum, vec_sum, states, head_size)
    return (layer_output, input_grad, jnp.sqrt(square[0, 0]), *updated)


def solution(mesh):
    in_specs = (
        P("dp", None),
        P("dp", None),
        P("dp"),
        P("dp", "tensor"),
        P("tensor", "dp"),
        P("dp", "tensor"),
        P("tensor", "dp"),
        P(None, "dp"),
        P("tensor", "dp"),
        P("dp", "tensor"),
        P("dp", "tensor"),
        P("tensor", "dp"),
        P("tensor", "dp"),
        P("dp", "tensor"),
        P("dp", "tensor"),
        P("tensor", "dp"),
        P("tensor", "dp"),
        P(None, "dp"),
        P(None, "dp"),
        P("tensor", "dp"),
        P("tensor", "dp"),
    )
    out_specs = (
        P("dp", None),
        P("dp", None),
        P(),
        P("dp", "tensor"),
        P("dp", "tensor"),
        P("dp", "tensor"),
        P("tensor", "dp"),
        P("tensor", "dp"),
        P("tensor", "dp"),
        P("dp", "tensor"),
        P("dp", "tensor"),
        P("dp", "tensor"),
        P("tensor", "dp"),
        P("tensor", "dp"),
        P("tensor", "dp"),
        P(None, "dp"),
        P(None, "dp"),
        P(None, "dp"),
        P("tensor", "dp"),
        P("tensor", "dp"),
        P("tensor", "dp"),
    )
    return jax.shard_map(
        on_device, mesh=mesh, in_specs=in_specs, out_specs=out_specs, check_vma=False
    )
```

```python
import functools
import math

import jax
import jax.numpy as jnp
from jax import lax
from jax.experimental import pallas as pl
from jax.experimental.pallas import tpu as pltpu
from jax.sharding import PartitionSpec as P

F32, BF = jnp.float32, jnp.bfloat16

D = 1024
HEADS = 16
STEP = 10


NORM_EPSILON = 1e-05
CLIP_LIMIT = 1.0
BETA_FIRST = 0.9
BETA_SECOND = 0.95
ADAM_EPSILON = 1e-08
MATRIX_RATE = 0.05
OUTPUT_RATE = 0.2
VECTOR_RATE = 0.6
MATRIX_DECAY = 0.1


def by_kind(values):
    rows, cols = values.shape
    size = D // HEADS
    return jnp.swapaxes(values.reshape(rows, cols // (3 * size), 3, size), 1, 2).reshape(rows, cols)


NN = (((1,), (0,)), ((), ()))
NT = (((1,), (1,)), ((), ()))
TN = (((0,), (0,)), ((), ()))
LOW = -1e30


def dot(left, right, dims=NN):
    return lax.dot_general(left, right, dims, preferred_element_type=F32)


def three(values):
    high = values.astype(BF).astype(F32)
    rest = values - high
    middle = rest.astype(BF).astype(F32)
    return high, middle, rest - middle


def stack_rows(shape, rows):
    ids = lax.broadcasted_iota(jnp.int32, shape, 0)
    out = jnp.zeros(shape, F32)
    for at, row in enumerate(rows):
        out = jnp.where(ids == at, row, out)
    return out.astype(BF)


def head_tile(ref, rows, col, head, d):
    lane = col + (head // 2) * 128
    tile = ref[rows, lane:lane + 128].astype(F32)
    if head % 2:
        tile = pltpu.roll(tile, 64, 1)
    return tile


def fill_keys(qkv_ref, ka_ref, heads, d, slope_of, first, count):
    rows = pl.ds(first, count)
    lanes = lax.broadcasted_iota(jnp.int32, (count, 128), 1)
    position = (lax.broadcasted_iota(jnp.int32, (count, 128), 0) + first).astype(F32)
    for head in range(heads):
        high, middle, low = three(position * slope_of(head))
        tile = head_tile(qkv_ref, rows, heads * d, head, d)
        for at, part in enumerate((high, middle, low, 1.0, 1.0, 1.0)):
            tile = jnp.where(lanes == d + at, part, tile)
        ka_ref[head, rows, :] = jnp.where(lanes < d + 6, tile, 0.0).astype(BF)


def causal(scores, bk, bq):
    kid = lax.broadcasted_iota(jnp.int32, (bk, bq), 0)
    qid = lax.broadcasted_iota(jnp.int32, (bk, bq), 1)
    return jnp.where(kid <= qid, scores, LOW)


def slope_fn(heads, total_heads):
    rank = lax.axis_index("tensor")
    def slope_of(head):
        index = jnp.full((1, 128), rank * heads + head + 1, jnp.int32).astype(F32)
        return jnp.exp2(index * (-8.0 / total_heads))
    return slope_of


def at_dp(index):
    return {"dp": index}


def at_tensor(index):
    return {"tensor": index}


def remote(src, dst, send, recv, where):
    return pltpu.make_async_remote_copy(
        src_ref=src, dst_ref=dst, send_sem=send, recv_sem=recv, device_id=where, device_id_type=pl.DeviceIdType.MESH
    )


def greet(n_dp, n_tensor):
    me, rank = lax.axis_index("dp"), lax.axis_index("tensor")
    barrier = pltpu.get_barrier_semaphore()

    def along_dp(k, c):
        pl.semaphore_signal(barrier, inc=1, device_id=at_dp(lax.rem(me + k, n_dp)), device_id_type=pl.DeviceIdType.MESH)
        return c

    lax.fori_loop(1, n_dp, along_dp, 0)
    for k in range(1, n_tensor):
        pl.semaphore_signal(
            barrier, inc=1, device_id=at_tensor(lax.rem(rank + k, n_tensor)), device_id_type=pl.DeviceIdType.MESH
        )
    pl.semaphore_wait(barrier, n_dp + n_tensor - 2)


def over(body, first, last):
    lax.fori_loop(first, last, lambda k, c: (body(k), c)[1], 0)


def greet_tensor(n_tensor):
    rank = lax.axis_index("tensor")
    barrier = pltpu.get_barrier_semaphore()
    for k in range(1, n_tensor):
        pl.semaphore_signal(
            barrier, inc=1, device_id=at_tensor(lax.rem(rank + k, n_tensor)), device_id_type=pl.DeviceIdType.MESH
        )
    pl.semaphore_wait(barrier, n_tensor - 1)


class Gather:
    def __init__(self, lines, rows, pieces, sems):
        me = lax.axis_index("dp")
        self.me, self.z, self.x = me, me // 2, lax.rem(me, 2)
        self.lines, self.rows, self.pieces, self.sems = lines, rows, pieces, sems
        self.other = at_dp(self.z * 2 + 1 - self.x)

    def own(self, s):
        shard, first, _, cols = self.pieces[s][:4]
        return shard.at[:, pl.ds(first, cols)]

    def spot(self, s, device):
        _, _, first, cols, out = self.pieces[s]
        return out.at[pl.ds(pl.multiple_of(device * self.rows, self.rows), self.rows), pl.ds(first, cols)]

    def to_x(self, s, zz, src):
        return remote(src, self.spot(s, zz * 2 + self.x), self.sems.at[0, s, zz], self.sems.at[1, s, zz], self.other)

    def from_x(self, s, zz):
        spot = self.spot(s, zz * 2 + 1 - self.x)
        return remote(spot, spot, self.sems.at[0, s, zz], self.sems.at[1, s, zz], self.other)

    def to_z(self, s, k):
        target = lax.rem(self.z + k, self.lines) * 2 + self.x
        return remote(self.own(s), self.spot(s, self.me), self.sems.at[2, s, k], self.sems.at[3, s, self.z], at_dp(target))

    def from_z(self, s, zz):
        spot = self.spot(s, zz * 2 + self.x)
        return remote(spot, spot, self.sems.at[2, s, 0], self.sems.at[3, s, zz], self.other)

    def keep(self, s):
        return pltpu.make_async_copy(self.own(s), self.spot(s, self.me), self.sems.at[2, s, 0])

    def begin_z(self, s):
        over(lambda k: self.to_z(s, k).start(), 1, self.lines)
        self.keep(s).start()

    def begin_x(self, s):
        self.to_x(s, self.z, self.own(s)).start()

    def begin(self, s):
        self.begin_z(s)
        self.begin_x(s)

    def forward(self, s):
        def step(k):
            zz = lax.rem(self.z + k, self.lines)
            self.from_z(s, zz).wait_recv()
            self.to_x(s, zz, self.spot(s, zz * 2 + self.x)).start()

        over(step, 1, self.lines)

    def finish(self, s):
        self.keep(s).wait()
        over(lambda k: self.to_z(s, k).wait_send(), 1, self.lines)
        over(lambda zz: self.to_x(s, zz, self.own(s)).wait_send(), 0, self.lines)
        over(lambda zz: self.from_x(s, zz).wait_recv(), 0, self.lines)


class Place:
    def __init__(self):
        rank = lax.axis_index("tensor")
        self.far, self.near = rank // 2, lax.rem(rank, 2)
        self.near_device = at_tensor(self.far * 2 + 1 - self.near)
        self.far_device = at_tensor((1 - self.far) * 2 + self.near)


class BlockSum:
    def __init__(self, place, quarter, part, slot, near_buf, send_buf, far_buf, sems):
        self.place, self.quarter, self.part, self.slot = place, quarter, part, slot
        self.near_buf, self.send_buf, self.far_buf, self.sems = near_buf, send_buf, far_buf, sems

    def rows(self, near, far):
        first = (near * 2 + far) * self.quarter
        return pl.ds(pl.multiple_of(first, self.quarter), self.quarter)

    def half(self, near):
        first = near * 2 * self.quarter
        return pl.ds(pl.multiple_of(first, self.quarter), 2 * self.quarter)

    def to_near(self, b):
        return remote(self.part.at[self.slot(b), self.half(1 - self.place.near)], self.near_buf.at[b],
                      self.sems.at[0, b], self.sems.at[1, b], self.place.near_device)

    def to_far(self, b):
        return remote(self.send_buf.at[b], self.far_buf.at[b], self.sems.at[2, b], self.sems.at[3, b],
                      self.place.far_device)

    def pair(self, b, far):
        own = self.part[self.slot(b), self.rows(self.place.near, far)].astype(F32)
        return own + self.near_buf[b, self.rows(0, far)].astype(F32)

    def begin(self, b):
        self.to_near(b).start()

    def stage(self, b):
        self.to_near(b).wait_recv()
        self.send_buf[b] = self.pair(b, 1 - self.place.far).astype(BF)

    def pass_on(self, b):
        self.stage(b)
        self.to_far(b).start()

    def total(self, b):
        self.to_far(b).wait()
        self.to_near(b).wait_send()
        return self.pair(b, self.place.far) + self.far_buf[b].astype(F32)

    def stage_all(self, b):
        self.stage(b)
        rows = self.rows(0, self.place.far)
        self.near_buf[b, rows] = self.pair(b, self.place.far).astype(BF)
        self.to_near(b).wait_send()

    def late_total(self, b):
        self.to_far(b).wait()
        return self.near_buf[b, self.rows(0, self.place.far)].astype(F32) + self.far_buf[b].astype(F32)


class BlockSpread:
    def __init__(self, place, quarter, out, sems, own=None):
        self.place, self.quarter, self.out, self.sems, self.own = place, quarter, out, sems, own

    def rows(self, b, near, far):
        first = (b * 4 + near * 2 + far) * self.quarter
        return pl.ds(pl.multiple_of(first, self.quarter), self.quarter)

    def spot(self, b, near, far):
        return self.out.at[self.rows(b, near, far)]

    def mine(self, b):
        return self.spot(b, self.place.near, self.place.far)

    def source(self, b):
        return self.mine(b) if self.own is None else self.own.at[b]

    def put(self, b, values):
        if self.own is None:
            self.out[self.rows(b, self.place.near, self.place.far), :] = values
        else:
            self.own[b] = values
        self.to_far(b).start()
        self.to_near(b).start()
        if self.own is not None:
            self.keep(b).start()

    def to_far(self, b):
        return remote(self.source(b), self.mine(b), self.sems.at[0, b], self.sems.at[1, b], self.place.far_device)

    def to_near(self, b):
        return remote(self.source(b), self.mine(b), self.sems.at[2, b], self.sems.at[3, b], self.place.near_device)

    def arrival(self, near, far, b, at):
        spot = self.spot(b, near, far)
        return remote(spot, spot, self.sems.at[at - 1, b], self.sems.at[at, b], self.place.near_device)

    def pass_far(self, b):
        spot = self.spot(b, self.place.near, 1 - self.place.far)
        return remote(spot, spot, self.sems.at[4, b], self.sems.at[5, b], self.place.near_device)

    def keep(self, b):
        return pltpu.make_async_copy(self.own.at[b], self.mine(b), self.sems.at[6, b])

    def relay(self, b):
        self.arrival(self.place.near, 1 - self.place.far, b, 1).wait_recv()
        self.pass_far(b).start()

    def finish(self, b):
        self.to_far(b).wait_send()
        self.to_near(b).wait_send()
        self.pass_far(b).wait_send()
        if self.own is not None:
            self.keep(b).wait()
        self.arrival(1 - self.place.near, self.place.far, b, 3).wait_recv()
        self.arrival(1 - self.place.near, 1 - self.place.far, b, 5).wait_recv()


def normalize(values):
    centred = values - jnp.mean(values, axis=-1, keepdims=True)
    inverse = lax.rsqrt(jnp.mean(centred * centred, axis=-1, keepdims=True) + NORM_EPSILON)
    return (centred * inverse, inverse)


def normalize_back(incoming, normed, inverse, gain):
    scaled = incoming * gain
    return inverse * (
        scaled
        - jnp.mean(scaled, axis=-1, keepdims=True)
        - normed * jnp.mean(scaled * normed, axis=-1, keepdims=True)
    )


def column_sum(values):
    return jnp.sum(values, axis=0, keepdims=True)


def params(collective_id, megabytes):
    return pltpu.CompilerParams(
        collective_id=collective_id, has_side_effects=True, vmem_limit_bytes=megabytes * 2**20
    )


ANYWHERE = pl.BlockSpec(memory_space=pl.ANY)


def fixed(shape):
    return pl.BlockSpec(shape, lambda i: (0,) * len(shape), pipeline_mode=pl.Buffered(1))


def whole(array):
    return fixed(array.shape)


class Scatter:
    def __init__(self, lines, rows, source, first, cols, x_buf, z_buf, total, at, sems, part):
        me = lax.axis_index("dp")
        self.z, self.x = me // 2, lax.rem(me, 2)
        self.lines, self.rows, self.source = lines, rows, source
        self.cols, self.total_cols = pl.ds(first, cols), pl.ds(at, cols)
        self.x_buf, self.z_buf, self.total, self.sems, self.part = x_buf, z_buf, total, sems, part

    def dest(self, k):
        return lax.rem(self.z + 1 + k, self.lines)

    def chunk(self, device):
        return (pl.ds(pl.multiple_of(device * self.rows, self.rows), self.rows), self.cols)

    def sem(self, kind, index):
        return self.sems.at[kind, self.part, index]

    def to_x(self, dz):
        return remote(self.source.at[self.chunk(dz * 2 + 1 - self.x)], self.x_buf.at[dz], self.sem(0, dz),
                      self.sem(1, dz), at_dp(self.z * 2 + 1 - self.x))

    def to_z(self, dz):
        return remote(self.x_buf.at[dz], self.z_buf.at[self.z], self.sem(2, dz), self.sem(3, self.z),
                      at_dp(dz * 2 + self.x))

    def from_z(self, zz):
        return remote(self.z_buf.at[zz], self.z_buf.at[zz], self.sem(2, zz), self.sem(3, zz), at_dp(zz * 2 + self.x))

    def begin(self):
        over(lambda k: self.to_x(self.dest(k)).start(), 0, self.lines)

    def summed(self, dz):
        self.to_x(dz).wait()
        return self.x_buf[dz].astype(F32) + self.source[self.chunk(dz * 2 + self.x)].astype(F32)

    def pass_on(self):
        def step(k):
            dz = self.dest(k)
            self.x_buf[dz] = self.summed(dz).astype(BF)
            self.to_z(dz).start()

        over(step, 0, self.lines - 1)
        self.total[:, self.total_cols] = self.summed(self.z)

    def finish(self):
        def add(k):
            zz = lax.rem(self.z + k, self.lines)
            self.from_z(zz).wait_recv()
            self.total[:, self.total_cols] += self.z_buf[zz].astype(F32)
            self.to_z(zz).wait_send()

        over(add, 1, self.lines)


class Exchange:
    def __init__(self, buf, index, count, where, send, recv):
        self.buf, self.index, self.count, self.where = buf, index, count, where
        self.send, self.recv = send, recv

    def to(self, k):
        other = lax.rem(self.index + k, self.count)
        return remote(self.buf.at[self.index], self.buf.at[self.index], self.send.at[k], self.recv.at[self.index],
                      self.where(other))

    def begin(self, values):
        self.buf[self.index] = values
        over(lambda k: self.to(k).start(), 1, self.count)

    def total(self):
        def arrived(k):
            other = lax.rem(self.index + k, self.count)
            remote(self.buf.at[other], self.buf.at[other], self.send.at[0], self.recv.at[other],
                   self.where(other)).wait_recv()
            self.to(k).wait_send()

        over(arrived, 1, self.count)
        zero = jnp.zeros(self.buf.shape[1:], F32)
        return lax.fori_loop(0, self.count, lambda k, acc: acc + self.buf[k].astype(F32), zero)


def layer_kernel(dims, len_ref, tok_ref, cot_ref, near_shard, far_shard, vec_shard,
                 total_ref, vec_out, square_out, in_out, lay_out, a_hbm, *scratch):
    heads, d, total_heads, bq, nb, n_dp, n_tensor, near_cuts, far_cuts, sum_cuts = dims
    (qkv, ka, big, wj, wo, ac, low, ot, lse, h1, gh1, acc, hid_buf, gu_buf, cot_buf,
     part, near_buf, send_buf, far_buf, part2, near2_buf, send2_buf, far2_buf, x_far, z_far, x_near, z_near,
     vec_buf, vec, vpart, v_buf, s_buf, q_buf, t_buf,
     gn_sems, gf_sems, sum_sems, spread_sems, sf_sems, sn_sems, copy_sems, vs, vr, vs2, vr2, qs, qr, ss, sr, ts, tr) = scratch
    s = pl.program_id(0)
    place = Place()
    me, rank = lax.axis_index("dp"), lax.axis_index("tensor")
    width, feats, hidden = heads * d, ac.shape[1], big.shape[1] // 2
    quarter, lines, rows = bq // 4, n_dp // 2, total_ref.shape[0]
    last = nb - 1
    halves = (slice(0, feats // 2), slice(feats // 2, feats))
    small = n_dp <= 8

    def slot_from(base):
        return lambda b: lax.rem(base + last - b, 3)

    sum1, sum3, sum4 = (
        BlockSum(place, quarter, part, slot_from(k * nb), near_buf, send_buf, far_buf, sum_sems.at[k]) for k in range(3)
    )
    sum2 = BlockSum(place, quarter, part2, lambda b: lax.rem(last - b, 2), near2_buf, send2_buf, far2_buf, sum_sems.at[3])
    spread_c = BlockSpread(place, quarter, ac, spread_sems.at[0])
    spread_low = BlockSpread(place, quarter, low, spread_sems.at[1])
    spread_lay = BlockSpread(place, quarter, lay_out, spread_sems.at[2], send2_buf)
    spread_in = BlockSpread(place, quarter, in_out, spread_sems.at[3], send_buf)
    near_gather = Gather(lines, rows, [(near_shard, first, at, cols, (wj, wo)[index]) for index, first, at, cols in near_cuts],
                         gn_sems)
    far_gather = Gather(lines, rows, [(far_shard, first, first, cols, big) for first, cols in far_cuts], gf_sems)
    grads_near = part2.reshape(2 * bq, feats)
    far_parts = [
        Scatter(lines, rows, big, first, cols, x_far.at[p], z_far.at[p], total_ref, feats + first, sf_sems, p)
        for p, (first, cols) in enumerate(sum_cuts[0])
    ]
    near_parts = [
        Scatter(lines, rows, grads_near, first, cols, x_near.at[p], z_near.at[p], total_ref, first, sn_sems, p)
        for p, (first, cols) in enumerate(sum_cuts[1])
    ]
    vec_gather = Exchange(vec_buf, me, n_dp, at_dp, vs, vr)
    vec_sum = Exchange(v_buf, me, n_dp, at_dp, vs2, vr2)
    vec_tensor = Exchange(s_buf, rank, n_tensor, at_tensor, ss, sr)
    square_sum = Exchange(q_buf, me, n_dp, at_dp, qs, qr)
    square_tensor = Exchange(t_buf, rank, n_tensor, at_tensor, ts, tr)

    def block_rows(b):
        return pl.ds(pl.multiple_of(b * bq, bq), bq)

    def turned_spot(b, first=0, count=None):
        row = pl.multiple_of(lax.rem(b, 2) * width + first, d)
        return (pl.ds(row, width if count is None else count), pl.ds(pl.multiple_of(b // 2 * bq, bq), bq))

    def value_spot(h, b):
        lane = pl.multiple_of(((h % 2) * nb + b) * 128, 128)
        return (h // 2, slice(None), pl.ds(lane, 128))

    def own_rows(b):
        return spread_c.rows(b, place.near, place.far)

    def copy_tokens():
        return pltpu.make_async_copy(tok_ref, low, copy_sems.at[0])

    def copy_a(b):
        return pltpu.make_async_copy(ac.at[block_rows(b)], a_hbm.at[block_rows(b)], copy_sems.at[1 + b])

    def copy_back():
        return pltpu.make_async_copy(a_hbm, ac, copy_sems.at[0])

    def copy_cot(b):
        return pltpu.make_async_copy(cot_ref.at[block_rows(b)], cot_buf, copy_sems.at[0])

    def own_spot(b):
        return pl.ds(pl.multiple_of(b * quarter, quarter), quarter)

    def copy_own(b):
        return pltpu.make_async_copy(tok_ref.at[own_rows(b)], cot_buf.at[own_spot(b)], copy_sems.at[1 + b])

    def norm1(b):
        hidden_one = h1[b] + sum1.total(b)
        h1[b] = hidden_one
        normed, _ = normalize(hidden_one)
        spread_c.put(b, (normed * vec[2:3, :feats] + vec[3:4, :feats]).astype(BF))

    def norm3(b):
        grad_c = sum3.total(b)
        normed, inverse = normalize(h1[b])
        grad_out = gh1[b]
        grad_h = grad_out + normalize_back(grad_c, normed, inverse, vec[2:3, :feats])
        gh1[b] = grad_h
        spread_low.put(b, grad_h.astype(BF))
        vpart[2:3, :feats] += column_sum(grad_c * normed)
        vpart[3:4, :feats] += column_sum(grad_c)
        vpart[4:5, :feats] += column_sum(grad_h)
        vpart[5:6, :feats] += column_sum(grad_out)

    def norm4(b):
        grad_a = sum4.total(b)
        copy_own(b).wait()
        normed, inverse = normalize(cot_buf[own_spot(b), :].astype(F32))
        spread_in.put(b, (gh1[b] + normalize_back(grad_a, normed, inverse, vec[0:1, :feats])).astype(BF))
        vpart[0:1, :feats] += column_sum(grad_a * normed)
        vpart[1:2, :feats] += column_sum(grad_a)

    def layer_block(b):
        ids = lax.broadcasted_iota(jnp.int32, (quarter, 1), 0) + (b * 4 + place.near * 2 + place.far) * quarter
        result = h1[b] + sum2.late_total(b) + vec[5:6, :feats]
        spread_lay.put(b, jnp.where(ids < len_ref[0], result, 0.0).astype(BF))

    forward, middle, backward = 1, 1 + nb, 1 + 2 * nb
    end = 3 * nb
    plan = {}

    def at(step, point, action, *args):
        plan.setdefault((step, point), []).append((action, args))

    for k in range(nb):
        b = last - k
        if k + 1 < nb:
            at(forward + k + 1, "early", sum1.pass_on, b)
            at(middle + k + 1, "early", sum3.pass_on, b)
            at(backward + k + 1, "early", sum4.pass_on, b)
        at(middle + k + 1, "early" if k + 1 < nb else "start", sum2.stage_all, b)
    at(forward + 1, "late", norm1, last)
    at(forward + 2, "late", spread_c.relay, last)
    at(forward + 3, "late", norm1, last - 1)
    at(forward, "late", far_gather.forward, 0)
    at(forward, "late", far_gather.begin_x, 1)
    at(forward + 1, "late", far_gather.begin, 2)
    at(forward + 2, "late", far_gather.forward, 1)
    at(forward + 2, "late", far_gather.begin, 3)
    at(forward + 3, "late", far_gather.begin, 4)
    at(forward + 3, "early", copy_cot(last).start)
    at(middle, "start", sum1.pass_on, 0)
    at(middle, "start", norm1, last - 2)
    at(middle, "start", far_gather.forward, 2)
    at(middle, "start", spread_c.relay, last - 1)
    at(middle, "start", norm1, last - 3)
    at(middle, "start", far_gather.forward, 3)
    at(middle, "start", spread_c.relay, last - 2)
    at(middle, "start", far_gather.forward, 4)
    for piece in range(len(far_cuts)):
        at(middle, "start", far_gather.finish, piece)
    at(middle, "mid", spread_c.relay, last - 3)
    at(middle + 1, "late", norm3, last)
    at(middle + 2, "mid", spread_low.relay, last)
    at(middle + 2, "late", norm3, last - 1)
    at(middle + 3, "mid", spread_low.relay, last - 1)
    at(middle + 3, "late", norm3, last - 2)
    at(backward, "early", sum3.pass_on, 0)
    for k in range(nb):
        at(backward, "early", sum2.to_far(last - k).start)
    at(backward, "mid", norm3, last - 3)
    at(backward, "mid", spread_low.relay, last - 2)
    at(backward, "mid", far_parts[0].pass_on)
    at(backward, "mid", far_parts[2].begin)
    at(backward, "late", spread_low.relay, last - 3)
    at(backward, "late", far_parts[1].pass_on)
    at(backward, "late", far_parts[3].begin)
    at(backward + 1, "mid", far_parts[2].pass_on)
    at(backward + 1, "late", far_parts[3].pass_on)
    at(backward + 1, "late", layer_block, last)
    at(backward + 2, "mid", norm4, last)
    at(backward + 2, "mid", layer_block, last - 1)
    at(backward + 2, "late", layer_block, last - 2)
    at(backward + 3, "mid", norm4, last - 1)
    at(backward + 3, "mid", layer_block, last - 3)

    def run(phase, point):
        for step in range(phase, phase + nb):
            actions = plan.get((step, point), ())
            if actions:
                @pl.when(s == step)
                def _(actions=actions):
                    for action, args in actions:
                        action(*args)

    @pl.when(s == 0)
    def _():
        copy_tokens().start()
        greet(n_dp, n_tensor)
        if small:
            vec_gather.begin(vec_shard[...])
        near_gather.begin(0)
        near_gather.begin(1)
        vpart[...] = jnp.zeros_like(vpart)
        copy_tokens().wait()
        vec[...] = vec_gather.total() if small else vec_shard[...].astype(F32)

        def norm(b):
            span = block_rows(b)
            normed, _ = normalize(low[span, :].astype(F32))
            ac[span, :] = (normed * vec[0:1, :feats] + vec[1:2, :feats]).astype(BF)
            copy_a(b).start()
            h1[b] = low[own_rows(b), :].astype(F32) + vec[4:5, :feats]

        over(norm, 0, nb)
        scale = 1.0 / d**0.5

        def project(kind):
            near_gather.finish(kind)
            cols = slice(kind * width, (kind + 1) * width)

            def step(b):
                span = block_rows(b)
                out = dot(ac[span, :], wj[:, cols])
                if kind == 0:
                    out = (out + vec[6:7, 0:width]) * scale
                if kind == 2:
                    out = out + vec[6:7, width:2 * width]
                qkv[span, cols] = out.astype(BF)

            over(step, 0, nb)

        near_gather.forward(0)
        near_gather.begin(2)
        near_gather.forward(1)
        near_gather.begin(3)
        project(0)
        near_gather.forward(2)
        far_gather.begin_z(0)
        project(1)
        near_gather.forward(3)
        far_gather.begin_z(1)
        project(2)
        far_gather.begin_x(0)

        def fill(b):
            first = pl.multiple_of(b * bq, bq)
            fill_keys(qkv, ka, heads, d, slope_fn(heads, total_heads), first, bq)
            gu_buf[turned_spot(b)] = qkv[pl.ds(first, bq), 2 * width:3 * width].T

        over(fill, 0, nb)
        near_gather.finish(3)
        over(lambda b: copy_a(b).wait(), 0, nb)

    @pl.when((s >= forward) & (s < middle))
    def _():
        i = middle - 1 - s
        qt = qkv[block_rows(i), 0:width].T
        ones = stack_rows((128 - d, bq), (1.0, 1.0, 1.0))
        queries = [jnp.concatenate([qt[h * d:(h + 1) * d], ones], axis=0) for h in range(heads)]
        run(forward, "early")

        def block(j, carry, diagonal):
            out = []
            kr = block_rows(j)
            for h in range(heads):
                m, l, total = carry[h]
                scores = dot(ka[h, kr, :], queries[h])
                if diagonal:
                    scores = causal(scores, bq, bq)
                top = jnp.maximum(m, jnp.max(scores, axis=0, keepdims=True))
                p = jnp.exp(scores - top)
                scale = jnp.exp(m - top)
                l = l * scale + jnp.sum(p, axis=0, keepdims=True)
                total = total * scale + dot(gu_buf[turned_spot(j, h * d, d)], p.astype(BF))
                out.append((top, l, total))
            return tuple(out)

        start = (jnp.full((1, bq), LOW, F32), jnp.zeros((1, bq), F32), jnp.zeros((d, bq), F32))
        carry = lax.fori_loop(0, i, lambda j, c: block(j, c, False), (start,) * heads)
        carry = block(i, carry, True)
        for h in range(heads):
            m, l, total = carry[h]
            ot[i, h * d:(h + 1) * d, :] = total / l
            lse[i, h:h + 1, :] = m + jnp.log(l)
        out_nat = ot[i].astype(BF).T
        for half_cols in halves:
            part[sum1.slot(i), :, half_cols] = dot(out_nat, wo[half_cols, :], NT).astype(BF)
        sum1.begin(i)
        run(forward, "late")

    @pl.when((s >= middle) & (s < backward))
    def _():
        i = backward - 1 - s
        run(middle, "start")

        @pl.when(s == middle)
        def _():
            acc[...] = jnp.zeros_like(acc)

        spread_c.finish(i)
        copy_cot(i).wait()
        row_ids = lax.broadcasted_iota(jnp.int32, (bq, 128), 0) + i * bq
        live = jnp.where(row_ids < len_ref[0], 1.0, 0.0).astype(BF)
        cot_buf[...] = cot_buf[...] * jnp.concatenate([live] * (feats // 128), axis=1)
        gh1[i] = cot_buf[sum1.rows(place.near, place.far), :].astype(F32)
        run(middle, "early")
        root = math.sqrt(2.0 / math.pi)
        step = 256
        for first in range(0, hidden, step):
            cols = slice(first, first + step)
            u = dot(ac[block_rows(i), :], big[:, cols]) + vec[6:7, 2 * width + first:2 * width + first + step]
            square = u * u
            bent = jnp.tanh(root * (u + 0.044715 * (square * u)))
            half = 0.5 * (1.0 + bent)
            hid_buf[:, cols] = (u * half).astype(BF)
            slope = half + 0.5 * u * (1.0 - bent * bent) * (root * (1.0 + 3 * 0.044715 * square))
            grad_u = (dot(cot_buf[...], big[:, hidden + first:hidden + first + step]) * slope).astype(BF)
            gu_buf[:, cols] = grad_u
            vpart[6:7, 2 * width + first:2 * width + first + step] += column_sum(grad_u.astype(F32))
        for half_cols in halves:
            part[sum3.slot(i), :, half_cols] = dot(gu_buf[...], big[half_cols, :hidden], NT).astype(BF)
        sum3.begin(i)
        run(middle, "mid")
        for half_cols in halves:
            part2[sum2.slot(i), :, half_cols] = dot(hid_buf[...], big[half_cols, hidden:], NT).astype(BF)
        sum2.begin(i)
        for r in range(2):
            cols = slice(r * bq, (r + 1) * bq)
            for half_cols in halves:
                acc[r, :, half_cols] += dot(ac[block_rows(i), cols], gu_buf[:, half_cols], TN)
                acc[2 + r, :, half_cols] += dot(cot_buf[:, cols], hid_buf[:, half_cols], TN)

        @pl.when(i > 0)
        def _():
            copy_cot(i - 1).start()

        run(middle, "late")

        @pl.when(s == backward - 1)
        def _():
            for r in range(2):
                span = slice(r * bq, (r + 1) * bq)
                big[span, :hidden] = acc[r].astype(BF)
                big[span, hidden:] = acc[2 + r].astype(BF)
            far_parts[0].begin()
            far_parts[1].begin()
            copy_back().start()
            over(lambda b: copy_own(b).start(), 0, nb)

    @pl.when(s >= backward)
    def _():
        i = end - s
        lanes = lax.broadcasted_iota(jnp.int32, (bq, 128), 1)
        run(backward, "start")

        @pl.when(s == backward)
        def _():
            acc[...] = jnp.zeros_like(acc)

            def fill(b):
                span = block_rows(b)
                gu_buf[turned_spot(b)] = (qkv[span, width:2 * width].astype(F32) * (1.0 / d**0.5)).astype(BF).T
                for h in range(heads):
                    tile = head_tile(qkv, span, 2 * width, h, d)
                    part2[value_spot(h, b)] = jnp.where(lanes < d, tile, jnp.where(lanes < d + 3, 1.0, 0.0)).astype(BF)

            over(fill, 0, nb)

        spread_low.finish(i)
        grad_o = dot(low[block_rows(i), :], wo[...]).astype(BF)
        grad_t = grad_o.T
        q_nat = qkv[block_rows(i), 0:width]
        qt = q_nat.T
        queries, grads, q_pair, g_pair = [], [], [], []
        for h in range(heads):
            hs = slice(h * d, (h + 1) * d)
            delta = jnp.sum(grad_t[hs].astype(F32) * ot[i, hs, :], axis=0, keepdims=True)
            queries.append(jnp.concatenate(
                [qt[hs], stack_rows((128 - d, bq), (1.0, 1.0, 1.0) + three(-lse[i, h:h + 1, :]))], axis=0))
            grads.append(jnp.concatenate([grad_t[hs], stack_rows((128 - d, bq), three(-delta))], axis=0))
            pair = slice((h // 2) * 128, (h // 2) * 128 + 128)
            mine = (lanes < d) if h % 2 == 0 else (lanes >= d)
            q_pair.append(jnp.where(mine, q_nat[:, pair].astype(F32), 0.0).astype(BF))
            g_pair.append(jnp.where(mine, grad_o[:, pair].astype(F32), 0.0).astype(BF))
        run(backward, "early")

        def block(j, carry, diagonal):
            out = []
            kr = block_rows(j)
            for h in range(heads):
                scores = dot(ka[h, kr, :], queries[h])
                if diagonal:
                    scores = causal(scores, bq, bq)
                p = jnp.exp(scores)
                gs = (p * dot(part2[value_spot(h, j)], grads[h])).astype(BF)
                at_k = slice((h // 2) * 128, (h // 2) * 128 + 128)
                at_v = slice(width + (h // 2) * 128, width + (h // 2) * 128 + 128)
                acc[j, :, at_v] += dot(p.astype(BF), g_pair[h])
                acc[j, :, at_k] += dot(gs, q_pair[h])
                out.append(carry[h] + dot(gu_buf[turned_spot(j, h * d, d)], gs))
            return tuple(out)

        carry = lax.fori_loop(0, i, lambda j, c: block(j, c, False), (jnp.zeros((d, bq), F32),) * heads)
        run(backward, "mid")
        carry = block(i, carry, True)
        hid_buf[:, 0:width] = jnp.concatenate(carry, axis=0).T.astype(BF)
        hid_buf[:, width:3 * width] = acc[i, :, 0:2 * width].astype(BF)
        gqkv = hid_buf[:, 0:3 * width]
        for half_cols in halves:
            part[sum4.slot(i), :, half_cols] = dot(gqkv, wj[half_cols, :], NT).astype(BF)
        sum4.begin(i)
        sums = column_sum(gqkv.astype(F32))
        vpart[6:7, 0:width] += sums[:, 0:width]
        vpart[6:7, width:2 * width] += sums[:, 2 * width:]

        @pl.when(s == backward)
        def _():
            copy_back().wait()

        out_nat = ot[i].astype(BF).T
        for r in range(2):
            cols = slice(r * bq, (r + 1) * bq)
            left = ac[block_rows(i), cols]
            acc[2 * r, :, 2 * width:] += dot(left, hid_buf[:, 0:2 * width], TN)
            acc[2 * r + 1, :, 2 * width:3 * width] += dot(left, hid_buf[:, 2 * width:3 * width], TN)
            acc[2 * r + 1, :, 3 * width:] += dot(low[block_rows(i), cols], out_nat, TN)
        run(backward, "late")

    @pl.when(s == end)
    def _():
        sum4.pass_on(0)
        for r in range(2):
            for c in range(2):
                grads_near[r * bq:(r + 1) * bq, c * 2 * width:(c + 1) * 2 * width] = acc[2 * r + c, :, 2 * width:].astype(BF)
        near_parts[0].begin()
        near_parts[1].begin()
        norm4(last - 2)
        near_parts[0].pass_on()
        near_parts[2].begin()
        over(spread_lay.relay, 0, nb)
        norm4(last - 3)
        if small:
            vec_sum.begin(vpart[...])
        near_parts[1].pass_on()
        near_parts[3].begin()
        for part_far in far_parts:
            part_far.finish()
        near_parts[2].pass_on()
        for b in range(last, 0, -1):
            spread_in.relay(b)
        square = jnp.sum(total_ref[:, feats:] * total_ref[:, feats:])
        if small:
            vec_tensor.begin(vec_sum.total())
            near_parts[3].pass_on()
            shared_total = vec_tensor.total()
            row_ids = lax.broadcasted_iota(jnp.int32, vec_out.shape, 0)
            vec_total = jnp.where(row_ids < 6, shared_total, s_buf[rank])
            vec_out[...] = vec_total
            first_row = jnp.where(me == 0, jnp.where(rank == 0, 0, 6), 8)
            vec_kept = jnp.where(row_ids >= first_row, vec_total, 0.0)
            square = square + jnp.sum(vec_kept * vec_kept)
        else:
            near_parts[3].pass_on()
            vec_out[...] = vpart[...]
        for part_near in near_parts:
            part_near.finish()
        square = square + jnp.sum(total_ref[:, :feats] * total_ref[:, :feats])
        square_sum.begin(jnp.full(q_buf.shape[1:], square, F32))
        spread_in.relay(0)
        square_tensor.begin(square_sum.total())
        square_out[...] = square_tensor.total()
        over(spread_lay.finish, 0, nb)
        over(spread_in.finish, 0, nb)


def layer(lengths, tokens, cot, near_shard, far_shard, vec_shard, heads, d, total_heads, bq, n_dp, n_tensor, collective_id):
    n, feats = tokens.shape
    rows = near_shard.shape[0]
    width = heads * d
    hidden = far_shard.shape[1] // 2
    nb, quarter, lines = n // bq, bq // 4, n_dp // 2
    wide = vec_shard.shape[1]
    near_cuts = [(0, k * width, k * width, width) for k in range(3)] + [(1, 3 * width, 0, width)]
    step = hidden // 2
    far_cuts = [(0, step), (step, step), (2 * step, step), (3 * step, step // 2), (3 * step + step // 2, step // 2)]
    sum_far = [(k * step, step) for k in range(4)]
    sum_near = [(k * width, width) for k in range(4)]
    dims = (heads, d, total_heads, bq, nb, n_dp, n_tensor, near_cuts, far_cuts, (sum_far, sum_near))
    vm, dma = pltpu.VMEM, pltpu.SemaphoreType.DMA
    own = (nb, quarter, feats)
    sums = [vm((nb, 2 * quarter, feats), BF), vm(own, BF), vm(own, BF)]
    tile = (8, 128)
    scratch = [
        vm((n, 3 * width), BF), vm((heads, n, 128), BF),
        vm((feats, 2 * hidden), BF), vm((feats, 3 * width), BF), vm((feats, width), BF), vm((n, feats), BF),
        vm((n, feats), BF), vm((nb, width, bq), F32), vm((nb, heads, bq), F32), vm(own, F32), vm(own, F32),
        vm((4, bq, hidden), F32), vm((bq, hidden), BF), vm((bq, hidden), BF), vm((bq, feats), BF),
        vm((3, bq, feats), BF), *sums, vm((2, bq, feats), BF), *sums,
        vm((4, lines, rows, step), BF), vm((4, lines, rows, step), BF),
        vm((4, lines, rows, width), BF), vm((4, lines, rows, width), BF),
        vm((n_dp if n_dp <= 8 else 1,) + vec_shard.shape, BF), vm(vec_shard.shape, F32), vm((8, wide), F32),
        vm((n_dp if n_dp <= 8 else 1, 8, wide), F32), vm((n_tensor, 8, wide), F32), vm((n_dp,) + tile, F32), vm((n_tensor,) + tile, F32),
        dma((4, len(near_cuts), lines)), dma((4, len(far_cuts), lines)), dma((4, 4, nb)), dma((4, 7, nb)),
        dma((4, 4, lines)), dma((4, 4, lines)), dma((1 + nb,)), dma((n_dp,)), dma((n_dp,)), dma((n_dp,)), dma((n_dp,)),
        dma((n_dp,)), dma((n_dp,)), dma((n_tensor,)), dma((n_tensor,)), dma((n_tensor,)), dma((n_tensor,)),
    ]
    shape = jax.ShapeDtypeStruct
    return pl.pallas_call(
        functools.partial(layer_kernel, dims),
        grid=(1 + 3 * nb,),
        in_specs=[pl.BlockSpec(memory_space=pltpu.SMEM)] + [ANYWHERE] * 4 + [whole(vec_shard)],
        out_specs=[fixed((rows, feats + 2 * hidden)), fixed((8, wide)), fixed(tile), ANYWHERE, ANYWHERE, ANYWHERE],
        out_shape=[shape((rows, feats + 2 * hidden), F32), shape((8, wide), F32), shape(tile, F32),
                   shape((n, feats), BF), shape((n, feats), BF), shape((n, feats), BF)],
        scratch_shapes=scratch,
        compiler_params=params(collective_id, 63),
        name="layer",
    )(lengths, tokens, cot, near_shard, far_shard, vec_shard)


def adam_step(master, moment, variance, gradient, rate, decay):
    moment_new = BETA_FIRST * moment + (1.0 - BETA_FIRST) * gradient
    variance_new = BETA_SECOND * variance + (1.0 - BETA_SECOND) * gradient * gradient
    moment_hat = moment_new / (1.0 - BETA_FIRST**STEP)
    variance_hat = variance_new / (1.0 - BETA_SECOND**STEP)
    master_new = master - rate * (
        moment_hat / (jnp.sqrt(variance_hat) + ADAM_EPSILON) + decay * master
    )
    return (master_new, moment_new, variance_new)


def update_kernel(head_size, square_ref, joint_sum, output_sum, widen_sum, narrow_sum, shared_sum, split_sum, *refs):
    ins, outs = refs[:18], refs[18:]
    norm = jnp.sqrt(square_ref[0:1, 0:1])
    factor = jnp.minimum(1.0, CLIP_LIMIT / (norm + 1e-06))

    def step(at, gradient, rate, decay, cols=slice(None)):
        new = adam_step(*[ref[:, cols] for ref in ins[3 * at:3 * at + 3]], factor * gradient, rate, decay)
        for ref, value in zip(outs[3 * at:3 * at + 3], new):
            ref[:, cols] = value

    joint = ins[0].shape[1]
    heads = joint // (3 * head_size)

    def source(piece):
        head, kind = piece // 3, piece % 3
        first = (kind * heads + head) * head_size
        return joint_sum[:, first:first + head_size]

    for piece in range(0, joint // head_size, 2):
        cols = slice(piece * head_size, (piece + 2) * head_size)
        step(0, jnp.concatenate([source(piece), source(piece + 1)], axis=1), MATRIX_RATE, MATRIX_DECAY, cols)
    step(1, output_sum[...].T, OUTPUT_RATE, MATRIX_DECAY)
    step(2, widen_sum[...], MATRIX_RATE, MATRIX_DECAY)
    step(3, narrow_sum[...].T, MATRIX_RATE, MATRIX_DECAY)

    @pl.when(pl.program_id(0) == 0)
    def _():
        step(4, shared_sum[...], VECTOR_RATE, 0.0)
        step(5, split_sum[...], VECTOR_RATE, 0.0)


def update(square, sums, shared, split, states, head_size):
    count = 2
    joint, output, widen, narrow = [states[3 * k].shape for k in range(4)]
    rows = joint[0]

    def halves(shape):
        return pl.BlockSpec((shape[0] // count, shape[1]), lambda i: (i, 0))

    def all_of(shape):
        return pl.BlockSpec(shape, lambda i: (0, 0))

    def columns(first, cols):
        wide = cols // count
        return pl.BlockSpec((rows, wide), lambda i: (0, first // wide + i))

    states_specs = [halves(state.shape) for state in states[:12]] + [all_of(state.shape) for state in states[12:]]
    widen_at, narrow_at = joint[1] + output[0], joint[1] + output[0] + widen[1]
    return pl.pallas_call(
        functools.partial(update_kernel, head_size),
        grid=(count,),
        in_specs=[all_of(square.shape), halves(joint), columns(joint[1], output[0]),
                  pl.BlockSpec((rows // count, widen[1]), lambda i: (i, widen_at // widen[1])),
                  columns(narrow_at, narrow[0]), all_of(shared.shape), all_of(split.shape)] + states_specs,
        out_specs=states_specs,
        out_shape=[jax.ShapeDtypeStruct(state.shape, F32) for state in states],
        compiler_params=pltpu.CompilerParams(vmem_limit_bytes=48 * 2**20),
        name="update",
    )(square, sums, sums, sums, sums, shared, split, *states)


def on_device(
    tokens,
    cotangent,
    lengths,
    joint_weight,
    output_weight,
    widen_weight,
    narrow_weight,
    shared_vectors,
    split_vectors,
    joint_first,
    joint_second,
    output_first,
    output_second,
    widen_first,
    widen_second,
    narrow_first,
    narrow_second,
    shared_first,
    shared_second,
    split_first,
    split_second,
):
    n_dp, n_tensor = lax.axis_size("dp"), lax.axis_size("tensor")
    me = lax.axis_index("dp")
    head_cols = output_weight.shape[0]
    near_shard = jnp.concatenate([by_kind(joint_weight), output_weight.T], axis=1).astype(BF)
    far_shard = jnp.concatenate([widen_weight, narrow_weight.T], axis=1).astype(BF)
    shared_cols, split_cols = shared_vectors.shape[1], split_vectors.shape[1]
    vec_cols = n_dp * max(shared_cols, split_cols)

    def placed(values, cols):
        here = lax.broadcasted_iota(jnp.int32, (1, n_dp * cols), 1) // cols == me
        wide = jnp.where(here, jnp.tile(values, (1, n_dp)), 0.0)
        return jnp.pad(wide, ((0, 0), (0, vec_cols - n_dp * cols)))

    vec_shard = jnp.pad(
        jnp.concatenate([placed(shared_vectors, shared_cols), placed(split_vectors, split_cols)], axis=0),
        ((0, 9), (0, 0)),
    ).astype(BF)
    if n_dp > 8:
        vec_shard = lax.psum(vec_shard, "dp")
    head_size = D // HEADS
    local_heads = head_cols // head_size
    total_rows = tokens.shape[0]
    block = min(512, total_rows)
    sums, vec_sum, square, input_grad, layer_output, _ = layer(
        lengths, tokens, cotangent, near_shard, far_shard, vec_shard, local_heads, head_size, HEADS, block, n_dp,
        n_tensor, 0,
    )
    if n_dp > 8:
        split_all = lax.psum(vec_sum[6:], "dp")
        shared_all = lax.psum(vec_sum[:6], ("dp", "tensor"))
        vec_sum = jnp.concatenate([shared_all, split_all], axis=0)
        square = square + jnp.sum(shared_all * shared_all) + lax.psum(jnp.sum(split_all * split_all), "tensor")
    shared_sum = lax.dynamic_slice(vec_sum, (0, me * shared_cols), (6, shared_cols))
    split_sum = lax.dynamic_slice(vec_sum, (6, me * split_cols), (1, split_cols))
    states = (
        joint_weight, joint_first, joint_second, output_weight, output_first, output_second,
        widen_weight, widen_first, widen_second, narrow_weight, narrow_first, narrow_second,
        shared_vectors, shared_first, shared_second, split_vectors, split_first, split_second,
    )
    updated = update(square, sums, shared_sum, split_sum, states, head_size)
    return (layer_output, input_grad, jnp.sqrt(square[0, 0]), *updated)


def solution(mesh):
    in_specs = (
        P("dp", None),
        P("dp", None),
        P("dp"),
        P("dp", "tensor"),
        P("tensor", "dp"),
        P("dp", "tensor"),
        P("tensor", "dp"),
        P(None, "dp"),
        P("tensor", "dp"),
        P("dp", "tensor"),
        P("dp", "tensor"),
        P("tensor", "dp"),
        P("tensor", "dp"),
        P("dp", "tensor"),
        P("dp", "tensor"),
        P("tensor", "dp"),
        P("tensor", "dp"),
        P(None, "dp"),
        P(None, "dp"),
        P("tensor", "dp"),
        P("tensor", "dp"),
    )
    out_specs = (
        P("dp", None),
        P("dp", None),
        P(),
        P("dp", "tensor"),
        P("dp", "tensor"),
        P("dp", "tensor"),
        P("tensor", "dp"),
        P("tensor", "dp"),
        P("tensor", "dp"),
        P("dp", "tensor"),
        P("dp", "tensor"),
        P("dp", "tensor"),
        P("tensor", "dp"),
        P("tensor", "dp"),
        P("tensor", "dp"),
        P(None, "dp"),
        P(None, "dp"),
        P(None, "dp"),
        P("tensor", "dp"),
        P("tensor", "dp"),
        P("tensor", "dp"),
    )
    return jax.shard_map(
        on_device, mesh=mesh, in_specs=in_specs, out_specs=out_specs, check_vma=False
    )
```

```python
import functools
import math

import jax
import jax.numpy as jnp
from jax import lax
from jax.experimental import pallas as pl
from jax.experimental.pallas import tpu as pltpu
from jax.sharding import PartitionSpec as P

F32, BF = jnp.float32, jnp.bfloat16

D = 1024
HEADS = 16
STEP = 10


NORM_EPSILON = 1e-05
CLIP_LIMIT = 1.0
BETA_FIRST = 0.9
BETA_SECOND = 0.95
ADAM_EPSILON = 1e-08
MATRIX_RATE = 0.05
OUTPUT_RATE = 0.2
VECTOR_RATE = 0.6
MATRIX_DECAY = 0.1


def by_kind(values):
    rows, cols = values.shape
    size = D // HEADS
    return jnp.swapaxes(values.reshape(rows, cols // (3 * size), 3, size), 1, 2).reshape(rows, cols)


NN = (((1,), (0,)), ((), ()))
NT = (((1,), (1,)), ((), ()))
TN = (((0,), (0,)), ((), ()))
LOW = -1e30


def dot(left, right, dims=NN):
    return lax.dot_general(left, right, dims, preferred_element_type=F32)


def three(values):
    high = values.astype(BF).astype(F32)
    rest = values - high
    middle = rest.astype(BF).astype(F32)
    return high, middle, rest - middle


def stack_rows(shape, rows):
    ids = lax.broadcasted_iota(jnp.int32, shape, 0)
    out = jnp.zeros(shape, F32)
    for at, row in enumerate(rows):
        out = jnp.where(ids == at, row, out)
    return out.astype(BF)


def head_tile(ref, rows, col, head, d):
    lane = col + (head // 2) * 128
    tile = ref[rows, lane:lane + 128].astype(F32)
    if head % 2:
        tile = pltpu.roll(tile, 64, 1)
    return tile


def fill_keys(qkv_ref, ka_ref, heads, d, slope_of, first, count):
    rows = pl.ds(first, count)
    lanes = lax.broadcasted_iota(jnp.int32, (count, 128), 1)
    position = (lax.broadcasted_iota(jnp.int32, (count, 128), 0) + first).astype(F32)
    for head in range(heads):
        high, middle, low = three(position * slope_of(head))
        tile = head_tile(qkv_ref, rows, heads * d, head, d)
        for at, part in enumerate((high, middle, low, 1.0, 1.0, 1.0)):
            tile = jnp.where(lanes == d + at, part, tile)
        ka_ref[head, rows, :] = jnp.where(lanes < d + 6, tile, 0.0).astype(BF)


def causal(scores, bk, bq):
    kid = lax.broadcasted_iota(jnp.int32, (bk, bq), 0)
    qid = lax.broadcasted_iota(jnp.int32, (bk, bq), 1)
    return jnp.where(kid <= qid, scores, LOW)


def slope_fn(heads, total_heads):
    rank = lax.axis_index("tensor")
    def slope_of(head):
        index = jnp.full((1, 128), rank * heads + head + 1, jnp.int32).astype(F32)
        return jnp.exp2(index * (-8.0 / total_heads))
    return slope_of


def at_dp(index):
    return {"dp": index}


def at_tensor(index):
    return {"tensor": index}


def remote(src, dst, send, recv, where):
    return pltpu.make_async_remote_copy(
        src_ref=src, dst_ref=dst, send_sem=send, recv_sem=recv, device_id=where, device_id_type=pl.DeviceIdType.MESH
    )


def greet(n_dp, n_tensor):
    me, rank = lax.axis_index("dp"), lax.axis_index("tensor")
    barrier = pltpu.get_barrier_semaphore()

    def along_dp(k, c):
        pl.semaphore_signal(barrier, inc=1, device_id=at_dp(lax.rem(me + k, n_dp)), device_id_type=pl.DeviceIdType.MESH)
        return c

    lax.fori_loop(1, n_dp, along_dp, 0)
    for k in range(1, n_tensor):
        pl.semaphore_signal(
            barrier, inc=1, device_id=at_tensor(lax.rem(rank + k, n_tensor)), device_id_type=pl.DeviceIdType.MESH
        )
    pl.semaphore_wait(barrier, n_dp + n_tensor - 2)


def over(body, first, last):
    lax.fori_loop(first, last, lambda k, c: (body(k), c)[1], 0)


def greet_tensor(n_tensor):
    rank = lax.axis_index("tensor")
    barrier = pltpu.get_barrier_semaphore()
    for k in range(1, n_tensor):
        pl.semaphore_signal(
            barrier, inc=1, device_id=at_tensor(lax.rem(rank + k, n_tensor)), device_id_type=pl.DeviceIdType.MESH
        )
    pl.semaphore_wait(barrier, n_tensor - 1)


class Gather:
    def __init__(self, lines, rows, pieces, sems):
        me = lax.axis_index("dp")
        self.me, self.z, self.x = me, me // 2, lax.rem(me, 2)
        self.lines, self.rows, self.pieces, self.sems = lines, rows, pieces, sems
        self.other = at_dp(self.z * 2 + 1 - self.x)
        self.relayed = lines == 4

    def crossing(self, s):
        return self.relayed and self.pieces[s][5]

    def own(self, s):
        shard, first, _, cols = self.pieces[s][:4]
        return shard.at[:, pl.ds(first, cols)]

    def spot(self, s, zz, column):
        _, _, first, cols, out = self.pieces[s][:5]
        device = zz * 2 + (self.x if column == 0 else 1 - self.x)
        return out.at[pl.ds(pl.multiple_of(device * self.rows, self.rows), self.rows), pl.ds(first, cols)]

    def sem(self, kind, s, index):
        return self.sems.at[kind, s, index]

    def to_x(self, s, zz, src):
        return remote(src, self.spot(s, zz, 0), self.sem(0, s, zz), self.sem(1, s, zz), self.other)

    def from_x(self, s, zz):
        spot = self.spot(s, zz, 1)
        return remote(spot, spot, self.sem(0, s, zz), self.sem(1, s, zz), self.other)

    def along_z(self, s, column, src, zz, send, target):
        kind = 2 + 2 * column
        return remote(src, self.spot(s, zz, column), send, self.sem(kind + 1, s, zz), at_dp(target * 2 + self.x))

    def to_z(self, s, column, k):
        src = self.own(s) if column == 0 else self.spot(s, self.z, 1)
        return self.along_z(s, column, src, self.z, self.sem(2 + 2 * column, s, k), lax.rem(self.z + k, self.lines))

    def each_to_z(self, s, column, action):
        def step(k):
            if not self.relayed:
                action(self.to_z(s, column, k))
                return
            gap = lax.rem(self.z + k, self.lines) - self.z

            @pl.when((gap != 3) & (gap != -3))
            def _():
                action(self.to_z(s, column, k))

        over(step, 1, self.lines)

    def from_z(self, s, column, zz):
        spot = self.spot(s, zz, column)
        return self.along_z(s, column, spot, zz, self.sem(2 + 2 * column, s, 0), self.z)

    def relay_copy(self, s, column):
        source, target = jnp.where(self.z == 2, 0, 3), jnp.where(self.z == 2, 3, 0)
        return self.along_z(s, column, self.spot(s, source, column), source, self.sem(6 + column, s, 0), target)

    def inner(self):
        return (self.z == 1) | (self.z == 2)

    def relays(self, zz):
        return ((self.z == 2) & (zz == 0)) | ((self.z == 1) & (zz == 3))

    def keep(self, s):
        return pltpu.make_async_copy(self.own(s), self.spot(s, self.z, 0), self.sem(self.sems.shape[0] - 1, s, 0))

    def begin_z(self, s):
        self.each_to_z(s, 0, lambda copy: copy.start())
        self.keep(s).start()

    def begin_x(self, s):
        self.to_x(s, self.z, self.own(s)).start()

    def forward(self, s):
        def step(k):
            zz = lax.rem(self.z + k, self.lines)
            self.from_z(s, 0, zz).wait_recv()
            if self.relayed:
                @pl.when(self.relays(zz))
                def _():
                    self.relay_copy(s, 0).start()
            self.to_x(s, zz, self.spot(s, zz, 0)).start()

        over(step, 1, self.lines)

    def cross(self, s):
        if not self.crossing(s):
            return
        self.from_x(s, self.z).wait_recv()
        self.each_to_z(s, 1, lambda copy: copy.start())

    def relay(self, s, column):
        if not self.crossing(s):
            if column == 0:
                self.forward(s)
            return

        @pl.when(self.inner())
        def _():
            self.from_z(s, column, jnp.where(self.z == 2, 0, 3)).wait_recv()
            self.relay_copy(s, column).start()

    def finish(self, s):
        self.keep(s).wait()
        columns = range(2 if self.crossing(s) else 1)
        for column in columns:
            self.each_to_z(s, column, lambda copy: copy.wait_send())
            if self.relayed:
                @pl.when(self.inner())
                def _(column=column):
                    self.relay_copy(s, column).wait_send()
        if self.crossing(s):
            self.to_x(s, self.z, self.own(s)).wait_send()
            for column in columns:
                def arrived(k, column=column):
                    zz = lax.rem(self.z + k, self.lines)

                    @pl.when(jnp.logical_not(self.relays(zz)))
                    def _():
                        self.from_z(s, column, zz).wait_recv()

                over(arrived, 1, self.lines)
        else:
            over(lambda zz: self.to_x(s, zz, self.own(s)).wait_send(), 0, self.lines)
            over(lambda zz: self.from_x(s, zz).wait_recv(), 0, self.lines)


class Place:
    def __init__(self):
        rank = lax.axis_index("tensor")
        self.far, self.near = rank // 2, lax.rem(rank, 2)
        self.near_device = at_tensor(self.far * 2 + 1 - self.near)
        self.far_device = at_tensor((1 - self.far) * 2 + self.near)


class BlockSum:
    def __init__(self, place, quarter, part, slot, near_buf, send_buf, far_buf, sems):
        self.place, self.quarter, self.part, self.slot = place, quarter, part, slot
        self.near_buf, self.send_buf, self.far_buf, self.sems = near_buf, send_buf, far_buf, sems

    def rows(self, near, far):
        first = (near * 2 + far) * self.quarter
        return pl.ds(pl.multiple_of(first, self.quarter), self.quarter)

    def half(self, near):
        first = near * 2 * self.quarter
        return pl.ds(pl.multiple_of(first, self.quarter), 2 * self.quarter)

    def to_near(self, b):
        return remote(self.part.at[self.slot(b), self.half(1 - self.place.near)], self.near_buf.at[b],
                      self.sems.at[0, b], self.sems.at[1, b], self.place.near_device)

    def to_far(self, b):
        return remote(self.send_buf.at[b], self.far_buf.at[b], self.sems.at[2, b], self.sems.at[3, b],
                      self.place.far_device)

    def pair(self, b, far):
        own = self.part[self.slot(b), self.rows(self.place.near, far)].astype(F32)
        return own + self.near_buf[b, self.rows(0, far)].astype(F32)

    def begin(self, b):
        self.to_near(b).start()

    def stage(self, b):
        self.to_near(b).wait_recv()
        self.send_buf[b] = self.pair(b, 1 - self.place.far).astype(BF)

    def pass_on(self, b):
        self.stage(b)
        self.to_far(b).start()

    def total(self, b):
        self.to_far(b).wait()
        self.to_near(b).wait_send()
        return self.pair(b, self.place.far) + self.far_buf[b].astype(F32)

    def stage_all(self, b):
        self.stage(b)
        rows = self.rows(0, self.place.far)
        self.near_buf[b, rows] = self.pair(b, self.place.far).astype(BF)
        self.to_near(b).wait_send()

    def late_total(self, b):
        self.to_far(b).wait()
        return self.near_buf[b, self.rows(0, self.place.far)].astype(F32) + self.far_buf[b].astype(F32)


class BlockSpread:
    def __init__(self, place, quarter, out, sems, own=None):
        self.place, self.quarter, self.out, self.sems, self.own = place, quarter, out, sems, own

    def rows(self, b, near, far):
        first = (b * 4 + near * 2 + far) * self.quarter
        return pl.ds(pl.multiple_of(first, self.quarter), self.quarter)

    def spot(self, b, near, far):
        return self.out.at[self.rows(b, near, far)]

    def mine(self, b):
        return self.spot(b, self.place.near, self.place.far)

    def source(self, b):
        return self.mine(b) if self.own is None else self.own.at[b]

    def put(self, b, values):
        if self.own is None:
            self.out[self.rows(b, self.place.near, self.place.far), :] = values
        else:
            self.own[b] = values
        self.to_far(b).start()
        self.to_near(b).start()
        if self.own is not None:
            self.keep(b).start()

    def to_far(self, b):
        return remote(self.source(b), self.mine(b), self.sems.at[0, b], self.sems.at[1, b], self.place.far_device)

    def to_near(self, b):
        return remote(self.source(b), self.mine(b), self.sems.at[2, b], self.sems.at[3, b], self.place.near_device)

    def arrival(self, near, far, b, at):
        spot = self.spot(b, near, far)
        return remote(spot, spot, self.sems.at[at - 1, b], self.sems.at[at, b], self.place.near_device)

    def pass_far(self, b):
        spot = self.spot(b, self.place.near, 1 - self.place.far)
        return remote(spot, spot, self.sems.at[4, b], self.sems.at[5, b], self.place.near_device)

    def keep(self, b):
        return pltpu.make_async_copy(self.own.at[b], self.mine(b), self.sems.at[6, b])

    def relay(self, b):
        self.arrival(self.place.near, 1 - self.place.far, b, 1).wait_recv()
        self.pass_far(b).start()

    def finish(self, b):
        self.to_far(b).wait_send()
        self.to_near(b).wait_send()
        self.pass_far(b).wait_send()
        if self.own is not None:
            self.keep(b).wait()
        self.arrival(1 - self.place.near, self.place.far, b, 3).wait_recv()
        self.arrival(1 - self.place.near, 1 - self.place.far, b, 5).wait_recv()


def normalize(values):
    centred = values - jnp.mean(values, axis=-1, keepdims=True)
    inverse = lax.rsqrt(jnp.mean(centred * centred, axis=-1, keepdims=True) + NORM_EPSILON)
    return (centred * inverse, inverse)


def normalize_back(incoming, normed, inverse, gain):
    scaled = incoming * gain
    return inverse * (
        scaled
        - jnp.mean(scaled, axis=-1, keepdims=True)
        - normed * jnp.mean(scaled * normed, axis=-1, keepdims=True)
    )


def column_sum(values):
    return jnp.sum(values, axis=0, keepdims=True)


def params(collective_id, megabytes):
    return pltpu.CompilerParams(
        collective_id=collective_id, has_side_effects=True, vmem_limit_bytes=megabytes * 2**20
    )


ANYWHERE = pl.BlockSpec(memory_space=pl.ANY)


def fixed(shape):
    return pl.BlockSpec(shape, lambda i: (0,) * len(shape), pipeline_mode=pl.Buffered(1))


def whole(array):
    return fixed(array.shape)


class Scatter:
    def __init__(self, lines, rows, source, first, cols, x_buf, z_buf, total, at, sems, part):
        me = lax.axis_index("dp")
        self.z, self.x = me // 2, lax.rem(me, 2)
        self.lines, self.rows, self.source = lines, rows, source
        self.cols, self.total_cols = pl.ds(first, cols), pl.ds(at, cols)
        self.x_buf, self.z_buf, self.total, self.sems, self.part = x_buf, z_buf, total, sems, part

    def dest(self, k):
        return lax.rem(self.z + 1 + k, self.lines)

    def chunk(self, device):
        return (pl.ds(pl.multiple_of(device * self.rows, self.rows), self.rows), self.cols)

    def sem(self, kind, index):
        return self.sems.at[kind, self.part, index]

    def to_x(self, dz):
        return remote(self.source.at[self.chunk(dz * 2 + 1 - self.x)], self.x_buf.at[dz], self.sem(0, dz),
                      self.sem(1, dz), at_dp(self.z * 2 + 1 - self.x))

    def to_z(self, dz):
        return remote(self.x_buf.at[dz], self.z_buf.at[self.z], self.sem(2, dz), self.sem(3, self.z),
                      at_dp(dz * 2 + self.x))

    def from_z(self, zz):
        return remote(self.z_buf.at[zz], self.z_buf.at[zz], self.sem(2, zz), self.sem(3, zz), at_dp(zz * 2 + self.x))

    def begin(self):
        over(lambda k: self.to_x(self.dest(k)).start(), 0, self.lines)

    def summed(self, dz):
        self.to_x(dz).wait()
        return self.x_buf[dz].astype(F32) + self.source[self.chunk(dz * 2 + self.x)].astype(F32)

    def pass_on(self):
        def step(k):
            dz = self.dest(k)
            self.x_buf[dz] = self.summed(dz).astype(BF)
            self.to_z(dz).start()

        over(step, 0, self.lines - 1)
        self.total[:, self.total_cols] = self.summed(self.z)

    def finish(self):
        def add(k):
            zz = lax.rem(self.z + k, self.lines)
            self.from_z(zz).wait_recv()
            self.total[:, self.total_cols] += self.z_buf[zz].astype(F32)
            self.to_z(zz).wait_send()

        over(add, 1, self.lines)


class Exchange:
    def __init__(self, buf, index, count, where, send, recv, pieces=None):
        self.buf, self.index, self.count, self.where = buf, index, count, where
        self.send, self.recv, self.pieces = send, recv, pieces

    def to(self, k):
        other = lax.rem(self.index + k, self.count)
        source = self.buf.at[self.index] if self.pieces is None else self.pieces.at[other]
        return remote(source, self.buf.at[self.index], self.send.at[k], self.recv.at[self.index], self.where(other))

    def begin(self, values):
        self.buf[self.index] = values
        over(lambda k: self.to(k).start(), 1, self.count)

    def finish(self):
        def arrived(k):
            other = lax.rem(self.index + k, self.count)
            remote(self.buf.at[other], self.buf.at[other], self.send.at[0], self.recv.at[other],
                   self.where(other)).wait_recv()
            self.to(k).wait_send()

        over(arrived, 1, self.count)

    def total(self):
        self.finish()
        zero = jnp.zeros(self.buf.shape[1:], F32)
        return lax.fori_loop(0, self.count, lambda k, acc: acc + self.buf[k], zero)


def layer_kernel(dims, len_ref, tok_ref, cot_ref, near_shard, far_shard, vec_shard,
                 total_ref, vec_out, square_out, in_out, lay_out, a_hbm, *scratch):
    heads, d, total_heads, bq, nb, n_dp, n_tensor, near_cuts, far_cuts, sum_cuts, vec_cols = dims
    (qkv, ka, big, wj, wo, ac, low, ot, lse, h1, gh1, acc, hid_buf, gu_buf, cot_buf,
     part, near_buf, send_buf, far_buf, part2, near2_buf, send2_buf, far2_buf, x_far, z_far, x_near, z_near,
     vec_buf, vec, vpart, v_send, v_buf, s_buf, q_buf, t_buf,
     gn_sems, gf_sems, sum_sems, spread_sems, sf_sems, sn_sems, copy_sems, vs, vr, vs2, vr2, qs, qr, ss, sr, ts, tr) = scratch
    s = pl.program_id(0)
    place = Place()
    me, rank = lax.axis_index("dp"), lax.axis_index("tensor")
    width, feats, hidden = heads * d, ac.shape[1], big.shape[1] // 2
    quarter, lines, rows = bq // 4, n_dp // 2, total_ref.shape[0]
    last = nb - 1
    halves = (slice(0, feats // 2), slice(feats // 2, feats))
    small = n_dp <= 8

    def slot_from(base):
        return lambda b: lax.rem(base + last - b, 3)

    sum1, sum3, sum4 = (
        BlockSum(place, quarter, part, slot_from(k * nb), near_buf, send_buf, far_buf, sum_sems.at[k]) for k in range(3)
    )
    sum2 = BlockSum(place, quarter, part2, lambda b: lax.rem(last - b, 2), near2_buf, send2_buf, far2_buf, sum_sems.at[3])
    spread_c = BlockSpread(place, quarter, ac, spread_sems.at[0])
    spread_low = BlockSpread(place, quarter, low, spread_sems.at[1])
    spread_lay = BlockSpread(place, quarter, lay_out, spread_sems.at[2], send2_buf)
    spread_in = BlockSpread(place, quarter, in_out, spread_sems.at[3], send_buf)
    near_gather = Gather(lines, rows, [
        (near_shard, first, at, cols, (wj, wo)[index], index == 1) for index, first, at, cols in near_cuts],
                         gn_sems)
    far_gather = Gather(lines, rows, [
        (far_shard, first, first, cols, big, p == len(far_cuts) - 1) for p, (first, cols) in enumerate(far_cuts)], gf_sems)
    grads_near = part2.reshape(2 * bq, feats)
    far_parts = [
        Scatter(lines, rows, big, first, cols, x_far.at[p], z_far.at[p], total_ref, feats + first, sf_sems, p)
        for p, (first, cols) in enumerate(sum_cuts[0])
    ]
    near_parts = [
        Scatter(lines, rows, grads_near, first, cols, x_near.at[p], z_near.at[p], total_ref, first, sn_sems, p)
        for p, (first, cols) in enumerate(sum_cuts[1])
    ]
    vec_gather = Exchange(vec_buf, me, n_dp, at_dp, vs, vr)
    vec_sum = Exchange(v_buf, me, n_dp, at_dp, vs2, vr2, v_send)
    shared_cols, split_cols = vec_cols
    vec_tensor = Exchange(s_buf, rank, n_tensor, at_tensor, ss, sr)
    square_sum = Exchange(q_buf, me, n_dp, at_dp, qs, qr)
    square_tensor = Exchange(t_buf, rank, n_tensor, at_tensor, ts, tr)

    def block_rows(b):
        return pl.ds(pl.multiple_of(b * bq, bq), bq)

    def turned_spot(b, first=0, count=None):
        row = pl.multiple_of(lax.rem(b, 2) * width + first, d)
        return (pl.ds(row, width if count is None else count), pl.ds(pl.multiple_of(b // 2 * bq, bq), bq))

    def value_spot(h, b):
        lane = pl.multiple_of(((h % 2) * nb + b) * 128, 128)
        return (h // 2, slice(None), pl.ds(lane, 128))

    def own_rows(b):
        return spread_c.rows(b, place.near, place.far)

    def copy_tokens():
        return pltpu.make_async_copy(tok_ref, low, copy_sems.at[0])

    def copy_a(b):
        return pltpu.make_async_copy(ac.at[block_rows(b)], a_hbm.at[block_rows(b)], copy_sems.at[1 + b])

    def copy_back():
        return pltpu.make_async_copy(a_hbm, ac, copy_sems.at[0])

    def copy_cot(b):
        return pltpu.make_async_copy(cot_ref.at[block_rows(b)], cot_buf, copy_sems.at[0])

    def own_spot(b):
        return pl.ds(pl.multiple_of(b * quarter, quarter), quarter)

    def copy_own(b):
        return pltpu.make_async_copy(tok_ref.at[own_rows(b)], cot_buf.at[own_spot(b)], copy_sems.at[1 + b])

    def norm1(b):
        hidden_one = h1[b] + sum1.total(b)
        h1[b] = hidden_one
        normed, _ = normalize(hidden_one)
        spread_c.put(b, (normed * vec[2:3, :feats] + vec[3:4, :feats]).astype(BF))

    def norm3(b):
        grad_c = sum3.total(b)
        normed, inverse = normalize(h1[b])
        grad_out = gh1[b]
        grad_h = grad_out + normalize_back(grad_c, normed, inverse, vec[2:3, :feats])
        gh1[b] = grad_h
        spread_low.put(b, grad_h.astype(BF))
        vpart[2:3, :feats] += column_sum(grad_c * normed)
        vpart[3:4, :feats] += column_sum(grad_c)
        vpart[4:5, :feats] += column_sum(grad_h)
        vpart[5:6, :feats] += column_sum(grad_out)

    def norm4(b):
        grad_a = sum4.total(b)
        copy_own(b).wait()
        normed, inverse = normalize(cot_buf[own_spot(b), :].astype(F32))
        spread_in.put(b, (gh1[b] + normalize_back(grad_a, normed, inverse, vec[0:1, :feats])).astype(BF))
        vpart[0:1, :feats] += column_sum(grad_a * normed)
        vpart[1:2, :feats] += column_sum(grad_a)

    def layer_block(b):
        ids = lax.broadcasted_iota(jnp.int32, (quarter, 1), 0) + (b * 4 + place.near * 2 + place.far) * quarter
        result = h1[b] + sum2.late_total(b) + vec[5:6, :feats]
        spread_lay.put(b, jnp.where(ids < len_ref[0], result, 0.0).astype(BF))

    forward, middle, backward = 1, 1 + nb, 1 + 2 * nb
    end = 3 * nb
    plan = {}

    def at(step, point, action, *args):
        plan.setdefault((step, point), []).append((action, args))

    for k in range(nb - 1):
        at(forward + k + 1, "early", sum1.pass_on, last - k)
    at(forward, "early", far_gather.forward, 0)
    at(forward, "mid", far_gather.forward, 1)
    at(forward, "late", far_gather.forward, 2)
    at(forward + 1, "mid", far_gather.forward, 3)
    at(forward + 1, "late", norm1, last)
    at(forward + 2, "mid", spread_c.relay, last)
    at(forward + 2, "late", far_gather.forward, 4)
    at(forward + 3, "early", copy_cot(last).start)
    at(forward + 3, "late", norm1, last - 1)
    at(forward + 3, "late", far_gather.forward, 5)
    at(middle, "start", sum1.pass_on, 0)
    at(middle, "start", norm1, last - 2)
    for piece in range(4):
        at(middle, "chunk%d" % (piece // 2), far_gather.finish, piece)
    at(middle, "chunk2", far_gather.forward, 6)
    at(middle, "chunk2", spread_c.relay, last - 1)
    for piece in range(4, 6):
        at(middle, "chunk2", far_gather.finish, piece)
    at(middle, "chunk3", far_gather.relay, 7, 0)
    at(middle, "chunk3", far_gather.relay, 7, 1)
    for piece in range(6, 8):
        at(middle, "chunk3", far_gather.finish, piece)
    at(middle, "mid", norm1, last - 3)
    at(middle, "late", spread_c.relay, last - 2)
    for k in range(1, nb):
        at(middle + k, "early", sum3.pass_on, last - k + 1)
        at(middle + k, "early", sum2.stage_all, last - k + 1)
    at(middle + 1, "mid", spread_c.relay, last - 3)
    at(middle + 1, "late", norm3, last)
    at(middle + 2, "early", sum2.to_far(last).start)
    at(middle + 2, "mid", spread_low.relay, last)
    at(middle + 2, "late", norm3, last - 1)
    at(middle + 3, "early", sum2.to_far(last - 1).start)
    at(backward, "start", sum2.stage_all, 0)
    at(backward, "early", spread_low.relay, last - 1)
    at(backward, "early", norm3, last - 2)
    at(backward, "early", sum3.pass_on, 0)
    at(backward, "mid", far_parts[0].pass_on)
    at(backward, "mid", far_parts[2].begin)
    at(backward, "late", spread_low.relay, last - 2)
    at(backward, "late", far_parts[1].pass_on)
    at(backward, "late", far_parts[3].begin)
    for k in range(nb - 1):
        at(backward + k + 1, "early", sum4.pass_on, last - k)
    at(backward + 1, "mid", norm3, last - 3)
    at(backward + 1, "mid", far_parts[2].pass_on)
    at(backward + 1, "late", sum2.to_far(last - 2).start)
    at(backward + 1, "late", sum2.to_far(last - 3).start)
    at(backward + 1, "late", far_parts[3].pass_on)
    at(backward + 2, "mid", spread_low.relay, last - 3)
    at(backward + 3, "mid", norm4, last)

    def run(phase, point):
        for step in range(phase, phase + nb):
            actions = plan.get((step, point), ())
            if actions:
                @pl.when(s == step)
                def _(actions=actions):
                    for action, args in actions:
                        action(*args)

    @pl.when(s == 0)
    def _():
        copy_tokens().start()
        greet(n_dp, n_tensor)
        if small:
            vec_gather.begin(vec_shard[...])
        near_gather.begin_x(3)
        for piece in range(3):
            near_gather.begin_z(piece)
            near_gather.begin_x(piece)
        near_gather.begin_z(3)
        near_gather.cross(3)
        vpart[...] = jnp.zeros_like(vpart)
        copy_tokens().wait()
        if small:
            vec_gather.finish()
            for k in range(n_dp):
                vec[0:6, k * shared_cols:(k + 1) * shared_cols] = vec_buf[k].astype(F32)[0:6, 0:shared_cols]
            for k in range(0, n_dp, 2):
                pair = [vec_buf[k + side].astype(F32)[6:7, 0:split_cols] for side in range(2)]
                vec[6:7, k * split_cols:(k + 2) * split_cols] = jnp.concatenate(pair, axis=1)
        else:
            vec[...] = vec_shard[...].astype(F32)

        def norm(b):
            span = block_rows(b)
            normed, _ = normalize(low[span, :].astype(F32))
            ac[span, :] = (normed * vec[0:1, :feats] + vec[1:2, :feats]).astype(BF)
            copy_a(b).start()
            h1[b] = low[own_rows(b), :].astype(F32) + vec[4:5, :feats]

        over(norm, 0, nb // 2)
        near_gather.forward(0)
        over(norm, nb // 2, nb)
        scale = 1.0 / d**0.5

        def project(kind):
            near_gather.finish(kind)
            cols = slice(kind * width, (kind + 1) * width)

            def step(b):
                span = block_rows(b)
                out = dot(ac[span, :], wj[:, cols])
                if kind == 0:
                    out = (out + vec[6:7, 0:width]) * scale
                if kind == 2:
                    out = out + vec[6:7, width:2 * width]
                qkv[span, cols] = out.astype(BF)

            over(step, 0, nb)

        near_gather.forward(1)
        far_gather.begin_x(len(far_cuts) - 1)
        project(0)
        near_gather.forward(2)
        for piece in range(len(far_cuts)):
            far_gather.begin_z(piece)
        project(1)
        near_gather.relay(3, 0)
        for piece in range(len(far_cuts) - 1):
            far_gather.begin_x(piece)
        project(2)
        far_gather.cross(len(far_cuts) - 1)

        def fill(b):
            first = pl.multiple_of(b * bq, bq)
            fill_keys(qkv, ka, heads, d, slope_fn(heads, total_heads), first, bq)
            gu_buf[turned_spot(b)] = qkv[pl.ds(first, bq), 2 * width:3 * width].T

        over(fill, 0, nb)
        near_gather.relay(3, 1)
        over(lambda b: copy_a(b).wait(), 0, nb)

    @pl.when((s >= forward) & (s < middle))
    def _():
        i = middle - 1 - s
        qt = qkv[block_rows(i), 0:width].T
        ones = stack_rows((128 - d, bq), (1.0, 1.0, 1.0))
        queries = [jnp.concatenate([qt[h * d:(h + 1) * d], ones], axis=0) for h in range(heads)]
        run(forward, "early")

        def block(j, carry, diagonal):
            out = []
            kr = block_rows(j)
            for h in range(heads):
                m, l, total = carry[h]
                scores = dot(ka[h, kr, :], queries[h])
                if diagonal:
                    scores = causal(scores, bq, bq)
                top = jnp.maximum(m, jnp.max(scores, axis=0, keepdims=True))
                p = jnp.exp(scores - top)
                scale = jnp.exp(m - top)
                l = l * scale + jnp.sum(p, axis=0, keepdims=True)
                total = total * scale + dot(gu_buf[turned_spot(j, h * d, d)], p.astype(BF))
                out.append((top, l, total))
            return tuple(out)

        start = (jnp.full((1, bq), LOW, F32), jnp.zeros((1, bq), F32), jnp.zeros((d, bq), F32))
        carry = lax.fori_loop(0, i, lambda j, c: block(j, c, False), (start,) * heads)
        run(forward, "mid")
        carry = block(i, carry, True)
        for h in range(heads):
            m, l, total = carry[h]
            ot[i, h * d:(h + 1) * d, :] = total / l
            lse[i, h:h + 1, :] = m + jnp.log(l)
        out_nat = ot[i].astype(BF).T

        @pl.when(s == forward)
        def _():
            near_gather.finish(3)

        for half_cols in halves:
            part[sum1.slot(i), :, half_cols] = dot(out_nat, wo[half_cols, :], NT).astype(BF)
        sum1.begin(i)
        run(forward, "late")

    @pl.when((s >= middle) & (s < backward))
    def _():
        i = backward - 1 - s
        run(middle, "start")

        @pl.when(s == middle)
        def _():
            acc[...] = jnp.zeros_like(acc)

        spread_c.finish(i)
        copy_cot(i).wait()
        row_ids = lax.broadcasted_iota(jnp.int32, (bq, 128), 0) + i * bq
        live = jnp.where(row_ids < len_ref[0], 1.0, 0.0).astype(BF)
        cot_buf[...] = cot_buf[...] * jnp.concatenate([live] * (feats // 128), axis=1)
        gh1[i] = cot_buf[sum1.rows(place.near, place.far), :].astype(F32)
        run(middle, "early")
        root = math.sqrt(2.0 / math.pi)
        step = 256
        for first in range(0, hidden, step):
            run(middle, "chunk%d" % (first // step))
            cols = slice(first, first + step)
            u = dot(ac[block_rows(i), :], big[:, cols]) + vec[6:7, 2 * width + first:2 * width + first + step]
            square = u * u
            bent = jnp.tanh(root * (u + 0.044715 * (square * u)))
            half = 0.5 * (1.0 + bent)
            hid_buf[:, cols] = (u * half).astype(BF)
            slope = half + 0.5 * u * (1.0 - bent * bent) * (root * (1.0 + 3 * 0.044715 * square))
            grad_u = (dot(cot_buf[...], big[:, hidden + first:hidden + first + step]) * slope).astype(BF)
            gu_buf[:, cols] = grad_u
            vpart[6:7, 2 * width + first:2 * width + first + step] += column_sum(grad_u.astype(F32))
        for half_cols in halves:
            part[sum3.slot(i), :, half_cols] = dot(gu_buf[...], big[half_cols, :hidden], NT).astype(BF)
        sum3.begin(i)
        run(middle, "mid")
        for half_cols in halves:
            part2[sum2.slot(i), :, half_cols] = dot(hid_buf[...], big[half_cols, hidden:], NT).astype(BF)
        sum2.begin(i)
        for r in range(2):
            cols = slice(r * bq, (r + 1) * bq)
            for half_cols in halves:
                acc[r, :, half_cols] += dot(ac[block_rows(i), cols], gu_buf[:, half_cols], TN)
                acc[2 + r, :, half_cols] += dot(cot_buf[:, cols], hid_buf[:, half_cols], TN)

        @pl.when(i > 0)
        def _():
            copy_cot(i - 1).start()

        run(middle, "late")

        @pl.when(s == backward - 1)
        def _():
            for r in range(2):
                span = slice(r * bq, (r + 1) * bq)
                big[span, :hidden] = acc[r].astype(BF)
                big[span, hidden:] = acc[2 + r].astype(BF)
            far_parts[0].begin()
            far_parts[1].begin()
            copy_back().start()
            over(lambda b: copy_own(b).start(), 0, nb)

    @pl.when(s >= backward)
    def _():
        i = end - s
        lanes = lax.broadcasted_iota(jnp.int32, (bq, 128), 1)
        run(backward, "start")

        @pl.when(s == backward)
        def _():
            acc[...] = jnp.zeros_like(acc)

            def fill(b):
                span = block_rows(b)
                gu_buf[turned_spot(b)] = (qkv[span, width:2 * width].astype(F32) * (1.0 / d**0.5)).astype(BF).T
                for h in range(heads):
                    tile = head_tile(qkv, span, 2 * width, h, d)
                    part2[value_spot(h, b)] = jnp.where(lanes < d, tile, jnp.where(lanes < d + 3, 1.0, 0.0)).astype(BF)

            over(fill, 0, nb)

        spread_low.finish(i)
        grad_o = dot(low[block_rows(i), :], wo[...]).astype(BF)
        grad_t = grad_o.T
        q_nat = qkv[block_rows(i), 0:width]
        qt = q_nat.T
        queries, grads, q_pair, g_pair = [], [], [], []
        for h in range(heads):
            hs = slice(h * d, (h + 1) * d)
            delta = jnp.sum(grad_t[hs].astype(F32) * ot[i, hs, :], axis=0, keepdims=True)
            queries.append(jnp.concatenate(
                [qt[hs], stack_rows((128 - d, bq), (1.0, 1.0, 1.0) + three(-lse[i, h:h + 1, :]))], axis=0))
            grads.append(jnp.concatenate([grad_t[hs], stack_rows((128 - d, bq), three(-delta))], axis=0))
            pair = slice((h // 2) * 128, (h // 2) * 128 + 128)
            mine = (lanes < d) if h % 2 == 0 else (lanes >= d)
            q_pair.append(jnp.where(mine, q_nat[:, pair].astype(F32), 0.0).astype(BF))
            g_pair.append(jnp.where(mine, grad_o[:, pair].astype(F32), 0.0).astype(BF))
        run(backward, "early")

        def block(j, carry, diagonal):
            out = []
            kr = block_rows(j)
            for h in range(heads):
                scores = dot(ka[h, kr, :], queries[h])
                if diagonal:
                    scores = causal(scores, bq, bq)
                p = jnp.exp(scores)
                gs = (p * dot(part2[value_spot(h, j)], grads[h])).astype(BF)
                at_k = slice((h // 2) * 128, (h // 2) * 128 + 128)
                at_v = slice(width + (h // 2) * 128, width + (h // 2) * 128 + 128)
                acc[j, :, at_v] += dot(p.astype(BF), g_pair[h])
                acc[j, :, at_k] += dot(gs, q_pair[h])
                out.append(carry[h] + dot(gu_buf[turned_spot(j, h * d, d)], gs))
            return tuple(out)

        carry = lax.fori_loop(0, i, lambda j, c: block(j, c, False), (jnp.zeros((d, bq), F32),) * heads)
        run(backward, "mid")
        carry = block(i, carry, True)
        hid_buf[:, 0:width] = jnp.concatenate(carry, axis=0).T.astype(BF)
        hid_buf[:, width:3 * width] = acc[i, :, 0:2 * width].astype(BF)
        gqkv = hid_buf[:, 0:3 * width]
        for half_cols in halves:
            part[sum4.slot(i), :, half_cols] = dot(gqkv, wj[half_cols, :], NT).astype(BF)
        sum4.begin(i)
        sums = column_sum(gqkv.astype(F32))
        vpart[6:7, 0:width] += sums[:, 0:width]
        vpart[6:7, width:2 * width] += sums[:, 2 * width:]

        @pl.when(s == backward)
        def _():
            copy_back().wait()

        out_nat = ot[i].astype(BF).T
        for r in range(2):
            cols = slice(r * bq, (r + 1) * bq)
            left = ac[block_rows(i), cols]
            acc[2 * r, :, 2 * width:] += dot(left, hid_buf[:, 0:2 * width], TN)
            acc[2 * r + 1, :, 2 * width:3 * width] += dot(left, hid_buf[:, 2 * width:3 * width], TN)
            acc[2 * r + 1, :, 3 * width:] += dot(low[block_rows(i), cols], out_nat, TN)
        run(backward, "late")

    @pl.when(s == end)
    def _():
        sum4.pass_on(0)
        for r in range(2):
            for c in range(2):
                grads_near[r * bq:(r + 1) * bq, c * 2 * width:(c + 1) * 2 * width] = acc[2 * r + c, :, 2 * width:].astype(BF)
        for part_near in near_parts:
            part_near.begin()
        norm4(last - 1)
        near_parts[0].pass_on()
        norm4(last - 2)
        near_parts[1].pass_on()
        norm4(last - 3)
        if small:
            v_send[...] = jnp.zeros_like(v_send)
            for k in range(n_dp):
                v_send[k, 0:6, 0:shared_cols] = vpart[0:6, k * shared_cols:(k + 1) * shared_cols]
                v_send[k, 6:7, 0:split_cols] = vpart[6:7, k * split_cols:(k + 1) * split_cols]
            vec_sum.begin(v_send[me])
        near_parts[2].pass_on()
        near_parts[3].pass_on()
        for part_far in far_parts:
            part_far.finish()
        square = jnp.sum(total_ref[:, feats:] * total_ref[:, feats:])
        if small:
            vec_tensor.begin(vec_sum.total())
        else:
            vec_out[...] = vpart[...]
        spread_in.relay(last)
        spread_in.relay(last - 1)
        layer_block(last)
        layer_block(last - 1)
        for part_near in near_parts:
            part_near.finish()
        square = square + jnp.sum(total_ref[:, :feats] * total_ref[:, :feats])
        if small:
            shared_total = vec_tensor.total()
            row_ids = lax.broadcasted_iota(jnp.int32, vec_out.shape, 0)
            vec_total = jnp.where(row_ids < 6, shared_total, s_buf[rank])
            vec_out[...] = vec_total
            vec_kept = jnp.where(row_ids >= jnp.where(rank == 0, 0, 6), vec_total, 0.0)
            square = square + jnp.sum(vec_kept * vec_kept)
        square_sum.begin(jnp.full(q_buf.shape[1:], square, F32))
        spread_in.relay(last - 2)
        layer_block(last - 2)
        square_tensor.begin(square_sum.total())
        layer_block(last - 3)
        spread_in.relay(last - 3)
        square_out[...] = square_tensor.total()
        for b in range(last, -1, -1):
            spread_lay.relay(b)
        over(spread_in.finish, 0, nb)
        over(spread_lay.finish, 0, nb)


def layer(lengths, tokens, cot, near_shard, far_shard, vec_shard, vec_cols, heads, d, total_heads, bq, n_dp, n_tensor, collective_id):
    n, feats = tokens.shape
    rows = near_shard.shape[0]
    width = heads * d
    hidden = far_shard.shape[1] // 2
    nb, quarter, lines = n // bq, bq // 4, n_dp // 2
    wide = n_dp * max(vec_cols)
    small = n_dp <= 8
    slot = (8, -(-max(vec_cols) // 128) * 128)
    slots = n_dp if small else 1
    near_cuts = [(0, k * width, k * width, width) for k in range(3)] + [(1, 3 * width, 0, width)]
    step = hidden // 2
    far_cuts = [(side * hidden + first, step // 2) for first in range(0, hidden, step // 2) for side in range(2)]
    sum_far = [(k * step, step) for k in range(4)]
    sum_near = [(k * width, width) for k in range(4)]
    dims = (heads, d, total_heads, bq, nb, n_dp, n_tensor, near_cuts, far_cuts, (sum_far, sum_near), vec_cols)
    vm, dma = pltpu.VMEM, pltpu.SemaphoreType.DMA
    own = (nb, quarter, feats)
    sums = [vm((nb, 2 * quarter, feats), BF), vm(own, BF), vm(own, BF)]
    tile = (8, 128)
    kinds = 9 if lines == 4 else 5
    scratch = [
        vm((n, 3 * width), BF), vm((heads, n, 128), BF),
        vm((feats, 2 * hidden), BF), vm((feats, 3 * width), BF), vm((feats, width), BF), vm((n, feats), BF),
        vm((n, feats), BF), vm((nb, width, bq), F32), vm((nb, heads, bq), F32), vm(own, F32), vm(own, F32),
        vm((4, bq, hidden), F32), vm((bq, hidden), BF), vm((bq, hidden), BF), vm((bq, feats), BF),
        vm((3, bq, feats), BF), *sums, vm((2, bq, feats), BF), *sums,
        vm((4, lines, rows, step), BF), vm((4, lines, rows, step), BF),
        vm((4, lines, rows, width), BF), vm((4, lines, rows, width), BF),
        vm((slots,) + vec_shard.shape, BF), vm((16, wide), F32), vm((8, wide), F32),
        vm((slots,) + slot, F32), vm((slots,) + slot, F32), vm((n_tensor,) + slot, F32), vm((n_dp,) + tile, F32), vm((n_tensor,) + tile, F32),
        dma((kinds, len(near_cuts), lines)), dma((kinds, len(far_cuts), lines)), dma((4, 4, nb)), dma((4, 7, nb)),
        dma((4, 4, lines)), dma((4, 4, lines)), dma((1 + nb,)), dma((n_dp,)), dma((n_dp,)), dma((n_dp,)), dma((n_dp,)),
        dma((n_dp,)), dma((n_dp,)), dma((n_tensor,)), dma((n_tensor,)), dma((n_tensor,)), dma((n_tensor,)),
    ]
    shape = jax.ShapeDtypeStruct
    return pl.pallas_call(
        functools.partial(layer_kernel, dims),
        grid=(1 + 3 * nb,),
        in_specs=[pl.BlockSpec(memory_space=pltpu.SMEM)] + [ANYWHERE] * 4 + [whole(vec_shard)],
        out_specs=[fixed((rows, feats + 2 * hidden)), fixed(slot if small else (8, wide)), fixed(tile), ANYWHERE, ANYWHERE, ANYWHERE],
        out_shape=[shape((rows, feats + 2 * hidden), F32), shape(slot if small else (8, wide), F32), shape(tile, F32),
                   shape((n, feats), BF), shape((n, feats), BF), shape((n, feats), BF)],
        scratch_shapes=scratch,
        compiler_params=params(collective_id, 63),
        name="layer",
    )(lengths, tokens, cot, near_shard, far_shard, vec_shard)


def adam_step(master, moment, variance, gradient, rate, decay):
    moment_new = BETA_FIRST * moment + (1.0 - BETA_FIRST) * gradient
    variance_new = BETA_SECOND * variance + (1.0 - BETA_SECOND) * gradient * gradient
    moment_hat = moment_new / (1.0 - BETA_FIRST**STEP)
    variance_hat = variance_new / (1.0 - BETA_SECOND**STEP)
    master_new = master - rate * (
        moment_hat / (jnp.sqrt(variance_hat) + ADAM_EPSILON) + decay * master
    )
    return (master_new, moment_new, variance_new)


def update_kernel(head_size, square_ref, joint_sum, output_sum, widen_sum, narrow_sum, vec_sum, *refs):
    ins, outs, norm_ref = refs[:18], refs[18:36], refs[36]
    norm = jnp.sqrt(square_ref[0:1, 0:1])
    factor = jnp.minimum(1.0, CLIP_LIMIT / (norm + 1e-06))

    def step(at, gradient, rate, decay, cols=slice(None)):
        new = adam_step(*[ref[:, cols] for ref in ins[3 * at:3 * at + 3]], factor * gradient, rate, decay)
        for ref, value in zip(outs[3 * at:3 * at + 3], new):
            ref[:, cols] = value

    joint = ins[0].shape[1]
    heads = joint // (3 * head_size)

    def source(piece):
        head, kind = piece // 3, piece % 3
        first = (kind * heads + head) * head_size
        return joint_sum[:, first:first + head_size]

    for piece in range(0, joint // head_size, 2):
        cols = slice(piece * head_size, (piece + 2) * head_size)
        step(0, jnp.concatenate([source(piece), source(piece + 1)], axis=1), MATRIX_RATE, MATRIX_DECAY, cols)
    step(1, output_sum[...].T, OUTPUT_RATE, MATRIX_DECAY)
    step(2, widen_sum[...], MATRIX_RATE, MATRIX_DECAY)
    step(3, narrow_sum[...].T, MATRIX_RATE, MATRIX_DECAY)

    @pl.when(pl.program_id(0) == 0)
    def _():
        norm_ref[...] = norm
        step(4, vec_sum[0:6, 0:ins[12].shape[1]], VECTOR_RATE, 0.0)
        step(5, vec_sum[6:7, 0:ins[15].shape[1]], VECTOR_RATE, 0.0)


def update(square, sums, vec, states, head_size):
    count = 2
    joint, output, widen, narrow = [states[3 * k].shape for k in range(4)]
    rows = joint[0]

    def halves(shape):
        return pl.BlockSpec((shape[0] // count, shape[1]), lambda i: (i, 0))

    def all_of(shape):
        return pl.BlockSpec(shape, lambda i: (0, 0))

    def columns(first, cols):
        wide = cols // count
        return pl.BlockSpec((rows, wide), lambda i: (0, first // wide + i))

    states_specs = [halves(state.shape) for state in states[:12]] + [all_of(state.shape) for state in states[12:]]
    widen_at, narrow_at = joint[1] + output[0], joint[1] + output[0] + widen[1]
    return pl.pallas_call(
        functools.partial(update_kernel, head_size),
        grid=(count,),
        in_specs=[all_of(square.shape), halves(joint), columns(joint[1], output[0]),
                  pl.BlockSpec((rows // count, widen[1]), lambda i: (i, widen_at // widen[1])),
                  columns(narrow_at, narrow[0]), all_of(vec.shape)] + states_specs,
        out_specs=states_specs + [all_of((1, 1))],
        out_shape=[jax.ShapeDtypeStruct(state.shape, F32) for state in states] + [jax.ShapeDtypeStruct((1, 1), F32)],
        compiler_params=pltpu.CompilerParams(vmem_limit_bytes=63 * 2**20),
        name="update",
    )(square, sums, sums, sums, sums, vec, *states)


def on_device(
    tokens,
    cotangent,
    lengths,
    joint_weight,
    output_weight,
    widen_weight,
    narrow_weight,
    shared_vectors,
    split_vectors,
    joint_first,
    joint_second,
    output_first,
    output_second,
    widen_first,
    widen_second,
    narrow_first,
    narrow_second,
    shared_first,
    shared_second,
    split_first,
    split_second,
):
    n_dp, n_tensor = lax.axis_size("dp"), lax.axis_size("tensor")
    me = lax.axis_index("dp")
    head_cols = output_weight.shape[0]
    near_shard = jnp.concatenate([by_kind(joint_weight), output_weight.T], axis=1).astype(BF)
    far_shard = jnp.concatenate([widen_weight, narrow_weight.T], axis=1).astype(BF)
    shared_cols, split_cols = shared_vectors.shape[1], split_vectors.shape[1]
    vec_cols = -(-max(shared_cols, split_cols) // 128) * 128
    if n_dp <= 8:
        wide = [(shared_vectors, vec_cols - shared_cols), (split_vectors, vec_cols - split_cols)]
        vec_shard = jnp.concatenate([jnp.pad(values, ((0, 0), (0, rest))) for values, rest in wide], axis=0)
    else:
        shared_all = lax.all_gather(shared_vectors.astype(BF), "dp", axis=1, tiled=True)
        split_all = lax.all_gather(split_vectors.astype(BF), "dp", axis=1, tiled=True)
        vec_shard = jnp.concatenate(
            [jnp.pad(shared_all, ((0, 0), (0, split_all.shape[1] - shared_all.shape[1]))), split_all], axis=0
        )
    vec_shard = jnp.pad(vec_shard, ((0, 9), (0, 0))).astype(BF)
    head_size = D // HEADS
    local_heads = head_cols // head_size
    total_rows = tokens.shape[0]
    block = min(512, total_rows)
    sums, vec_sum, square, input_grad, layer_output, _ = layer(
        lengths, tokens, cotangent, near_shard, far_shard, vec_shard, (shared_cols, split_cols), local_heads, head_size, HEADS, block, n_dp,
        n_tensor, 0,
    )
    if n_dp > 8:
        split_all = lax.psum(vec_sum[6:7], "dp")
        shared_all = lax.psum(vec_sum[:6], ("dp", "tensor"))
        square = square + jnp.sum(shared_all * shared_all) + lax.psum(jnp.sum(split_all * split_all), "tensor")
        shared_sum = lax.dynamic_slice(shared_all, (0, me * shared_cols), (6, shared_cols))
        split_sum = lax.dynamic_slice(split_all, (0, me * split_cols), (1, split_cols))
        vec_sum = jnp.concatenate(
            [
                jnp.pad(shared_sum, ((0, 0), (0, vec_cols - shared_cols))),
                jnp.pad(split_sum, ((0, 1), (0, vec_cols - split_cols))),
            ],
            axis=0,
        )
    states = (
        joint_weight, joint_first, joint_second, output_weight, output_first, output_second,
        widen_weight, widen_first, widen_second, narrow_weight, narrow_first, narrow_second,
        shared_vectors, shared_first, shared_second, split_vectors, split_first, split_second,
    )
    *updated, grad_norm = update(square, sums, vec_sum, states, head_size)
    return (layer_output, input_grad, grad_norm.reshape(()), *updated)


def solution(mesh):
    in_specs = (
        P("dp", None),
        P("dp", None),
        P("dp"),
        P("dp", "tensor"),
        P("tensor", "dp"),
        P("dp", "tensor"),
        P("tensor", "dp"),
        P(None, "dp"),
        P("tensor", "dp"),
        P("dp", "tensor"),
        P("dp", "tensor"),
        P("tensor", "dp"),
        P("tensor", "dp"),
        P("dp", "tensor"),
        P("dp", "tensor"),
        P("tensor", "dp"),
        P("tensor", "dp"),
        P(None, "dp"),
        P(None, "dp"),
        P("tensor", "dp"),
        P("tensor", "dp"),
    )
    out_specs = (
        P("dp", None),
        P("dp", None),
        P(),
        P("dp", "tensor"),
        P("dp", "tensor"),
        P("dp", "tensor"),
        P("tensor", "dp"),
        P("tensor", "dp"),
        P("tensor", "dp"),
        P("dp", "tensor"),
        P("dp", "tensor"),
        P("dp", "tensor"),
        P("tensor", "dp"),
        P("tensor", "dp"),
        P("tensor", "dp"),
        P(None, "dp"),
        P(None, "dp"),
        P(None, "dp"),
        P("tensor", "dp"),
        P("tensor", "dp"),
        P("tensor", "dp"),
    )
    return jax.shard_map(
        on_device, mesh=mesh, in_specs=in_specs, out_specs=out_specs, check_vma=False
    )
```

```python
import functools
import math

import jax
import jax.numpy as jnp
from jax import lax
from jax.experimental import pallas as pl
from jax.experimental.pallas import tpu as pltpu
from jax.sharding import PartitionSpec as P

F32, BF = jnp.float32, jnp.bfloat16

D = 1024
HEADS = 16
STEP = 10


NORM_EPSILON = 1e-05
CLIP_LIMIT = 1.0
BETA_FIRST = 0.9
BETA_SECOND = 0.95
ADAM_EPSILON = 1e-08
MATRIX_RATE = 0.05
OUTPUT_RATE = 0.2
VECTOR_RATE = 0.6
MATRIX_DECAY = 0.1


NN = (((1,), (0,)), ((), ()))
NT = (((1,), (1,)), ((), ()))
TN = (((0,), (0,)), ((), ()))
LOW = -1e30


def dot(left, right, dims=NN):
    return lax.dot_general(left, right, dims, preferred_element_type=F32)


def three(values):
    high = values.astype(BF).astype(F32)
    rest = values - high
    middle = rest.astype(BF).astype(F32)
    return high, middle, rest - middle


def stack_rows(shape, rows):
    ids = lax.broadcasted_iota(jnp.int32, shape, 0)
    out = jnp.zeros(shape, F32)
    for at, row in enumerate(rows):
        out = jnp.where(ids == at, row, out)
    return out.astype(BF)


def head_tile(ref, rows, col, head, d):
    lane = col + (head // 2) * 128
    tile = ref[rows, lane:lane + 128].astype(F32)
    if head % 2:
        tile = pltpu.roll(tile, 64, 1)
    return tile


def fill_keys(qkv_ref, ka_ref, heads, d, slope_of, first, count):
    rows = pl.ds(first, count)
    lanes = lax.broadcasted_iota(jnp.int32, (count, 128), 1)
    position = (lax.broadcasted_iota(jnp.int32, (count, 128), 0) + first).astype(F32)
    for head in range(heads):
        high, middle, low = three(position * slope_of(head))
        tile = head_tile(qkv_ref, rows, heads * d, head, d)
        for at, part in enumerate((high, middle, low, 1.0, 1.0, 1.0)):
            tile = jnp.where(lanes == d + at, part, tile)
        ka_ref[head, rows, :] = jnp.where(lanes < d + 6, tile, 0.0).astype(BF)


def causal(scores, bk, bq):
    kid = lax.broadcasted_iota(jnp.int32, (bk, bq), 0)
    qid = lax.broadcasted_iota(jnp.int32, (bk, bq), 1)
    return jnp.where(kid <= qid, scores, LOW)


def slope_fn(heads, total_heads):
    rank = lax.axis_index("tensor")
    def slope_of(head):
        index = jnp.full((1, 128), rank * heads + head + 1, jnp.int32).astype(F32)
        return jnp.exp2(index * (-8.0 / total_heads))
    return slope_of


def at_dp(index):
    return {"dp": index}


def at_tensor(index):
    return {"tensor": index}


def remote(src, dst, send, recv, where):
    return pltpu.make_async_remote_copy(
        src_ref=src, dst_ref=dst, send_sem=send, recv_sem=recv, device_id=where, device_id_type=pl.DeviceIdType.MESH
    )


def greet(n_dp, n_tensor):
    me, rank = lax.axis_index("dp"), lax.axis_index("tensor")
    barrier = pltpu.get_barrier_semaphore()

    def along_dp(k, c):
        pl.semaphore_signal(barrier, inc=1, device_id=at_dp(lax.rem(me + k, n_dp)), device_id_type=pl.DeviceIdType.MESH)
        return c

    lax.fori_loop(1, n_dp, along_dp, 0)
    for k in range(1, n_tensor):
        pl.semaphore_signal(
            barrier, inc=1, device_id=at_tensor(lax.rem(rank + k, n_tensor)), device_id_type=pl.DeviceIdType.MESH
        )
    pl.semaphore_wait(barrier, n_dp + n_tensor - 2)


def over(body, first, last):
    lax.fori_loop(first, last, lambda k, c: (body(k), c)[1], 0)


def greet_tensor(n_tensor):
    rank = lax.axis_index("tensor")
    barrier = pltpu.get_barrier_semaphore()
    for k in range(1, n_tensor):
        pl.semaphore_signal(
            barrier, inc=1, device_id=at_tensor(lax.rem(rank + k, n_tensor)), device_id_type=pl.DeviceIdType.MESH
        )
    pl.semaphore_wait(barrier, n_tensor - 1)


class Gather:
    def __init__(self, lines, rows, pieces, sems):
        me = lax.axis_index("dp")
        self.me, self.z, self.x = me, me // 2, lax.rem(me, 2)
        self.lines, self.rows, self.pieces, self.sems = lines, rows, pieces, sems
        self.other = at_dp(self.z * 2 + 1 - self.x)
        self.relayed = lines == 4

    def crossing(self, s):
        return self.relayed and self.pieces[s][5]

    def own(self, s):
        shard, first, _, cols = self.pieces[s][:4]
        return shard.at[:, pl.ds(first, cols)]

    def spot(self, s, zz, column):
        _, _, first, cols, out = self.pieces[s][:5]
        device = zz * 2 + (self.x if column == 0 else 1 - self.x)
        return out.at[pl.ds(pl.multiple_of(device * self.rows, self.rows), self.rows), pl.ds(first, cols)]

    def sem(self, kind, s, index):
        return self.sems.at[kind, s, index]

    def to_x(self, s, zz, src):
        return remote(src, self.spot(s, zz, 0), self.sem(0, s, zz), self.sem(1, s, zz), self.other)

    def from_x(self, s, zz):
        spot = self.spot(s, zz, 1)
        return remote(spot, spot, self.sem(0, s, zz), self.sem(1, s, zz), self.other)

    def along_z(self, s, column, src, zz, send, target):
        kind = 2 + 2 * column
        return remote(src, self.spot(s, zz, column), send, self.sem(kind + 1, s, zz), at_dp(target * 2 + self.x))

    def to_z(self, s, column, k):
        src = self.own(s) if column == 0 else self.spot(s, self.z, 1)
        return self.along_z(s, column, src, self.z, self.sem(2 + 2 * column, s, k), lax.rem(self.z + k, self.lines))

    def each_to_z(self, s, column, action):
        def step(k):
            if not self.relayed:
                action(self.to_z(s, column, k))
                return
            gap = lax.rem(self.z + k, self.lines) - self.z

            @pl.when((gap != 3) & (gap != -3))
            def _():
                action(self.to_z(s, column, k))

        over(step, 1, self.lines)

    def from_z(self, s, column, zz):
        spot = self.spot(s, zz, column)
        return self.along_z(s, column, spot, zz, self.sem(2 + 2 * column, s, 0), self.z)

    def relay_copy(self, s, column):
        source, target = jnp.where(self.z == 2, 0, 3), jnp.where(self.z == 2, 3, 0)
        return self.along_z(s, column, self.spot(s, source, column), source, self.sem(6 + column, s, 0), target)

    def inner(self):
        return (self.z == 1) | (self.z == 2)

    def relays(self, zz):
        return ((self.z == 2) & (zz == 0)) | ((self.z == 1) & (zz == 3))

    def keep(self, s):
        return pltpu.make_async_copy(self.own(s), self.spot(s, self.z, 0), self.sem(self.sems.shape[0] - 1, s, 0))

    def begin_z(self, s):
        self.each_to_z(s, 0, lambda copy: copy.start())
        self.keep(s).start()

    def begin_x(self, s):
        self.to_x(s, self.z, self.own(s)).start()

    def forward(self, s):
        def step(k):
            zz = lax.rem(self.z + k, self.lines)
            self.from_z(s, 0, zz).wait_recv()
            if self.relayed:
                @pl.when(self.relays(zz))
                def _():
                    self.relay_copy(s, 0).start()
            self.to_x(s, zz, self.spot(s, zz, 0)).start()

        over(step, 1, self.lines)

    def cross(self, s):
        if not self.crossing(s):
            return
        self.from_x(s, self.z).wait_recv()
        self.each_to_z(s, 1, lambda copy: copy.start())

    def relay(self, s, column):
        if not self.crossing(s):
            if column == 0:
                self.forward(s)
            return

        @pl.when(self.inner())
        def _():
            self.from_z(s, column, jnp.where(self.z == 2, 0, 3)).wait_recv()
            self.relay_copy(s, column).start()

    def finish(self, s):
        self.keep(s).wait()
        columns = range(2 if self.crossing(s) else 1)
        for column in columns:
            self.each_to_z(s, column, lambda copy: copy.wait_send())
            if self.relayed:
                @pl.when(self.inner())
                def _(column=column):
                    self.relay_copy(s, column).wait_send()
        if self.crossing(s):
            self.to_x(s, self.z, self.own(s)).wait_send()
            for column in columns:
                def arrived(k, column=column):
                    zz = lax.rem(self.z + k, self.lines)

                    @pl.when(jnp.logical_not(self.relays(zz)))
                    def _():
                        self.from_z(s, column, zz).wait_recv()

                over(arrived, 1, self.lines)
        else:
            over(lambda zz: self.to_x(s, zz, self.own(s)).wait_send(), 0, self.lines)
            over(lambda zz: self.from_x(s, zz).wait_recv(), 0, self.lines)


class Place:
    def __init__(self):
        rank = lax.axis_index("tensor")
        self.far, self.near = rank // 2, lax.rem(rank, 2)
        self.near_device = at_tensor(self.far * 2 + 1 - self.near)
        self.far_device = at_tensor((1 - self.far) * 2 + self.near)


class BlockSum:
    def __init__(self, place, quarter, part, slot, near_buf, send_buf, far_buf, sems):
        self.place, self.quarter, self.part, self.slot = place, quarter, part, slot
        self.near_buf, self.send_buf, self.far_buf, self.sems = near_buf, send_buf, far_buf, sems

    def rows(self, near, far):
        first = (near * 2 + far) * self.quarter
        return pl.ds(pl.multiple_of(first, self.quarter), self.quarter)

    def half(self, near):
        first = near * 2 * self.quarter
        return pl.ds(pl.multiple_of(first, self.quarter), 2 * self.quarter)

    def to_near(self, b):
        return remote(self.part.at[self.slot(b), self.half(1 - self.place.near)], self.near_buf.at[b],
                      self.sems.at[0, b], self.sems.at[1, b], self.place.near_device)

    def to_far(self, b):
        return remote(self.send_buf.at[b], self.far_buf.at[b], self.sems.at[2, b], self.sems.at[3, b],
                      self.place.far_device)

    def pair(self, b, far):
        own = self.part[self.slot(b), self.rows(self.place.near, far)].astype(F32)
        return own + self.near_buf[b, self.rows(0, far)].astype(F32)

    def begin(self, b):
        self.to_near(b).start()

    def stage(self, b):
        self.to_near(b).wait_recv()
        self.send_buf[b] = self.pair(b, 1 - self.place.far).astype(BF)

    def pass_on(self, b):
        self.stage(b)
        self.to_far(b).start()

    def total(self, b):
        self.to_far(b).wait()
        self.to_near(b).wait_send()
        return self.pair(b, self.place.far) + self.far_buf[b].astype(F32)

    def stage_all(self, b):
        self.stage(b)
        rows = self.rows(0, self.place.far)
        self.near_buf[b, rows] = self.pair(b, self.place.far).astype(BF)
        self.to_near(b).wait_send()

    def late_total(self, b):
        self.to_far(b).wait()
        return self.near_buf[b, self.rows(0, self.place.far)].astype(F32) + self.far_buf[b].astype(F32)


class BlockSpread:
    def __init__(self, place, quarter, out, sems, own=None):
        self.place, self.quarter, self.out, self.sems, self.own = place, quarter, out, sems, own

    def rows(self, b, near, far):
        first = (b * 4 + near * 2 + far) * self.quarter
        return pl.ds(pl.multiple_of(first, self.quarter), self.quarter)

    def spot(self, b, near, far):
        return self.out.at[self.rows(b, near, far)]

    def mine(self, b):
        return self.spot(b, self.place.near, self.place.far)

    def source(self, b):
        return self.mine(b) if self.own is None else self.own.at[b]

    def put(self, b, values):
        if self.own is None:
            self.out[self.rows(b, self.place.near, self.place.far), :] = values
        else:
            self.own[b] = values
        self.to_far(b).start()
        self.to_near(b).start()
        if self.own is not None:
            self.keep(b).start()

    def to_far(self, b):
        return remote(self.source(b), self.mine(b), self.sems.at[0, b], self.sems.at[1, b], self.place.far_device)

    def to_near(self, b):
        return remote(self.source(b), self.mine(b), self.sems.at[2, b], self.sems.at[3, b], self.place.near_device)

    def arrival(self, near, far, b, at):
        spot = self.spot(b, near, far)
        return remote(spot, spot, self.sems.at[at - 1, b], self.sems.at[at, b], self.place.near_device)

    def pass_far(self, b):
        spot = self.spot(b, self.place.near, 1 - self.place.far)
        return remote(spot, spot, self.sems.at[4, b], self.sems.at[5, b], self.place.near_device)

    def keep(self, b):
        return pltpu.make_async_copy(self.own.at[b], self.mine(b), self.sems.at[6, b])

    def relay(self, b):
        self.arrival(self.place.near, 1 - self.place.far, b, 1).wait_recv()
        self.pass_far(b).start()

    def finish(self, b):
        self.to_far(b).wait_send()
        self.to_near(b).wait_send()
        self.pass_far(b).wait_send()
        if self.own is not None:
            self.keep(b).wait()
        self.arrival(1 - self.place.near, self.place.far, b, 3).wait_recv()
        self.arrival(1 - self.place.near, 1 - self.place.far, b, 5).wait_recv()


def normalize(values):
    centred = values - jnp.mean(values, axis=-1, keepdims=True)
    inverse = lax.rsqrt(jnp.mean(centred * centred, axis=-1, keepdims=True) + NORM_EPSILON)
    return (centred * inverse, inverse)


def normalize_back(incoming, normed, inverse, gain):
    scaled = incoming * gain
    return inverse * (
        scaled
        - jnp.mean(scaled, axis=-1, keepdims=True)
        - normed * jnp.mean(scaled * normed, axis=-1, keepdims=True)
    )


def column_sum(values):
    return jnp.sum(values, axis=0, keepdims=True)


def params(collective_id, megabytes):
    return pltpu.CompilerParams(
        collective_id=collective_id, has_side_effects=True, vmem_limit_bytes=megabytes * 2**20
    )


ANYWHERE = pl.BlockSpec(memory_space=pl.ANY)


def fixed(shape):
    return pl.BlockSpec(shape, lambda i: (0,) * len(shape), pipeline_mode=pl.Buffered(1))


def whole(array):
    return fixed(array.shape)


class Scatter:
    def __init__(self, lines, rows, source, first, cols, x_buf, z_buf, total, at, sems, part):
        me = lax.axis_index("dp")
        self.z, self.x = me // 2, lax.rem(me, 2)
        self.lines, self.rows, self.source = lines, rows, source
        self.cols, self.total_cols = pl.ds(first, cols), pl.ds(at, cols)
        self.x_buf, self.z_buf, self.total, self.sems, self.part = x_buf, z_buf, total, sems, part

    def dest(self, k):
        return lax.rem(self.z + 1 + k, self.lines)

    def chunk(self, device):
        return (pl.ds(pl.multiple_of(device * self.rows, self.rows), self.rows), self.cols)

    def sem(self, kind, index):
        return self.sems.at[kind, self.part, index]

    def to_x(self, dz):
        return remote(self.source.at[self.chunk(dz * 2 + 1 - self.x)], self.x_buf.at[dz], self.sem(0, dz),
                      self.sem(1, dz), at_dp(self.z * 2 + 1 - self.x))

    def to_z(self, dz):
        return remote(self.x_buf.at[dz], self.z_buf.at[self.z], self.sem(2, dz), self.sem(3, self.z),
                      at_dp(dz * 2 + self.x))

    def from_z(self, zz):
        return remote(self.z_buf.at[zz], self.z_buf.at[zz], self.sem(2, zz), self.sem(3, zz), at_dp(zz * 2 + self.x))

    def begin(self):
        over(lambda k: self.to_x(self.dest(k)).start(), 0, self.lines)

    def summed(self, dz):
        self.to_x(dz).wait()
        return self.x_buf[dz].astype(F32) + self.source[self.chunk(dz * 2 + self.x)].astype(F32)

    def pass_on(self):
        def step(k):
            dz = self.dest(k)
            self.x_buf[dz] = self.summed(dz).astype(BF)
            self.to_z(dz).start()

        over(step, 0, self.lines - 1)
        self.total[:, self.total_cols] = self.summed(self.z)

    def finish(self):
        def add(k):
            zz = lax.rem(self.z + k, self.lines)
            self.from_z(zz).wait_recv()
            self.total[:, self.total_cols] += self.z_buf[zz].astype(F32)
            self.to_z(zz).wait_send()

        over(add, 1, self.lines)


class Exchange:
    def __init__(self, buf, index, count, where, send, recv, pieces=None):
        self.buf, self.index, self.count, self.where = buf, index, count, where
        self.send, self.recv, self.pieces = send, recv, pieces

    def to(self, k):
        other = lax.rem(self.index + k, self.count)
        source = self.buf.at[self.index] if self.pieces is None else self.pieces.at[other]
        return remote(source, self.buf.at[self.index], self.send.at[k], self.recv.at[self.index], self.where(other))

    def begin(self, values):
        self.buf[self.index] = values
        over(lambda k: self.to(k).start(), 1, self.count)

    def finish(self):
        def arrived(k):
            other = lax.rem(self.index + k, self.count)
            remote(self.buf.at[other], self.buf.at[other], self.send.at[0], self.recv.at[other],
                   self.where(other)).wait_recv()
            self.to(k).wait_send()

        over(arrived, 1, self.count)

    def total(self):
        self.finish()
        zero = jnp.zeros(self.buf.shape[1:], F32)
        return lax.fori_loop(0, self.count, lambda k, acc: acc + self.buf[k], zero)


def layer_kernel(dims, len_ref, tok_ref, cot_ref, near_shard, far_shard, vec_shard,
                 total_ref, vec_out, square_out, in_out, lay_out, a_hbm, *scratch):
    heads, d, total_heads, bq, nb, n_dp, n_tensor, near_cuts, far_cuts, sum_cuts, vec_cols = dims
    (qkv, ka, big, wj, wo, ac, low, ot, lse, h1, gh1, acc, hid_buf, gu_buf, cot_buf,
     part, near_buf, send_buf, far_buf, part2, near2_buf, send2_buf, far2_buf, x_far, z_far, x_near, z_near,
     vec_buf, vec, vpart, v_send, v_buf, s_buf, q_buf, t_buf,
     gn_sems, gf_sems, sum_sems, spread_sems, sf_sems, sn_sems, copy_sems, vs, vr, vs2, vr2, qs, qr, ss, sr, ts, tr) = scratch
    s = pl.program_id(0)
    place = Place()
    me, rank = lax.axis_index("dp"), lax.axis_index("tensor")
    width, feats, hidden = heads * d, ac.shape[1], big.shape[1] // 2
    quarter, lines, rows = bq // 4, n_dp // 2, total_ref.shape[0]
    last = nb - 1
    halves = (slice(0, feats // 2), slice(feats // 2, feats))
    small = n_dp <= 8

    def slot_from(base):
        return lambda b: lax.rem(base + last - b, 3)

    sum1, sum3, sum4 = (
        BlockSum(place, quarter, part, slot_from(k * nb), near_buf, send_buf, far_buf, sum_sems.at[k]) for k in range(3)
    )
    sum2 = BlockSum(place, quarter, part2, lambda b: lax.rem(last - b, 2), near2_buf, send2_buf, far2_buf, sum_sems.at[3])
    spread_c = BlockSpread(place, quarter, ac, spread_sems.at[0])
    spread_low = BlockSpread(place, quarter, low, spread_sems.at[1])
    spread_lay = BlockSpread(place, quarter, lay_out, spread_sems.at[2], send2_buf)
    spread_in = BlockSpread(place, quarter, in_out, spread_sems.at[3], send_buf)
    near_gather = Gather(lines, rows, [
        (near_shard, first, at, cols, (wj, wo)[index], index == 1) for index, first, at, cols in near_cuts],
                         gn_sems)
    far_gather = Gather(lines, rows, [
        (far_shard, first, first, cols, big, p == len(far_cuts) - 1) for p, (first, cols) in enumerate(far_cuts)], gf_sems)
    grads_near = part2.reshape(2 * bq, feats)
    far_parts = [
        Scatter(lines, rows, big, first, cols, x_far.at[p], z_far.at[p], total_ref, feats + first, sf_sems, p)
        for p, (first, cols) in enumerate(sum_cuts[0])
    ]
    near_parts = [
        Scatter(lines, rows, grads_near, first, cols, x_near.at[p], z_near.at[p], total_ref, first, sn_sems, p)
        for p, (first, cols) in enumerate(sum_cuts[1])
    ]
    vec_gather = Exchange(vec_buf, me, n_dp, at_dp, vs, vr)
    vec_sum = Exchange(v_buf, me, n_dp, at_dp, vs2, vr2, v_send)
    shared_cols, split_cols = vec_cols
    vec_tensor = Exchange(s_buf, rank, n_tensor, at_tensor, ss, sr)
    square_sum = Exchange(q_buf, me, n_dp, at_dp, qs, qr)
    square_tensor = Exchange(t_buf, rank, n_tensor, at_tensor, ts, tr)

    def block_rows(b):
        return pl.ds(pl.multiple_of(b * bq, bq), bq)

    def turned_spot(b, first=0, count=None):
        row = pl.multiple_of(lax.rem(b, 2) * width + first, d)
        return (pl.ds(row, width if count is None else count), pl.ds(pl.multiple_of(b // 2 * bq, bq), bq))

    def value_spot(h, b):
        lane = pl.multiple_of(((h % 2) * nb + b) * 128, 128)
        return (h // 2, slice(None), pl.ds(lane, 128))

    def own_rows(b):
        return spread_c.rows(b, place.near, place.far)

    def copy_tokens():
        return pltpu.make_async_copy(tok_ref, low, copy_sems.at[0])

    def copy_a(b):
        return pltpu.make_async_copy(ac.at[block_rows(b)], a_hbm.at[block_rows(b)], copy_sems.at[1 + b])

    def copy_back():
        return pltpu.make_async_copy(a_hbm, ac, copy_sems.at[0])

    def copy_cot(b):
        return pltpu.make_async_copy(cot_ref.at[block_rows(b)], cot_buf, copy_sems.at[0])

    def own_spot(b):
        return pl.ds(pl.multiple_of(b * quarter, quarter), quarter)

    def copy_own(b):
        return pltpu.make_async_copy(tok_ref.at[own_rows(b)], cot_buf.at[own_spot(b)], copy_sems.at[1 + b])

    def norm1(b):
        hidden_one = h1[b] + sum1.total(b)
        h1[b] = hidden_one
        normed, _ = normalize(hidden_one)
        spread_c.put(b, (normed * vec[2:3, :feats] + vec[3:4, :feats]).astype(BF))

    def norm3(b):
        grad_c = sum3.total(b)
        normed, inverse = normalize(h1[b])
        grad_out = gh1[b]
        grad_h = grad_out + normalize_back(grad_c, normed, inverse, vec[2:3, :feats])
        gh1[b] = grad_h
        spread_low.put(b, grad_h.astype(BF))
        vpart[2:3, :feats] += column_sum(grad_c * normed)
        vpart[3:4, :feats] += column_sum(grad_c)
        vpart[4:5, :feats] += column_sum(grad_h)
        vpart[5:6, :feats] += column_sum(grad_out)

    def norm4(b):
        grad_a = sum4.total(b)
        copy_own(b).wait()
        normed, inverse = normalize(cot_buf[own_spot(b), :].astype(F32))
        spread_in.put(b, (gh1[b] + normalize_back(grad_a, normed, inverse, vec[0:1, :feats])).astype(BF))
        vpart[0:1, :feats] += column_sum(grad_a * normed)
        vpart[1:2, :feats] += column_sum(grad_a)

    def layer_block(b):
        ids = lax.broadcasted_iota(jnp.int32, (quarter, 1), 0) + (b * 4 + place.near * 2 + place.far) * quarter
        result = h1[b] + sum2.late_total(b) + vec[5:6, :feats]
        spread_lay.put(b, jnp.where(ids < len_ref[0], result, 0.0).astype(BF))

    forward, middle, backward = 1, 1 + nb, 1 + 2 * nb
    end = 3 * nb
    plan = {}

    def at(step, point, action, *args):
        plan.setdefault((step, point), []).append((action, args))

    for k in range(nb - 1):
        at(forward + k + 1, "early", sum1.pass_on, last - k)
    at(forward, "early", far_gather.forward, 0)
    at(forward, "mid", far_gather.forward, 1)
    at(forward, "late", far_gather.forward, 2)
    at(forward + 1, "mid", far_gather.forward, 3)
    at(forward + 1, "late", norm1, last)
    at(forward + 2, "mid", spread_c.relay, last)
    at(forward + 2, "late", far_gather.forward, 4)
    at(forward + 3, "early", copy_cot(last).start)
    at(forward + 3, "late", norm1, last - 1)
    at(forward + 3, "late", far_gather.forward, 5)
    at(middle, "start", sum1.pass_on, 0)
    at(middle, "start", norm1, last - 2)
    for piece in range(4):
        at(middle, "chunk%d" % (piece // 2), far_gather.finish, piece)
    at(middle, "chunk2", far_gather.forward, 6)
    at(middle, "chunk2", spread_c.relay, last - 1)
    for piece in range(4, 6):
        at(middle, "chunk2", far_gather.finish, piece)
    at(middle, "chunk3", far_gather.relay, 7, 0)
    at(middle, "chunk3", far_gather.relay, 7, 1)
    for piece in range(6, 8):
        at(middle, "chunk3", far_gather.finish, piece)
    at(middle, "mid", norm1, last - 3)
    at(middle, "late", spread_c.relay, last - 2)
    for k in range(1, nb):
        at(middle + k, "early", sum3.pass_on, last - k + 1)
        at(middle + k, "early", sum2.stage_all, last - k + 1)
    at(middle + 1, "mid", spread_c.relay, last - 3)
    at(middle + 1, "late", norm3, last)
    at(middle + 2, "early", sum2.to_far(last).start)
    at(middle + 2, "mid", spread_low.relay, last)
    at(middle + 2, "late", norm3, last - 1)
    at(middle + 3, "early", sum2.to_far(last - 1).start)
    at(backward, "start", sum2.stage_all, 0)
    at(backward, "early", spread_low.relay, last - 1)
    at(backward, "early", norm3, last - 2)
    at(backward, "early", sum3.pass_on, 0)
    at(backward, "mid", far_parts[0].pass_on)
    at(backward, "mid", far_parts[2].begin)
    at(backward, "late", spread_low.relay, last - 2)
    at(backward, "late", far_parts[1].pass_on)
    at(backward, "late", far_parts[3].begin)
    for k in range(nb - 1):
        at(backward + k + 1, "early", sum4.pass_on, last - k)
    at(backward + 1, "mid", norm3, last - 3)
    at(backward + 1, "mid", far_parts[2].pass_on)
    at(backward + 1, "late", sum2.to_far(last - 2).start)
    at(backward + 1, "late", sum2.to_far(last - 3).start)
    at(backward + 1, "late", far_parts[3].pass_on)
    at(backward + 2, "mid", spread_low.relay, last - 3)
    at(backward + 3, "mid", norm4, last)

    def run(phase, point):
        for step in range(phase, phase + nb):
            actions = plan.get((step, point), ())
            if actions:
                @pl.when(s == step)
                def _(actions=actions):
                    for action, args in actions:
                        action(*args)

    @pl.when(s == 0)
    def _():
        copy_tokens().start()
        greet(n_dp, n_tensor)
        if small:
            vec_gather.begin(vec_shard[...])
        near_gather.begin_x(3)
        for piece in range(3):
            near_gather.begin_z(piece)
            near_gather.begin_x(piece)
        near_gather.begin_z(3)
        near_gather.cross(3)
        vpart[...] = jnp.zeros_like(vpart)
        copy_tokens().wait()
        if small:
            vec_gather.finish()
            for k in range(n_dp):
                vec[0:6, k * shared_cols:(k + 1) * shared_cols] = vec_buf[k].astype(F32)[0:6, 0:shared_cols]
            for k in range(0, n_dp, 2):
                pair = [vec_buf[k + side].astype(F32)[6:7, 0:split_cols] for side in range(2)]
                vec[6:7, k * split_cols:(k + 2) * split_cols] = jnp.concatenate(pair, axis=1)
        else:
            vec[...] = vec_shard[...].astype(F32)

        def norm(b):
            span = block_rows(b)
            normed, _ = normalize(low[span, :].astype(F32))
            ac[span, :] = (normed * vec[0:1, :feats] + vec[1:2, :feats]).astype(BF)
            copy_a(b).start()
            h1[b] = low[own_rows(b), :].astype(F32) + vec[4:5, :feats]

        over(norm, 0, nb // 2)
        near_gather.forward(0)
        over(norm, nb // 2, nb)
        scale = 1.0 / d**0.5

        def project(kind):
            near_gather.finish(kind)
            cols = slice(kind * width, (kind + 1) * width)

            def step(b):
                span = block_rows(b)
                out = dot(ac[span, :], wj[:, cols])
                if kind == 0:
                    out = (out + vec[6:7, 0:width]) * scale
                if kind == 2:
                    out = out + vec[6:7, width:2 * width]
                qkv[span, cols] = out.astype(BF)

            over(step, 0, nb)

        near_gather.forward(1)
        far_gather.begin_x(len(far_cuts) - 1)
        project(0)
        near_gather.forward(2)
        for piece in range(len(far_cuts)):
            far_gather.begin_z(piece)
        project(1)
        near_gather.relay(3, 0)
        for piece in range(len(far_cuts) - 1):
            far_gather.begin_x(piece)
        project(2)
        far_gather.cross(len(far_cuts) - 1)

        def fill(b):
            first = pl.multiple_of(b * bq, bq)
            fill_keys(qkv, ka, heads, d, slope_fn(heads, total_heads), first, bq)
            gu_buf[turned_spot(b)] = qkv[pl.ds(first, bq), 2 * width:3 * width].T

        over(fill, 0, nb)
        near_gather.relay(3, 1)
        over(lambda b: copy_a(b).wait(), 0, nb)

    @pl.when((s >= forward) & (s < middle))
    def _():
        i = middle - 1 - s
        qt = qkv[block_rows(i), 0:width].T
        ones = stack_rows((128 - d, bq), (1.0, 1.0, 1.0))
        queries = [jnp.concatenate([qt[h * d:(h + 1) * d], ones], axis=0) for h in range(heads)]
        run(forward, "early")

        def block(j, carry, diagonal):
            out = []
            kr = block_rows(j)
            for h in range(heads):
                m, l, total = carry[h]
                scores = dot(ka[h, kr, :], queries[h])
                if diagonal:
                    scores = causal(scores, bq, bq)
                top = jnp.maximum(m, jnp.max(scores, axis=0, keepdims=True))
                p = jnp.exp(scores - top)
                scale = jnp.exp(m - top)
                l = l * scale + jnp.sum(p, axis=0, keepdims=True)
                total = total * scale + dot(gu_buf[turned_spot(j, h * d, d)], p.astype(BF))
                out.append((top, l, total))
            return tuple(out)

        start = (jnp.full((1, bq), LOW, F32), jnp.zeros((1, bq), F32), jnp.zeros((d, bq), F32))
        carry = lax.fori_loop(0, i, lambda j, c: block(j, c, False), (start,) * heads)
        run(forward, "mid")
        carry = block(i, carry, True)
        for h in range(heads):
            m, l, total = carry[h]
            ot[i, h * d:(h + 1) * d, :] = total / l
            lse[i, h:h + 1, :] = m + jnp.log(l)
        out_nat = ot[i].astype(BF).T

        @pl.when(s == forward)
        def _():
            near_gather.finish(3)

        for half_cols in halves:
            part[sum1.slot(i), :, half_cols] = dot(out_nat, wo[half_cols, :], NT).astype(BF)
        sum1.begin(i)
        run(forward, "late")

    @pl.when((s >= middle) & (s < backward))
    def _():
        i = backward - 1 - s
        run(middle, "start")

        @pl.when(s == middle)
        def _():
            acc[...] = jnp.zeros_like(acc)

        spread_c.finish(i)
        copy_cot(i).wait()
        row_ids = lax.broadcasted_iota(jnp.int32, (bq, 128), 0) + i * bq
        live = jnp.where(row_ids < len_ref[0], 1.0, 0.0).astype(BF)
        cot_buf[...] = cot_buf[...] * jnp.concatenate([live] * (feats // 128), axis=1)
        gh1[i] = cot_buf[sum1.rows(place.near, place.far), :].astype(F32)
        run(middle, "early")
        root = math.sqrt(2.0 / math.pi)
        step = 256
        for first in range(0, hidden, step):
            run(middle, "chunk%d" % (first // step))
            cols = slice(first, first + step)
            u = dot(ac[block_rows(i), :], big[:, cols]) + vec[6:7, 2 * width + first:2 * width + first + step]
            square = u * u
            bent = jnp.tanh(root * (u + 0.044715 * (square * u)))
            half = 0.5 * (1.0 + bent)
            hid_buf[:, cols] = (u * half).astype(BF)
            slope = half + 0.5 * u * (1.0 - bent * bent) * (root * (1.0 + 3 * 0.044715 * square))
            grad_u = (dot(cot_buf[...], big[:, hidden + first:hidden + first + step]) * slope).astype(BF)
            gu_buf[:, cols] = grad_u
            vpart[6:7, 2 * width + first:2 * width + first + step] += column_sum(grad_u.astype(F32))
        for half_cols in halves:
            part[sum3.slot(i), :, half_cols] = dot(gu_buf[...], big[half_cols, :hidden], NT).astype(BF)
        sum3.begin(i)
        run(middle, "mid")
        for half_cols in halves:
            part2[sum2.slot(i), :, half_cols] = dot(hid_buf[...], big[half_cols, hidden:], NT).astype(BF)
        sum2.begin(i)
        for r in range(2):
            cols = slice(r * bq, (r + 1) * bq)
            for half_cols in halves:
                acc[r, :, half_cols] += dot(ac[block_rows(i), cols], gu_buf[:, half_cols], TN)
                acc[2 + r, :, half_cols] += dot(cot_buf[:, cols], hid_buf[:, half_cols], TN)

        @pl.when(i > 0)
        def _():
            copy_cot(i - 1).start()

        run(middle, "late")

        @pl.when(s == backward - 1)
        def _():
            for r in range(2):
                span = slice(r * bq, (r + 1) * bq)
                big[span, :hidden] = acc[r].astype(BF)
                big[span, hidden:] = acc[2 + r].astype(BF)
            far_parts[0].begin()
            far_parts[1].begin()
            copy_back().start()
            over(lambda b: copy_own(b).start(), 0, nb)

    @pl.when(s >= backward)
    def _():
        i = end - s
        lanes = lax.broadcasted_iota(jnp.int32, (bq, 128), 1)
        run(backward, "start")

        @pl.when(s == backward)
        def _():
            acc[...] = jnp.zeros_like(acc)

            def fill(b):
                span = block_rows(b)
                gu_buf[turned_spot(b)] = (qkv[span, width:2 * width].astype(F32) * (1.0 / d**0.5)).astype(BF).T
                for h in range(heads):
                    tile = head_tile(qkv, span, 2 * width, h, d)
                    part2[value_spot(h, b)] = jnp.where(lanes < d, tile, jnp.where(lanes < d + 3, 1.0, 0.0)).astype(BF)

            over(fill, 0, nb)

        spread_low.finish(i)
        grad_o = dot(low[block_rows(i), :], wo[...]).astype(BF)
        grad_t = grad_o.T
        q_nat = qkv[block_rows(i), 0:width]
        qt = q_nat.T
        queries, grads, q_pair, g_pair = [], [], [], []
        for h in range(heads):
            hs = slice(h * d, (h + 1) * d)
            delta = jnp.sum(grad_t[hs].astype(F32) * ot[i, hs, :], axis=0, keepdims=True)
            queries.append(jnp.concatenate(
                [qt[hs], stack_rows((128 - d, bq), (1.0, 1.0, 1.0) + three(-lse[i, h:h + 1, :]))], axis=0))
            grads.append(jnp.concatenate([grad_t[hs], stack_rows((128 - d, bq), three(-delta))], axis=0))
            pair = slice((h // 2) * 128, (h // 2) * 128 + 128)
            mine = (lanes < d) if h % 2 == 0 else (lanes >= d)
            q_pair.append(jnp.where(mine, q_nat[:, pair].astype(F32), 0.0).astype(BF))
            g_pair.append(jnp.where(mine, grad_o[:, pair].astype(F32), 0.0).astype(BF))
        run(backward, "early")

        def block(j, carry, diagonal):
            out = []
            kr = block_rows(j)
            for h in range(heads):
                scores = dot(ka[h, kr, :], queries[h])
                if diagonal:
                    scores = causal(scores, bq, bq)
                p = jnp.exp(scores)
                gs = (p * dot(part2[value_spot(h, j)], grads[h])).astype(BF)
                at_k = slice((h // 2) * 128, (h // 2) * 128 + 128)
                at_v = slice(width + (h // 2) * 128, width + (h // 2) * 128 + 128)
                acc[j, :, at_v] += dot(p.astype(BF), g_pair[h])
                acc[j, :, at_k] += dot(gs, q_pair[h])
                out.append(carry[h] + dot(gu_buf[turned_spot(j, h * d, d)], gs))
            return tuple(out)

        carry = lax.fori_loop(0, i, lambda j, c: block(j, c, False), (jnp.zeros((d, bq), F32),) * heads)
        run(backward, "mid")
        carry = block(i, carry, True)
        hid_buf[:, 0:width] = jnp.concatenate(carry, axis=0).T.astype(BF)
        hid_buf[:, width:3 * width] = acc[i, :, 0:2 * width].astype(BF)
        gqkv = hid_buf[:, 0:3 * width]
        for half_cols in halves:
            part[sum4.slot(i), :, half_cols] = dot(gqkv, wj[half_cols, :], NT).astype(BF)
        sum4.begin(i)
        sums = column_sum(gqkv.astype(F32))
        vpart[6:7, 0:width] += sums[:, 0:width]
        vpart[6:7, width:2 * width] += sums[:, 2 * width:]

        @pl.when(s == backward)
        def _():
            copy_back().wait()

        out_nat = ot[i].astype(BF).T
        for r in range(2):
            cols = slice(r * bq, (r + 1) * bq)
            left = ac[block_rows(i), cols]
            acc[2 * r, :, 2 * width:] += dot(left, hid_buf[:, 0:2 * width], TN)
            acc[2 * r + 1, :, 2 * width:3 * width] += dot(left, hid_buf[:, 2 * width:3 * width], TN)
            acc[2 * r + 1, :, 3 * width:] += dot(low[block_rows(i), cols], out_nat, TN)
        run(backward, "late")

    @pl.when(s == end)
    def _():
        sum4.pass_on(0)
        for r in range(2):
            for c in range(2):
                grads_near[r * bq:(r + 1) * bq, c * 2 * width:(c + 1) * 2 * width] = acc[2 * r + c, :, 2 * width:].astype(BF)
        for part_near in near_parts:
            part_near.begin()
        norm4(last - 1)
        near_parts[0].pass_on()
        norm4(last - 2)
        near_parts[1].pass_on()
        norm4(last - 3)
        if small:
            v_send[...] = jnp.zeros_like(v_send)
            for k in range(n_dp):
                v_send[k, 0:6, 0:shared_cols] = vpart[0:6, k * shared_cols:(k + 1) * shared_cols]
                v_send[k, 6:7, 0:split_cols] = vpart[6:7, k * split_cols:(k + 1) * split_cols]
            vec_sum.begin(v_send[me])
        near_parts[2].pass_on()
        near_parts[3].pass_on()
        for part_far in far_parts:
            part_far.finish()
        square = jnp.sum(total_ref[:, feats:] * total_ref[:, feats:])
        if small:
            vec_tensor.begin(vec_sum.total())
        else:
            vec_out[...] = vpart[...]
        spread_in.relay(last)
        spread_in.relay(last - 1)
        layer_block(last)
        layer_block(last - 1)
        for part_near in near_parts:
            part_near.finish()
        square = square + jnp.sum(total_ref[:, :feats] * total_ref[:, :feats])
        if small:
            shared_total = vec_tensor.total()
            row_ids = lax.broadcasted_iota(jnp.int32, vec_out.shape, 0)
            vec_total = jnp.where(row_ids < 6, shared_total, s_buf[rank])
            vec_out[...] = vec_total
            vec_kept = jnp.where(row_ids >= jnp.where(rank == 0, 0, 6), vec_total, 0.0)
            square = square + jnp.sum(vec_kept * vec_kept)
        square_sum.begin(jnp.full(q_buf.shape[1:], square, F32))
        spread_in.relay(last - 2)
        layer_block(last - 2)
        square_tensor.begin(square_sum.total())
        layer_block(last - 3)
        spread_in.relay(last - 3)
        square_out[...] = square_tensor.total()
        for b in range(last, -1, -1):
            spread_lay.relay(b)
        over(spread_in.finish, 0, nb)
        over(spread_lay.finish, 0, nb)


def layer(lengths, tokens, cot, near_shard, far_shard, vec_shard, vec_cols, heads, d, total_heads, bq, n_dp, n_tensor, collective_id):
    n, feats = tokens.shape
    rows = near_shard.shape[0]
    width = heads * d
    hidden = far_shard.shape[1] // 2
    nb, quarter, lines = n // bq, bq // 4, n_dp // 2
    wide = n_dp * max(vec_cols)
    small = n_dp <= 8
    slot = (8, -(-max(vec_cols) // 128) * 128)
    slots = n_dp if small else 1
    near_cuts = [(0, k * width, k * width, width) for k in range(3)] + [(1, 3 * width, 0, width)]
    step = hidden // 2
    far_cuts = [(side * hidden + first, step // 2) for first in range(0, hidden, step // 2) for side in range(2)]
    sum_far = [(k * step, step) for k in range(4)]
    sum_near = [(k * width, width) for k in range(4)]
    dims = (heads, d, total_heads, bq, nb, n_dp, n_tensor, near_cuts, far_cuts, (sum_far, sum_near), vec_cols)
    vm, dma = pltpu.VMEM, pltpu.SemaphoreType.DMA
    own = (nb, quarter, feats)
    sums = [vm((nb, 2 * quarter, feats), BF), vm(own, BF), vm(own, BF)]
    tile = (8, 128)
    kinds = 9 if lines == 4 else 5
    scratch = [
        vm((n, 3 * width), BF), vm((heads, n, 128), BF),
        vm((feats, 2 * hidden), BF), vm((feats, 3 * width), BF), vm((feats, width), BF), vm((n, feats), BF),
        vm((n, feats), BF), vm((nb, width, bq), F32), vm((nb, heads, bq), F32), vm(own, F32), vm(own, F32),
        vm((4, bq, hidden), F32), vm((bq, hidden), BF), vm((bq, hidden), BF), vm((bq, feats), BF),
        vm((3, bq, feats), BF), *sums, vm((2, bq, feats), BF), *sums,
        vm((4, lines, rows, step), BF), vm((4, lines, rows, step), BF),
        vm((4, lines, rows, width), BF), vm((4, lines, rows, width), BF),
        vm((slots,) + vec_shard.shape, BF), vm((16, wide), F32), vm((8, wide), F32),
        vm((slots,) + slot, F32), vm((slots,) + slot, F32), vm((n_tensor,) + slot, F32), vm((n_dp,) + tile, F32), vm((n_tensor,) + tile, F32),
        dma((kinds, len(near_cuts), lines)), dma((kinds, len(far_cuts), lines)), dma((4, 4, nb)), dma((4, 7, nb)),
        dma((4, 4, lines)), dma((4, 4, lines)), dma((1 + nb,)), dma((n_dp,)), dma((n_dp,)), dma((n_dp,)), dma((n_dp,)),
        dma((n_dp,)), dma((n_dp,)), dma((n_tensor,)), dma((n_tensor,)), dma((n_tensor,)), dma((n_tensor,)),
    ]
    shape = jax.ShapeDtypeStruct
    return pl.pallas_call(
        functools.partial(layer_kernel, dims),
        grid=(1 + 3 * nb,),
        in_specs=[pl.BlockSpec(memory_space=pltpu.SMEM)] + [ANYWHERE] * 4 + [whole(vec_shard)],
        out_specs=[fixed((rows, feats + 2 * hidden)), fixed(slot if small else (8, wide)), fixed(tile), ANYWHERE, ANYWHERE, ANYWHERE],
        out_shape=[shape((rows, feats + 2 * hidden), F32), shape(slot if small else (8, wide), F32), shape(tile, F32),
                   shape((n, feats), BF), shape((n, feats), BF), shape((n, feats), BF)],
        scratch_shapes=scratch,
        compiler_params=params(collective_id, 63),
        name="layer",
    )(lengths, tokens, cot, near_shard, far_shard, vec_shard)


def adam_step(master, moment, variance, gradient, rate, decay):
    moment_new = BETA_FIRST * moment + (1.0 - BETA_FIRST) * gradient
    variance_new = BETA_SECOND * variance + (1.0 - BETA_SECOND) * gradient * gradient
    moment_hat = moment_new / (1.0 - BETA_FIRST**STEP)
    variance_hat = variance_new / (1.0 - BETA_SECOND**STEP)
    master_new = master - rate * (
        moment_hat / (jnp.sqrt(variance_hat) + ADAM_EPSILON) + decay * master
    )
    return (master_new, moment_new, variance_new)


def update_kernel(head_size, square_ref, joint_sum, output_sum, widen_sum, narrow_sum, vec_sum, *refs):
    ins, outs, norm_ref = refs[:18], refs[18:36], refs[36]
    norm = jnp.sqrt(square_ref[0:1, 0:1])
    factor = jnp.minimum(1.0, CLIP_LIMIT / (norm + 1e-06))

    def step(at, gradient, rate, decay, cols=slice(None)):
        new = adam_step(*[ref[:, cols] for ref in ins[3 * at:3 * at + 3]], factor * gradient, rate, decay)
        for ref, value in zip(outs[3 * at:3 * at + 3], new):
            ref[:, cols] = value

    joint = ins[0].shape[1]
    heads = joint // (3 * head_size)

    def source(piece):
        head, kind = piece // 3, piece % 3
        first = (kind * heads + head) * head_size
        return joint_sum[:, first:first + head_size]

    for piece in range(0, joint // head_size, 2):
        cols = slice(piece * head_size, (piece + 2) * head_size)
        step(0, jnp.concatenate([source(piece), source(piece + 1)], axis=1), MATRIX_RATE, MATRIX_DECAY, cols)
    step(1, output_sum[...].T, OUTPUT_RATE, MATRIX_DECAY)
    step(2, widen_sum[...], MATRIX_RATE, MATRIX_DECAY)
    step(3, narrow_sum[...].T, MATRIX_RATE, MATRIX_DECAY)

    @pl.when(pl.program_id(0) == 0)
    def _():
        norm_ref[...] = norm
        step(4, vec_sum[0:6, 0:ins[12].shape[1]], VECTOR_RATE, 0.0)
        step(5, vec_sum[6:7, 0:ins[15].shape[1]], VECTOR_RATE, 0.0)


def update(square, sums, vec, states, head_size):
    count = 2
    joint, output, widen, narrow = [states[3 * k].shape for k in range(4)]
    rows = joint[0]

    def halves(shape):
        return pl.BlockSpec((shape[0] // count, shape[1]), lambda i: (i, 0))

    def all_of(shape):
        return pl.BlockSpec(shape, lambda i: (0, 0))

    def columns(first, cols):
        wide = cols // count
        return pl.BlockSpec((rows, wide), lambda i: (0, first // wide + i))

    states_specs = [halves(state.shape) for state in states[:12]] + [all_of(state.shape) for state in states[12:]]
    widen_at, narrow_at = joint[1] + output[0], joint[1] + output[0] + widen[1]
    return pl.pallas_call(
        functools.partial(update_kernel, head_size),
        grid=(count,),
        in_specs=[all_of(square.shape), halves(joint), columns(joint[1], output[0]),
                  pl.BlockSpec((rows // count, widen[1]), lambda i: (i, widen_at // widen[1])),
                  columns(narrow_at, narrow[0]), all_of(vec.shape)] + states_specs,
        out_specs=states_specs + [all_of((1, 1))],
        out_shape=[jax.ShapeDtypeStruct(state.shape, F32) for state in states] + [jax.ShapeDtypeStruct((1, 1), F32)],
        compiler_params=pltpu.CompilerParams(vmem_limit_bytes=63 * 2**20),
        name="update",
    )(square, sums, sums, sums, sums, vec, *states)


def pack_kernel(head_size, joint_ref, widen_ref, output_ref, narrow_ref, shared_ref, split_ref, near_ref, far_ref, vec_ref):
    joint = joint_ref.shape[1]
    heads = joint // (3 * head_size)

    def source(piece):
        kind, head = piece // heads, piece % heads
        first = (head * 3 + kind) * head_size
        return joint_ref[:, first:first + head_size]

    for piece in range(0, joint // head_size, 2):
        cols = slice(piece * head_size, (piece + 2) * head_size)
        near_ref[:, cols] = jnp.concatenate([source(piece), source(piece + 1)], axis=1).astype(BF)
    near_ref[:, joint:] = output_ref[...].T.astype(BF)
    far_ref[:, :widen_ref.shape[1]] = widen_ref[...].astype(BF)
    far_ref[:, widen_ref.shape[1]:] = narrow_ref[...].T.astype(BF)

    def padded(values):
        return jnp.concatenate([values, jnp.zeros((values.shape[0], vec_ref.shape[1] - values.shape[1]), F32)], axis=1)

    rest = jnp.zeros((9, vec_ref.shape[1]), F32)
    vec_ref[...] = jnp.concatenate([padded(shared_ref[...]), padded(split_ref[...]), rest], axis=0).astype(BF)


def pack(joint, widen, output, narrow, shared, split, vec_cols, head_size):
    rows = joint.shape[0]
    shapes = [(rows, joint.shape[1] + output.shape[0]), (rows, widen.shape[1] + narrow.shape[0]), (16, vec_cols)]
    whole_of = lambda array: pl.BlockSpec(array.shape, lambda i: (0, 0))
    arrays = (joint, widen, output, narrow, shared, split)
    return pl.pallas_call(
        functools.partial(pack_kernel, head_size),
        grid=(1,),
        in_specs=[whole_of(array) for array in arrays],
        out_specs=[pl.BlockSpec(shape, lambda i: (0, 0)) for shape in shapes],
        out_shape=[jax.ShapeDtypeStruct(shape, BF) for shape in shapes],
        compiler_params=pltpu.CompilerParams(vmem_limit_bytes=63 * 2**20),
        name="pack",
    )(*arrays)


def on_device(
    tokens,
    cotangent,
    lengths,
    joint_weight,
    output_weight,
    widen_weight,
    narrow_weight,
    shared_vectors,
    split_vectors,
    joint_first,
    joint_second,
    output_first,
    output_second,
    widen_first,
    widen_second,
    narrow_first,
    narrow_second,
    shared_first,
    shared_second,
    split_first,
    split_second,
):
    n_dp, n_tensor = lax.axis_size("dp"), lax.axis_size("tensor")
    me = lax.axis_index("dp")
    head_cols = output_weight.shape[0]
    shared_cols, split_cols = shared_vectors.shape[1], split_vectors.shape[1]
    vec_cols = -(-max(shared_cols, split_cols) // 128) * 128
    head_size = D // HEADS
    near_shard, far_shard, vec_shard = pack(
        joint_weight, widen_weight, output_weight, narrow_weight, shared_vectors, split_vectors, vec_cols, head_size
    )
    if n_dp > 8:
        shared_all = lax.all_gather(shared_vectors.astype(BF), "dp", axis=1, tiled=True)
        split_all = lax.all_gather(split_vectors.astype(BF), "dp", axis=1, tiled=True)
        vec_shard = jnp.concatenate(
            [jnp.pad(shared_all, ((0, 0), (0, split_all.shape[1] - shared_all.shape[1]))), split_all], axis=0
        )
        vec_shard = jnp.pad(vec_shard, ((0, 9), (0, 0)))
    local_heads = head_cols // head_size
    total_rows = tokens.shape[0]
    block = min(512, total_rows)
    sums, vec_sum, square, input_grad, layer_output, _ = layer(
        lengths, tokens, cotangent, near_shard, far_shard, vec_shard, (shared_cols, split_cols), local_heads, head_size, HEADS, block, n_dp,
        n_tensor, 0,
    )
    if n_dp > 8:
        split_all = lax.psum(vec_sum[6:7], "dp")
        shared_all = lax.psum(vec_sum[:6], ("dp", "tensor"))
        square = square + jnp.sum(shared_all * shared_all) + lax.psum(jnp.sum(split_all * split_all), "tensor")
        shared_sum = lax.dynamic_slice(shared_all, (0, me * shared_cols), (6, shared_cols))
        split_sum = lax.dynamic_slice(split_all, (0, me * split_cols), (1, split_cols))
        vec_sum = jnp.concatenate(
            [
                jnp.pad(shared_sum, ((0, 0), (0, vec_cols - shared_cols))),
                jnp.pad(split_sum, ((0, 1), (0, vec_cols - split_cols))),
            ],
            axis=0,
        )
    states = (
        joint_weight, joint_first, joint_second, output_weight, output_first, output_second,
        widen_weight, widen_first, widen_second, narrow_weight, narrow_first, narrow_second,
        shared_vectors, shared_first, shared_second, split_vectors, split_first, split_second,
    )
    *updated, grad_norm = update(square, sums, vec_sum, states, head_size)
    return (layer_output, input_grad, grad_norm.reshape(()), *updated)


def solution(mesh):
    in_specs = (
        P("dp", None),
        P("dp", None),
        P("dp"),
        P("dp", "tensor"),
        P("tensor", "dp"),
        P("dp", "tensor"),
        P("tensor", "dp"),
        P(None, "dp"),
        P("tensor", "dp"),
        P("dp", "tensor"),
        P("dp", "tensor"),
        P("tensor", "dp"),
        P("tensor", "dp"),
        P("dp", "tensor"),
        P("dp", "tensor"),
        P("tensor", "dp"),
        P("tensor", "dp"),
        P(None, "dp"),
        P(None, "dp"),
        P("tensor", "dp"),
        P("tensor", "dp"),
    )
    out_specs = (
        P("dp", None),
        P("dp", None),
        P(),
        P("dp", "tensor"),
        P("dp", "tensor"),
        P("dp", "tensor"),
        P("tensor", "dp"),
        P("tensor", "dp"),
        P("tensor", "dp"),
        P("dp", "tensor"),
        P("dp", "tensor"),
        P("dp", "tensor"),
        P("tensor", "dp"),
        P("tensor", "dp"),
        P("tensor", "dp"),
        P(None, "dp"),
        P(None, "dp"),
        P(None, "dp"),
        P("tensor", "dp"),
        P("tensor", "dp"),
        P("tensor", "dp"),
    )
    return jax.shard_map(
        on_device, mesh=mesh, in_specs=in_specs, out_specs=out_specs, check_vma=False
    )
```

```python
import functools
import math

import jax
import jax.numpy as jnp
from jax import lax
from jax.experimental import pallas as pl
from jax.experimental.pallas import tpu as pltpu
from jax.sharding import PartitionSpec as P

F32, BF = jnp.float32, jnp.bfloat16

D = 1024
HEADS = 16
STEP = 10


NORM_EPSILON = 1e-05
CLIP_LIMIT = 1.0
BETA_FIRST = 0.9
BETA_SECOND = 0.95
ADAM_EPSILON = 1e-08
MATRIX_RATE = 0.05
OUTPUT_RATE = 0.2
VECTOR_RATE = 0.6
MATRIX_DECAY = 0.1


NN = (((1,), (0,)), ((), ()))
NT = (((1,), (1,)), ((), ()))
TN = (((0,), (0,)), ((), ()))
LOW = -1e30


def dot(left, right, dims=NN):
    return lax.dot_general(left, right, dims, preferred_element_type=F32)


def three(values):
    high = values.astype(BF).astype(F32)
    rest = values - high
    middle = rest.astype(BF).astype(F32)
    return high, middle, rest - middle


def stack_rows(shape, rows):
    ids = lax.broadcasted_iota(jnp.int32, shape, 0)
    out = jnp.zeros(shape, F32)
    for at, row in enumerate(rows):
        out = jnp.where(ids == at, row, out)
    return out.astype(BF)


def head_tile(ref, rows, col, head, d):
    lane = col + (head // 2) * 128
    tile = ref[rows, lane:lane + 128].astype(F32)
    if head % 2:
        tile = pltpu.roll(tile, 64, 1)
    return tile


def fill_keys(qkv_ref, ka_ref, heads, d, slope_of, first, count):
    rows = pl.ds(first, count)
    lanes = lax.broadcasted_iota(jnp.int32, (count, 128), 1)
    position = (lax.broadcasted_iota(jnp.int32, (count, 128), 0) + first).astype(F32)
    for head in range(heads):
        high, middle, low = three(position * slope_of(head))
        tile = head_tile(qkv_ref, rows, heads * d, head, d)
        for at, part in enumerate((high, middle, low, 1.0, 1.0, 1.0)):
            tile = jnp.where(lanes == d + at, part, tile)
        ka_ref[head, rows, :] = jnp.where(lanes < d + 6, tile, 0.0).astype(BF)


def causal(scores, bk, bq):
    kid = lax.broadcasted_iota(jnp.int32, (bk, bq), 0)
    qid = lax.broadcasted_iota(jnp.int32, (bk, bq), 1)
    return jnp.where(kid <= qid, scores, LOW)


def slope_fn(heads, total_heads):
    rank = lax.axis_index("tensor")
    def slope_of(head):
        index = jnp.full((1, 128), rank * heads + head + 1, jnp.int32).astype(F32)
        return jnp.exp2(index * (-8.0 / total_heads))
    return slope_of


def at_dp(index):
    return {"dp": index}


def at_tensor(index):
    return {"tensor": index}


def remote(src, dst, send, recv, where):
    return pltpu.make_async_remote_copy(
        src_ref=src, dst_ref=dst, send_sem=send, recv_sem=recv, device_id=where, device_id_type=pl.DeviceIdType.MESH
    )


def greet(n_dp, n_tensor):
    me, rank = lax.axis_index("dp"), lax.axis_index("tensor")
    barrier = pltpu.get_barrier_semaphore()

    def along_dp(k, c):
        pl.semaphore_signal(barrier, inc=1, device_id=at_dp(lax.rem(me + k, n_dp)), device_id_type=pl.DeviceIdType.MESH)
        return c

    lax.fori_loop(1, n_dp, along_dp, 0)
    for k in range(1, n_tensor):
        pl.semaphore_signal(
            barrier, inc=1, device_id=at_tensor(lax.rem(rank + k, n_tensor)), device_id_type=pl.DeviceIdType.MESH
        )
    pl.semaphore_wait(barrier, n_dp + n_tensor - 2)


def over(body, first, last):
    lax.fori_loop(first, last, lambda k, c: (body(k), c)[1], 0)


def greet_tensor(n_tensor):
    rank = lax.axis_index("tensor")
    barrier = pltpu.get_barrier_semaphore()
    for k in range(1, n_tensor):
        pl.semaphore_signal(
            barrier, inc=1, device_id=at_tensor(lax.rem(rank + k, n_tensor)), device_id_type=pl.DeviceIdType.MESH
        )
    pl.semaphore_wait(barrier, n_tensor - 1)


class Gather:
    def __init__(self, lines, rows, pieces, sems):
        me = lax.axis_index("dp")
        self.me, self.z, self.x = me, me // 2, lax.rem(me, 2)
        self.lines, self.rows, self.pieces, self.sems = lines, rows, pieces, sems
        self.other = at_dp(self.z * 2 + 1 - self.x)
        self.relayed = lines == 4

    def crossing(self, s):
        return self.relayed and self.pieces[s][5]

    def own(self, s):
        shard, first, _, cols = self.pieces[s][:4]
        return shard.at[:, pl.ds(first, cols)]

    def spot(self, s, zz, column):
        _, _, first, cols, out = self.pieces[s][:5]
        device = zz * 2 + (self.x if column == 0 else 1 - self.x)
        return out.at[pl.ds(pl.multiple_of(device * self.rows, self.rows), self.rows), pl.ds(first, cols)]

    def sem(self, kind, s, index):
        return self.sems.at[kind, s, index]

    def to_x(self, s, zz, src):
        return remote(src, self.spot(s, zz, 0), self.sem(0, s, zz), self.sem(1, s, zz), self.other)

    def from_x(self, s, zz):
        spot = self.spot(s, zz, 1)
        return remote(spot, spot, self.sem(0, s, zz), self.sem(1, s, zz), self.other)

    def along_z(self, s, column, src, zz, send, target):
        kind = 2 + 2 * column
        return remote(src, self.spot(s, zz, column), send, self.sem(kind + 1, s, zz), at_dp(target * 2 + self.x))

    def to_z(self, s, column, k):
        src = self.own(s) if column == 0 else self.spot(s, self.z, 1)
        return self.along_z(s, column, src, self.z, self.sem(2 + 2 * column, s, k), lax.rem(self.z + k, self.lines))

    def each_to_z(self, s, column, action):
        def step(k):
            if not self.relayed:
                action(self.to_z(s, column, k))
                return
            gap = lax.rem(self.z + k, self.lines) - self.z

            @pl.when((gap != 3) & (gap != -3))
            def _():
                action(self.to_z(s, column, k))

        over(step, 1, self.lines)

    def from_z(self, s, column, zz):
        spot = self.spot(s, zz, column)
        return self.along_z(s, column, spot, zz, self.sem(2 + 2 * column, s, 0), self.z)

    def relay_copy(self, s, column):
        source, target = jnp.where(self.z == 2, 0, 3), jnp.where(self.z == 2, 3, 0)
        return self.along_z(s, column, self.spot(s, source, column), source, self.sem(6 + column, s, 0), target)

    def inner(self):
        return (self.z == 1) | (self.z == 2)

    def relays(self, zz):
        return ((self.z == 2) & (zz == 0)) | ((self.z == 1) & (zz == 3))

    def keep(self, s):
        return pltpu.make_async_copy(self.own(s), self.spot(s, self.z, 0), self.sem(self.sems.shape[0] - 1, s, 0))

    def begin_z(self, s):
        self.each_to_z(s, 0, lambda copy: copy.start())
        self.keep(s).start()

    def begin_x(self, s):
        self.to_x(s, self.z, self.own(s)).start()

    def forward(self, s):
        def step(k):
            zz = lax.rem(self.z + k, self.lines)
            self.from_z(s, 0, zz).wait_recv()
            if self.relayed:
                @pl.when(self.relays(zz))
                def _():
                    self.relay_copy(s, 0).start()
            self.to_x(s, zz, self.spot(s, zz, 0)).start()

        over(step, 1, self.lines)

    def cross(self, s):
        if not self.crossing(s):
            return
        self.from_x(s, self.z).wait_recv()
        self.each_to_z(s, 1, lambda copy: copy.start())

    def relay(self, s, column):
        if not self.crossing(s):
            if column == 0:
                self.forward(s)
            return

        @pl.when(self.inner())
        def _():
            self.from_z(s, column, jnp.where(self.z == 2, 0, 3)).wait_recv()
            self.relay_copy(s, column).start()

    def finish(self, s):
        self.keep(s).wait()
        columns = range(2 if self.crossing(s) else 1)
        for column in columns:
            self.each_to_z(s, column, lambda copy: copy.wait_send())
            if self.relayed:
                @pl.when(self.inner())
                def _(column=column):
                    self.relay_copy(s, column).wait_send()
        if self.crossing(s):
            self.to_x(s, self.z, self.own(s)).wait_send()
            for column in columns:
                def arrived(k, column=column):
                    zz = lax.rem(self.z + k, self.lines)

                    @pl.when(jnp.logical_not(self.relays(zz)))
                    def _():
                        self.from_z(s, column, zz).wait_recv()

                over(arrived, 1, self.lines)
        else:
            over(lambda zz: self.to_x(s, zz, self.own(s)).wait_send(), 0, self.lines)
            over(lambda zz: self.from_x(s, zz).wait_recv(), 0, self.lines)


class Place:
    def __init__(self):
        rank = lax.axis_index("tensor")
        self.far, self.near = rank // 2, lax.rem(rank, 2)
        self.near_device = at_tensor(self.far * 2 + 1 - self.near)
        self.far_device = at_tensor((1 - self.far) * 2 + self.near)


class BlockSum:
    def __init__(self, place, quarter, part, slot, near_buf, send_buf, far_buf, sems):
        self.place, self.quarter, self.part, self.slot = place, quarter, part, slot
        self.near_buf, self.send_buf, self.far_buf, self.sems = near_buf, send_buf, far_buf, sems

    def rows(self, near, far):
        first = (near * 2 + far) * self.quarter
        return pl.ds(pl.multiple_of(first, self.quarter), self.quarter)

    def half(self, near):
        first = near * 2 * self.quarter
        return pl.ds(pl.multiple_of(first, self.quarter), 2 * self.quarter)

    def to_near(self, b):
        return remote(self.part.at[self.slot(b), self.half(1 - self.place.near)], self.near_buf.at[b],
                      self.sems.at[0, b], self.sems.at[1, b], self.place.near_device)

    def to_far(self, b):
        return remote(self.send_buf.at[b], self.far_buf.at[b], self.sems.at[2, b], self.sems.at[3, b],
                      self.place.far_device)

    def pair(self, b, far):
        own = self.part[self.slot(b), self.rows(self.place.near, far)].astype(F32)
        return own + self.near_buf[b, self.rows(0, far)].astype(F32)

    def begin(self, b):
        self.to_near(b).start()

    def stage(self, b):
        self.to_near(b).wait_recv()
        self.send_buf[b] = self.pair(b, 1 - self.place.far).astype(BF)

    def pass_on(self, b):
        self.stage(b)
        self.to_far(b).start()

    def total(self, b):
        self.to_far(b).wait()
        self.to_near(b).wait_send()
        return self.pair(b, self.place.far) + self.far_buf[b].astype(F32)

    def stage_all(self, b):
        self.stage(b)
        rows = self.rows(0, self.place.far)
        self.near_buf[b, rows] = self.pair(b, self.place.far).astype(BF)
        self.to_near(b).wait_send()

    def late_total(self, b):
        self.to_far(b).wait()
        return self.near_buf[b, self.rows(0, self.place.far)].astype(F32) + self.far_buf[b].astype(F32)


class BlockSpread:
    def __init__(self, place, quarter, out, sems, own=None):
        self.place, self.quarter, self.out, self.sems, self.own = place, quarter, out, sems, own

    def rows(self, b, near, far):
        first = (b * 4 + near * 2 + far) * self.quarter
        return pl.ds(pl.multiple_of(first, self.quarter), self.quarter)

    def spot(self, b, near, far):
        return self.out.at[self.rows(b, near, far)]

    def mine(self, b):
        return self.spot(b, self.place.near, self.place.far)

    def source(self, b):
        return self.mine(b) if self.own is None else self.own.at[b]

    def put(self, b, values):
        if self.own is None:
            self.out[self.rows(b, self.place.near, self.place.far), :] = values
        else:
            self.own[b] = values
        self.to_far(b).start()
        self.to_near(b).start()
        if self.own is not None:
            self.keep(b).start()

    def to_far(self, b):
        return remote(self.source(b), self.mine(b), self.sems.at[0, b], self.sems.at[1, b], self.place.far_device)

    def to_near(self, b):
        return remote(self.source(b), self.mine(b), self.sems.at[2, b], self.sems.at[3, b], self.place.near_device)

    def arrival(self, near, far, b, at):
        spot = self.spot(b, near, far)
        return remote(spot, spot, self.sems.at[at - 1, b], self.sems.at[at, b], self.place.near_device)

    def pass_far(self, b):
        spot = self.spot(b, self.place.near, 1 - self.place.far)
        return remote(spot, spot, self.sems.at[4, b], self.sems.at[5, b], self.place.near_device)

    def keep(self, b):
        return pltpu.make_async_copy(self.own.at[b], self.mine(b), self.sems.at[6, b])

    def relay(self, b):
        self.arrival(self.place.near, 1 - self.place.far, b, 1).wait_recv()
        self.pass_far(b).start()

    def finish(self, b):
        self.to_far(b).wait_send()
        self.to_near(b).wait_send()
        self.pass_far(b).wait_send()
        if self.own is not None:
            self.keep(b).wait()
        self.arrival(1 - self.place.near, self.place.far, b, 3).wait_recv()
        self.arrival(1 - self.place.near, 1 - self.place.far, b, 5).wait_recv()


def normalize(values):
    centred = values - jnp.mean(values, axis=-1, keepdims=True)
    inverse = lax.rsqrt(jnp.mean(centred * centred, axis=-1, keepdims=True) + NORM_EPSILON)
    return (centred * inverse, inverse)


def normalize_back(incoming, normed, inverse, gain):
    scaled = incoming * gain
    return inverse * (
        scaled
        - jnp.mean(scaled, axis=-1, keepdims=True)
        - normed * jnp.mean(scaled * normed, axis=-1, keepdims=True)
    )


def column_sum(values):
    return jnp.sum(values, axis=0, keepdims=True)


def params(collective_id, megabytes):
    return pltpu.CompilerParams(
        collective_id=collective_id, has_side_effects=True, vmem_limit_bytes=megabytes * 2**20
    )


ANYWHERE = pl.BlockSpec(memory_space=pl.ANY)


def fixed(shape):
    return pl.BlockSpec(shape, lambda i: (0,) * len(shape), pipeline_mode=pl.Buffered(1))


def whole(array):
    return fixed(array.shape)


class Scatter:
    def __init__(self, lines, rows, source, first, cols, x_buf, z_buf, total, at, sems, part):
        me = lax.axis_index("dp")
        self.z, self.x = me // 2, lax.rem(me, 2)
        self.lines, self.rows, self.source = lines, rows, source
        self.cols, self.total_cols = pl.ds(first, cols), pl.ds(at, cols)
        self.x_buf, self.z_buf, self.total, self.sems, self.part = x_buf, z_buf, total, sems, part

    def dest(self, k):
        return lax.rem(self.z + 1 + k, self.lines)

    def chunk(self, device):
        return (pl.ds(pl.multiple_of(device * self.rows, self.rows), self.rows), self.cols)

    def sem(self, kind, index):
        return self.sems.at[kind, self.part, index]

    def to_x(self, dz):
        return remote(self.source.at[self.chunk(dz * 2 + 1 - self.x)], self.x_buf.at[dz], self.sem(0, dz),
                      self.sem(1, dz), at_dp(self.z * 2 + 1 - self.x))

    def to_z(self, dz):
        return remote(self.x_buf.at[dz], self.z_buf.at[self.z], self.sem(2, dz), self.sem(3, self.z),
                      at_dp(dz * 2 + self.x))

    def from_z(self, zz):
        return remote(self.z_buf.at[zz], self.z_buf.at[zz], self.sem(2, zz), self.sem(3, zz), at_dp(zz * 2 + self.x))

    def begin(self):
        over(lambda k: self.to_x(self.dest(k)).start(), 0, self.lines)

    def summed(self, dz):
        self.to_x(dz).wait()
        return self.x_buf[dz].astype(F32) + self.source[self.chunk(dz * 2 + self.x)].astype(F32)

    def pass_on(self):
        def step(k):
            dz = self.dest(k)
            self.x_buf[dz] = self.summed(dz).astype(BF)
            self.to_z(dz).start()

        over(step, 0, self.lines - 1)
        self.total[:, self.total_cols] = self.summed(self.z)

    def finish(self):
        def add(k):
            zz = lax.rem(self.z + k, self.lines)
            self.from_z(zz).wait_recv()
            self.total[:, self.total_cols] += self.z_buf[zz].astype(F32)
            self.to_z(zz).wait_send()

        over(add, 1, self.lines)


class Exchange:
    def __init__(self, buf, index, count, where, send, recv, pieces=None):
        self.buf, self.index, self.count, self.where = buf, index, count, where
        self.send, self.recv, self.pieces = send, recv, pieces

    def to(self, k):
        other = lax.rem(self.index + k, self.count)
        source = self.buf.at[self.index] if self.pieces is None else self.pieces.at[other]
        return remote(source, self.buf.at[self.index], self.send.at[k], self.recv.at[self.index], self.where(other))

    def begin(self, values):
        self.buf[self.index] = values
        over(lambda k: self.to(k).start(), 1, self.count)

    def finish(self):
        def arrived(k):
            other = lax.rem(self.index + k, self.count)
            remote(self.buf.at[other], self.buf.at[other], self.send.at[0], self.recv.at[other],
                   self.where(other)).wait_recv()
            self.to(k).wait_send()

        over(arrived, 1, self.count)

    def total(self):
        self.finish()
        zero = jnp.zeros(self.buf.shape[1:], F32)
        return lax.fori_loop(0, self.count, lambda k, acc: acc + self.buf[k], zero)


def layer_kernel(dims, len_ref, tok_ref, cot_ref, near_shard, far_shard, vec_shard,
                 total_ref, vec_out, square_out, in_out, lay_out, a_hbm, *scratch):
    heads, d, total_heads, bq, nb, n_dp, n_tensor, near_cuts, far_cuts, sum_cuts, vec_cols = dims
    (qkv, ka, big, wj, wo, ac, low, ot, lse, h1, gh1, acc, hid_buf, gu_buf, cot_buf,
     part, near_buf, send_buf, far_buf, part2, near2_buf, send2_buf, far2_buf, x_far, z_far, x_near, z_near,
     vec_buf, vec, vpart, v_send, v_buf, s_buf, q_buf, t_buf,
     gn_sems, gf_sems, sum_sems, spread_sems, sf_sems, sn_sems, copy_sems, vs, vr, vs2, vr2, qs, qr, ss, sr, ts, tr) = scratch
    s = pl.program_id(0)
    place = Place()
    me, rank = lax.axis_index("dp"), lax.axis_index("tensor")
    width, feats, hidden = heads * d, ac.shape[1], big.shape[1] // 2
    quarter, lines, rows = bq // 4, n_dp // 2, total_ref.shape[0]
    last = nb - 1
    halves = (slice(0, feats // 2), slice(feats // 2, feats))
    small = n_dp <= 8

    def slot_from(base):
        return lambda b: lax.rem(base + last - b, 3)

    sum1, sum3, sum4 = (
        BlockSum(place, quarter, part, slot_from(k * nb), near_buf, send_buf, far_buf, sum_sems.at[k]) for k in range(3)
    )
    sum2 = BlockSum(place, quarter, part2, lambda b: lax.rem(last - b, 2), near2_buf, send2_buf, far2_buf, sum_sems.at[3])
    spread_c = BlockSpread(place, quarter, ac, spread_sems.at[0])
    spread_low = BlockSpread(place, quarter, low, spread_sems.at[1])
    spread_lay = BlockSpread(place, quarter, lay_out, spread_sems.at[2], send2_buf)
    spread_in = BlockSpread(place, quarter, in_out, spread_sems.at[3], send_buf)
    near_gather = Gather(lines, rows, [
        (near_shard, first, at, cols, (wj, wo)[index], index == 1) for index, first, at, cols in near_cuts],
                         gn_sems)
    far_gather = Gather(lines, rows, [
        (far_shard, first, first, cols, big, p == len(far_cuts) - 1) for p, (first, cols) in enumerate(far_cuts)], gf_sems)
    grads_near = part2.reshape(2 * bq, feats)
    far_parts = [
        Scatter(lines, rows, big, first, cols, x_far.at[p], z_far.at[p], total_ref, feats + first, sf_sems, p)
        for p, (first, cols) in enumerate(sum_cuts[0])
    ]
    near_parts = [
        Scatter(lines, rows, grads_near, first, cols, x_near.at[p], z_near.at[p], total_ref, first, sn_sems, p)
        for p, (first, cols) in enumerate(sum_cuts[1])
    ]
    vec_gather = Exchange(vec_buf, me, n_dp, at_dp, vs, vr)
    vec_sum = Exchange(v_buf, me, n_dp, at_dp, vs2, vr2, v_send)
    shared_cols, split_cols = vec_cols
    vec_tensor = Exchange(s_buf, rank, n_tensor, at_tensor, ss, sr)
    square_sum = Exchange(q_buf, me, n_dp, at_dp, qs, qr)
    square_tensor = Exchange(t_buf, rank, n_tensor, at_tensor, ts, tr)

    def block_rows(b):
        return pl.ds(pl.multiple_of(b * bq, bq), bq)

    def turned_spot(b, first=0, count=None):
        row = pl.multiple_of(lax.rem(b, 2) * width + first, d)
        return (pl.ds(row, width if count is None else count), pl.ds(pl.multiple_of(b // 2 * bq, bq), bq))

    def value_spot(h, b):
        lane = pl.multiple_of(((h % 2) * nb + b) * 128, 128)
        return (h // 2, slice(None), pl.ds(lane, 128))

    def own_rows(b):
        return spread_c.rows(b, place.near, place.far)

    def copy_tokens():
        return pltpu.make_async_copy(tok_ref, low, copy_sems.at[0])

    def copy_a(b):
        return pltpu.make_async_copy(ac.at[block_rows(b)], a_hbm.at[block_rows(b)], copy_sems.at[1 + b])

    def copy_back():
        return pltpu.make_async_copy(a_hbm, ac, copy_sems.at[0])

    def copy_cot(b):
        return pltpu.make_async_copy(cot_ref.at[block_rows(b)], cot_buf, copy_sems.at[0])

    def own_spot(b):
        return pl.ds(pl.multiple_of(b * quarter, quarter), quarter)

    def copy_own(b):
        return pltpu.make_async_copy(tok_ref.at[own_rows(b)], cot_buf.at[own_spot(b)], copy_sems.at[1 + b])

    def norm1(b):
        hidden_one = h1[b] + sum1.total(b)
        h1[b] = hidden_one
        normed, _ = normalize(hidden_one)
        spread_c.put(b, (normed * vec[2:3, :feats] + vec[3:4, :feats]).astype(BF))

    def norm3(b):
        grad_c = sum3.total(b)
        normed, inverse = normalize(h1[b])
        grad_out = gh1[b]
        grad_h = grad_out + normalize_back(grad_c, normed, inverse, vec[2:3, :feats])
        gh1[b] = grad_h
        spread_low.put(b, grad_h.astype(BF))
        vpart[2:3, :feats] += column_sum(grad_c * normed)
        vpart[3:4, :feats] += column_sum(grad_c)
        vpart[4:5, :feats] += column_sum(grad_h)
        vpart[5:6, :feats] += column_sum(grad_out)

    def norm4(b):
        grad_a = sum4.total(b)
        copy_own(b).wait()
        normed, inverse = normalize(cot_buf[own_spot(b), :].astype(F32))
        spread_in.put(b, (gh1[b] + normalize_back(grad_a, normed, inverse, vec[0:1, :feats])).astype(BF))
        vpart[0:1, :feats] += column_sum(grad_a * normed)
        vpart[1:2, :feats] += column_sum(grad_a)

    def layer_block(b):
        ids = lax.broadcasted_iota(jnp.int32, (quarter, 1), 0) + (b * 4 + place.near * 2 + place.far) * quarter
        result = h1[b] + sum2.late_total(b) + vec[5:6, :feats]
        spread_lay.put(b, jnp.where(ids < len_ref[0], result, 0.0).astype(BF))

    forward, middle, backward = 1, 1 + nb, 1 + 2 * nb
    end = 3 * nb
    plan = {}

    def at(step, point, action, *args):
        plan.setdefault((step, point), []).append((action, args))

    for k in range(nb - 1):
        at(forward + k + 1, "early", sum1.pass_on, last - k)
    at(forward, "early", far_gather.forward, 0)
    at(forward, "mid", far_gather.forward, 1)
    at(forward, "late", far_gather.forward, 2)
    at(forward + 1, "mid", far_gather.forward, 3)
    at(forward + 1, "late", norm1, last)
    at(forward + 2, "mid", spread_c.relay, last)
    at(forward + 2, "late", far_gather.forward, 4)
    at(forward + 3, "early", copy_cot(last).start)
    at(forward + 3, "late", norm1, last - 1)
    at(forward + 3, "late", far_gather.forward, 5)
    at(middle, "start", sum1.pass_on, 0)
    at(middle, "start", norm1, last - 2)
    for piece in range(4):
        at(middle, "chunk%d" % (piece // 2), far_gather.finish, piece)
    at(middle, "chunk2", far_gather.forward, 6)
    at(middle, "chunk2", spread_c.relay, last - 1)
    for piece in range(4, 6):
        at(middle, "chunk2", far_gather.finish, piece)
    at(middle, "chunk3", far_gather.relay, 7, 0)
    at(middle, "chunk3", far_gather.relay, 7, 1)
    for piece in range(6, 8):
        at(middle, "chunk3", far_gather.finish, piece)
    at(middle, "mid", norm1, last - 3)
    at(middle, "late", spread_c.relay, last - 2)
    for k in range(1, nb):
        at(middle + k, "early", sum3.pass_on, last - k + 1)
        at(middle + k, "early", sum2.stage_all, last - k + 1)
    at(middle + 1, "mid", spread_c.relay, last - 3)
    at(middle + 1, "late", norm3, last)
    at(middle + 2, "early", sum2.to_far(last).start)
    at(middle + 2, "mid", spread_low.relay, last)
    at(middle + 2, "late", norm3, last - 1)
    at(middle + 3, "early", sum2.to_far(last - 1).start)
    at(backward, "start", sum2.stage_all, 0)
    at(backward, "early", spread_low.relay, last - 1)
    at(backward, "early", norm3, last - 2)
    at(backward, "early", sum3.pass_on, 0)
    at(backward, "mid", far_parts[0].pass_on)
    at(backward, "mid", far_parts[2].begin)
    at(backward, "late", spread_low.relay, last - 2)
    at(backward, "late", far_parts[1].pass_on)
    at(backward, "late", far_parts[3].begin)
    for k in range(nb - 1):
        at(backward + k + 1, "early", sum4.pass_on, last - k)
    at(backward + 1, "mid", norm3, last - 3)
    at(backward + 1, "mid", far_parts[2].pass_on)
    at(backward + 1, "late", sum2.to_far(last - 2).start)
    at(backward + 1, "late", sum2.to_far(last - 3).start)
    at(backward + 1, "late", far_parts[3].pass_on)
    at(backward + 2, "mid", spread_low.relay, last - 3)
    at(backward + 3, "mid", norm4, last)

    def run(phase, point):
        for step in range(phase, phase + nb):
            actions = plan.get((step, point), ())
            if actions:
                @pl.when(s == step)
                def _(actions=actions):
                    for action, args in actions:
                        action(*args)

    @pl.when(s == 0)
    def _():
        copy_tokens().start()
        greet(n_dp, n_tensor)
        if small:
            vec_gather.begin(vec_shard[...])
        near_gather.begin_x(3)
        for piece in range(3):
            near_gather.begin_z(piece)
            near_gather.begin_x(piece)
        near_gather.begin_z(3)
        near_gather.cross(3)
        vpart[...] = jnp.zeros_like(vpart)
        copy_tokens().wait()
        if small:
            vec_gather.finish()
            for k in range(n_dp):
                vec[0:6, k * shared_cols:(k + 1) * shared_cols] = vec_buf[k].astype(F32)[0:6, 0:shared_cols]
            for k in range(0, n_dp, 2):
                pair = [vec_buf[k + side].astype(F32)[6:7, 0:split_cols] for side in range(2)]
                vec[6:7, k * split_cols:(k + 2) * split_cols] = jnp.concatenate(pair, axis=1)
        else:
            vec[...] = vec_shard[...].astype(F32)

        def norm(b):
            span = block_rows(b)
            normed, _ = normalize(low[span, :].astype(F32))
            ac[span, :] = (normed * vec[0:1, :feats] + vec[1:2, :feats]).astype(BF)
            copy_a(b).start()
            h1[b] = low[own_rows(b), :].astype(F32) + vec[4:5, :feats]

        over(norm, 0, nb // 2)
        near_gather.forward(0)
        over(norm, nb // 2, nb)
        scale = 1.0 / d**0.5

        def project(kind):
            near_gather.finish(kind)
            cols = slice(kind * width, (kind + 1) * width)

            def step(b):
                span = block_rows(b)
                out = dot(ac[span, :], wj[:, cols])
                if kind == 0:
                    out = (out + vec[6:7, 0:width]) * scale
                if kind == 2:
                    out = out + vec[6:7, width:2 * width]
                qkv[span, cols] = out.astype(BF)

            over(step, 0, nb)

        near_gather.forward(1)
        far_gather.begin_x(len(far_cuts) - 1)
        project(0)
        near_gather.forward(2)
        for piece in range(len(far_cuts)):
            far_gather.begin_z(piece)
        project(1)
        near_gather.relay(3, 0)
        for piece in range(len(far_cuts) - 1):
            far_gather.begin_x(piece)
        project(2)
        far_gather.cross(len(far_cuts) - 1)

        def fill(b):
            first = pl.multiple_of(b * bq, bq)
            fill_keys(qkv, ka, heads, d, slope_fn(heads, total_heads), first, bq)
            gu_buf[turned_spot(b)] = qkv[pl.ds(first, bq), 2 * width:3 * width].T

        over(fill, 0, nb)
        near_gather.relay(3, 1)
        over(lambda b: copy_a(b).wait(), 0, nb)

    @pl.when((s >= forward) & (s < middle))
    def _():
        i = middle - 1 - s
        qt = qkv[block_rows(i), 0:width].T
        ones = stack_rows((128 - d, bq), (1.0, 1.0, 1.0))
        queries = [jnp.concatenate([qt[h * d:(h + 1) * d], ones], axis=0) for h in range(heads)]
        run(forward, "early")

        def block(j, carry, diagonal):
            out = []
            kr = block_rows(j)
            for h in range(heads):
                m, l, total = carry[h]
                scores = dot(ka[h, kr, :], queries[h])
                if diagonal:
                    scores = causal(scores, bq, bq)
                top = jnp.maximum(m, jnp.max(scores, axis=0, keepdims=True))
                p = jnp.exp(scores - top)
                scale = jnp.exp(m - top)
                l = l * scale + jnp.sum(p, axis=0, keepdims=True)
                total = total * scale + dot(gu_buf[turned_spot(j, h * d, d)], p.astype(BF))
                out.append((top, l, total))
            return tuple(out)

        start = (jnp.full((1, bq), LOW, F32), jnp.zeros((1, bq), F32), jnp.zeros((d, bq), F32))
        carry = lax.fori_loop(0, i, lambda j, c: block(j, c, False), (start,) * heads)
        run(forward, "mid")
        carry = block(i, carry, True)
        for h in range(heads):
            m, l, total = carry[h]
            ot[i, h * d:(h + 1) * d, :] = total / l
            lse[i, h:h + 1, :] = m + jnp.log(l)
        out_nat = ot[i].astype(BF).T

        @pl.when(s == forward)
        def _():
            near_gather.finish(3)

        for half_cols in halves:
            part[sum1.slot(i), :, half_cols] = dot(out_nat, wo[half_cols, :], NT).astype(BF)
        sum1.begin(i)
        run(forward, "late")

    @pl.when((s >= middle) & (s < backward))
    def _():
        i = backward - 1 - s
        run(middle, "start")

        @pl.when(s == middle)
        def _():
            acc[...] = jnp.zeros_like(acc)

        spread_c.finish(i)
        copy_cot(i).wait()
        row_ids = lax.broadcasted_iota(jnp.int32, (bq, 128), 0) + i * bq
        live = jnp.where(row_ids < len_ref[0], 1.0, 0.0).astype(BF)
        cot_buf[...] = cot_buf[...] * jnp.concatenate([live] * (feats // 128), axis=1)
        gh1[i] = cot_buf[sum1.rows(place.near, place.far), :].astype(F32)
        run(middle, "early")
        root = math.sqrt(2.0 / math.pi)
        step = 256
        for first in range(0, hidden, step):
            run(middle, "chunk%d" % (first // step))
            cols = slice(first, first + step)
            u = dot(ac[block_rows(i), :], big[:, cols]) + vec[6:7, 2 * width + first:2 * width + first + step]
            square = u * u
            bent = jnp.tanh(root * (u + 0.044715 * (square * u)))
            half = 0.5 * (1.0 + bent)
            hid_buf[:, cols] = (u * half).astype(BF)
            slope = half + 0.5 * u * (1.0 - bent * bent) * (root * (1.0 + 3 * 0.044715 * square))
            grad_u = (dot(cot_buf[...], big[:, hidden + first:hidden + first + step]) * slope).astype(BF)
            gu_buf[:, cols] = grad_u
            vpart[6:7, 2 * width + first:2 * width + first + step] += column_sum(grad_u.astype(F32))
        for half_cols in halves:
            part[sum3.slot(i), :, half_cols] = dot(gu_buf[...], big[half_cols, :hidden], NT).astype(BF)
        sum3.begin(i)
        run(middle, "mid")
        for half_cols in halves:
            part2[sum2.slot(i), :, half_cols] = dot(hid_buf[...], big[half_cols, hidden:], NT).astype(BF)
        sum2.begin(i)
        for r in range(2):
            cols = slice(r * bq, (r + 1) * bq)
            for half_cols in halves:
                acc[r, :, half_cols] += dot(ac[block_rows(i), cols], gu_buf[:, half_cols], TN)
                acc[2 + r, :, half_cols] += dot(cot_buf[:, cols], hid_buf[:, half_cols], TN)

        @pl.when(i > 0)
        def _():
            copy_cot(i - 1).start()

        run(middle, "late")

        @pl.when(s == backward - 1)
        def _():
            for r in range(2):
                span = slice(r * bq, (r + 1) * bq)
                big[span, :hidden] = acc[r].astype(BF)
                big[span, hidden:] = acc[2 + r].astype(BF)
            far_parts[0].begin()
            far_parts[1].begin()
            copy_back().start()
            over(lambda b: copy_own(b).start(), 0, nb)

    @pl.when(s >= backward)
    def _():
        i = end - s
        lanes = lax.broadcasted_iota(jnp.int32, (bq, 128), 1)
        run(backward, "start")

        @pl.when(s == backward)
        def _():
            acc[...] = jnp.zeros_like(acc)

            def fill(b):
                span = block_rows(b)
                gu_buf[turned_spot(b)] = (qkv[span, width:2 * width].astype(F32) * (1.0 / d**0.5)).astype(BF).T
                for h in range(heads):
                    tile = head_tile(qkv, span, 2 * width, h, d)
                    part2[value_spot(h, b)] = jnp.where(lanes < d, tile, jnp.where(lanes < d + 3, 1.0, 0.0)).astype(BF)

            over(fill, 0, nb)

        spread_low.finish(i)
        grad_o = dot(low[block_rows(i), :], wo[...]).astype(BF)
        grad_t = grad_o.T
        q_nat = qkv[block_rows(i), 0:width]
        qt = q_nat.T
        queries, grads, q_pair, g_pair = [], [], [], []
        for h in range(heads):
            hs = slice(h * d, (h + 1) * d)
            delta = jnp.sum(grad_t[hs].astype(F32) * ot[i, hs, :], axis=0, keepdims=True)
            queries.append(jnp.concatenate(
                [qt[hs], stack_rows((128 - d, bq), (1.0, 1.0, 1.0) + three(-lse[i, h:h + 1, :]))], axis=0))
            grads.append(jnp.concatenate([grad_t[hs], stack_rows((128 - d, bq), three(-delta))], axis=0))
            pair = slice((h // 2) * 128, (h // 2) * 128 + 128)
            mine = (lanes < d) if h % 2 == 0 else (lanes >= d)
            q_pair.append(jnp.where(mine, q_nat[:, pair].astype(F32), 0.0).astype(BF))
            g_pair.append(jnp.where(mine, grad_o[:, pair].astype(F32), 0.0).astype(BF))
        run(backward, "early")

        def block(j, carry, diagonal):
            out = []
            kr = block_rows(j)
            for h in range(heads):
                scores = dot(ka[h, kr, :], queries[h])
                if diagonal:
                    scores = causal(scores, bq, bq)
                p = jnp.exp(scores)
                gs = (p * dot(part2[value_spot(h, j)], grads[h])).astype(BF)
                at_k = slice((h // 2) * 128, (h // 2) * 128 + 128)
                at_v = slice(width + (h // 2) * 128, width + (h // 2) * 128 + 128)
                acc[j, :, at_v] += dot(p.astype(BF), g_pair[h])
                acc[j, :, at_k] += dot(gs, q_pair[h])
                out.append(carry[h] + dot(gu_buf[turned_spot(j, h * d, d)], gs))
            return tuple(out)

        carry = lax.fori_loop(0, i, lambda j, c: block(j, c, False), (jnp.zeros((d, bq), F32),) * heads)
        run(backward, "mid")
        carry = block(i, carry, True)
        hid_buf[:, 0:width] = jnp.concatenate(carry, axis=0).T.astype(BF)
        hid_buf[:, width:3 * width] = acc[i, :, 0:2 * width].astype(BF)
        gqkv = hid_buf[:, 0:3 * width]
        for half_cols in halves:
            part[sum4.slot(i), :, half_cols] = dot(gqkv, wj[half_cols, :], NT).astype(BF)
        sum4.begin(i)
        sums = column_sum(gqkv.astype(F32))
        vpart[6:7, 0:width] += sums[:, 0:width]
        vpart[6:7, width:2 * width] += sums[:, 2 * width:]

        @pl.when(s == backward)
        def _():
            copy_back().wait()

        out_nat = ot[i].astype(BF).T
        for r in range(2):
            cols = slice(r * bq, (r + 1) * bq)
            left = ac[block_rows(i), cols]
            acc[2 * r, :, 2 * width:] += dot(left, hid_buf[:, 0:2 * width], TN)
            acc[2 * r + 1, :, 2 * width:3 * width] += dot(left, hid_buf[:, 2 * width:3 * width], TN)
            acc[2 * r + 1, :, 3 * width:] += dot(low[block_rows(i), cols], out_nat, TN)
        run(backward, "late")

    @pl.when(s == end)
    def _():
        sum4.pass_on(0)
        for r in range(2):
            for c in range(2):
                grads_near[r * bq:(r + 1) * bq, c * 2 * width:(c + 1) * 2 * width] = acc[2 * r + c, :, 2 * width:].astype(BF)
        for part_near in near_parts:
            part_near.begin()
        norm4(last - 1)
        near_parts[0].pass_on()
        norm4(last - 2)
        near_parts[1].pass_on()
        norm4(last - 3)
        if small:
            v_send[...] = jnp.zeros_like(v_send)
            for k in range(n_dp):
                v_send[k, 0:6, 0:shared_cols] = vpart[0:6, k * shared_cols:(k + 1) * shared_cols]
                v_send[k, 6:7, 0:split_cols] = vpart[6:7, k * split_cols:(k + 1) * split_cols]
            vec_sum.begin(v_send[me])
        near_parts[2].pass_on()
        near_parts[3].pass_on()
        for part_far in far_parts:
            part_far.finish()
        square = jnp.sum(total_ref[:, feats:] * total_ref[:, feats:])
        if small:
            vec_tensor.begin(vec_sum.total())
        else:
            vec_out[...] = vpart[...]
        spread_in.relay(last)
        spread_in.relay(last - 1)
        layer_block(last)
        layer_block(last - 1)
        for part_near in near_parts:
            part_near.finish()
        square = square + jnp.sum(total_ref[:, :feats] * total_ref[:, :feats])
        if small:
            shared_total = vec_tensor.total()
            row_ids = lax.broadcasted_iota(jnp.int32, vec_out.shape, 0)
            vec_total = jnp.where(row_ids < 6, shared_total, s_buf[rank])
            vec_out[...] = vec_total
            vec_kept = jnp.where(row_ids >= jnp.where(rank == 0, 0, 6), vec_total, 0.0)
            square = square + jnp.sum(vec_kept * vec_kept)
        square_sum.begin(jnp.full(q_buf.shape[1:], square, F32))
        spread_in.relay(last - 2)
        layer_block(last - 2)
        square_tensor.begin(square_sum.total())
        layer_block(last - 3)
        spread_in.relay(last - 3)
        square_out[...] = square_tensor.total()
        for b in range(last, -1, -1):
            spread_lay.relay(b)
        over(spread_in.finish, 0, nb)
        over(spread_lay.finish, 0, nb)


def layer(lengths, tokens, cot, near_shard, far_shard, vec_shard, vec_cols, heads, d, total_heads, bq, n_dp, n_tensor, collective_id):
    n, feats = tokens.shape
    rows = near_shard.shape[0]
    width = heads * d
    hidden = far_shard.shape[1] // 2
    nb, quarter, lines = n // bq, bq // 4, n_dp // 2
    wide = n_dp * max(vec_cols)
    small = n_dp <= 8
    slot = (8, -(-max(vec_cols) // 128) * 128)
    slots = n_dp if small else 1
    near_cuts = [(0, k * width, k * width, width) for k in range(3)] + [(1, 3 * width, 0, width)]
    step = hidden // 2
    far_cuts = [(side * hidden + first, step // 2) for first in range(0, hidden, step // 2) for side in range(2)]
    sum_far = [(k * step, step) for k in range(4)]
    sum_near = [(k * width, width) for k in range(4)]
    dims = (heads, d, total_heads, bq, nb, n_dp, n_tensor, near_cuts, far_cuts, (sum_far, sum_near), vec_cols)
    vm, dma = pltpu.VMEM, pltpu.SemaphoreType.DMA
    own = (nb, quarter, feats)
    sums = [vm((nb, 2 * quarter, feats), BF), vm(own, BF), vm(own, BF)]
    tile = (8, 128)
    kinds = 9 if lines == 4 else 5
    scratch = [
        vm((n, 3 * width), BF), vm((heads, n, 128), BF),
        vm((feats, 2 * hidden), BF), vm((feats, 3 * width), BF), vm((feats, width), BF), vm((n, feats), BF),
        vm((n, feats), BF), vm((nb, width, bq), F32), vm((nb, heads, bq), F32), vm(own, F32), vm(own, F32),
        vm((4, bq, hidden), F32), vm((bq, hidden), BF), vm((bq, hidden), BF), vm((bq, feats), BF),
        vm((3, bq, feats), BF), *sums, vm((2, bq, feats), BF), *sums,
        vm((4, lines, rows, step), BF), vm((4, lines, rows, step), BF),
        vm((4, lines, rows, width), BF), vm((4, lines, rows, width), BF),
        vm((slots,) + vec_shard.shape, BF), vm((16, wide), F32), vm((8, wide), F32),
        vm((slots,) + slot, F32), vm((slots,) + slot, F32), vm((n_tensor,) + slot, F32), vm((n_dp,) + tile, F32), vm((n_tensor,) + tile, F32),
        dma((kinds, len(near_cuts), lines)), dma((kinds, len(far_cuts), lines)), dma((4, 4, nb)), dma((4, 7, nb)),
        dma((4, 4, lines)), dma((4, 4, lines)), dma((1 + nb,)), dma((n_dp,)), dma((n_dp,)), dma((n_dp,)), dma((n_dp,)),
        dma((n_dp,)), dma((n_dp,)), dma((n_tensor,)), dma((n_tensor,)), dma((n_tensor,)), dma((n_tensor,)),
    ]
    shape = jax.ShapeDtypeStruct
    return pl.pallas_call(
        functools.partial(layer_kernel, dims),
        grid=(1 + 3 * nb,),
        in_specs=[pl.BlockSpec(memory_space=pltpu.SMEM)] + [ANYWHERE] * 4 + [whole(vec_shard)],
        out_specs=[fixed((rows, feats + 2 * hidden)), fixed(slot if small else (8, wide)), fixed(tile), ANYWHERE, ANYWHERE, ANYWHERE],
        out_shape=[shape((rows, feats + 2 * hidden), F32), shape(slot if small else (8, wide), F32), shape(tile, F32),
                   shape((n, feats), BF), shape((n, feats), BF), shape((n, feats), BF)],
        scratch_shapes=scratch,
        compiler_params=params(collective_id, 63),
        name="layer",
    )(lengths, tokens, cot, near_shard, far_shard, vec_shard)


def adam_step(master, moment, variance, gradient, rate, decay):
    moment_new = BETA_FIRST * moment + (1.0 - BETA_FIRST) * gradient
    variance_new = BETA_SECOND * variance + (1.0 - BETA_SECOND) * gradient * gradient
    moment_hat = moment_new / (1.0 - BETA_FIRST**STEP)
    variance_hat = variance_new / (1.0 - BETA_SECOND**STEP)
    master_new = master - rate * (
        moment_hat / (jnp.sqrt(variance_hat) + ADAM_EPSILON) + decay * master
    )
    return (master_new, moment_new, variance_new)


def update_kernel(head_size, square_ref, joint_sum, output_sum, widen_sum, narrow_sum, vec_sum, *refs):
    ins, outs, norm_ref = refs[:18], refs[18:36], refs[36]
    norm = jnp.sqrt(square_ref[0:1, 0:1])
    factor = jnp.minimum(1.0, CLIP_LIMIT / (norm + 1e-06))

    def step(at, gradient, rate, decay, cols=slice(None)):
        new = adam_step(*[ref[:, cols] for ref in ins[3 * at:3 * at + 3]], factor * gradient, rate, decay)
        for ref, value in zip(outs[3 * at:3 * at + 3], new):
            ref[:, cols] = value

    joint = ins[0].shape[1]
    heads = joint // (3 * head_size)

    def source(piece):
        head, kind = piece // 3, piece % 3
        first = (kind * heads + head) * head_size
        return joint_sum[:, first:first + head_size]

    for piece in range(0, joint // head_size, 2):
        cols = slice(piece * head_size, (piece + 2) * head_size)
        step(0, jnp.concatenate([source(piece), source(piece + 1)], axis=1), MATRIX_RATE, MATRIX_DECAY, cols)
    step(1, output_sum[...].T, OUTPUT_RATE, MATRIX_DECAY)
    step(2, widen_sum[...], MATRIX_RATE, MATRIX_DECAY)
    step(3, narrow_sum[...].T, MATRIX_RATE, MATRIX_DECAY)

    @pl.when(pl.program_id(0) == 0)
    def _():
        norm_ref[...] = norm
        step(4, vec_sum[0:6, 0:ins[12].shape[1]], VECTOR_RATE, 0.0)
        step(5, vec_sum[6:7, 0:ins[15].shape[1]], VECTOR_RATE, 0.0)


def update(square, sums, vec, states, head_size):
    count = 2
    joint, output, widen, narrow = [states[3 * k].shape for k in range(4)]
    rows = joint[0]

    def halves(shape):
        return pl.BlockSpec((shape[0] // count, shape[1]), lambda i: (i, 0))

    def all_of(shape):
        return pl.BlockSpec(shape, lambda i: (0, 0))

    def columns(first, cols):
        wide = cols // count
        return pl.BlockSpec((rows, wide), lambda i: (0, first // wide + i))

    states_specs = [halves(state.shape) for state in states[:12]] + [all_of(state.shape) for state in states[12:]]
    widen_at, narrow_at = joint[1] + output[0], joint[1] + output[0] + widen[1]
    return pl.pallas_call(
        functools.partial(update_kernel, head_size),
        grid=(count,),
        in_specs=[all_of(square.shape), halves(joint), columns(joint[1], output[0]),
                  pl.BlockSpec((rows // count, widen[1]), lambda i: (i, widen_at // widen[1])),
                  columns(narrow_at, narrow[0]), all_of(vec.shape)] + states_specs,
        out_specs=states_specs + [all_of((1, 1))],
        out_shape=[jax.ShapeDtypeStruct(state.shape, F32) for state in states] + [jax.ShapeDtypeStruct((1, 1), F32)],
        compiler_params=pltpu.CompilerParams(vmem_limit_bytes=63 * 2**20),
        name="update",
    )(square, sums, sums, sums, sums, vec, *states)


def pack_kernel(head_size, joint_ref, widen_ref, output_ref, narrow_ref, shared_ref, split_ref, near_ref, far_ref, vec_ref):
    joint = joint_ref.shape[1]
    heads = joint // (3 * head_size)

    def source(piece):
        kind, head = piece // heads, piece % heads
        first = (head * 3 + kind) * head_size
        return joint_ref[:, first:first + head_size]

    for piece in range(0, joint // head_size, 2):
        cols = slice(piece * head_size, (piece + 2) * head_size)
        near_ref[:, cols] = jnp.concatenate([source(piece), source(piece + 1)], axis=1).astype(BF)
    near_ref[:, joint:] = output_ref[...].T.astype(BF)
    far_ref[:, :widen_ref.shape[1]] = widen_ref[...].astype(BF)
    far_ref[:, widen_ref.shape[1]:] = narrow_ref[...].T.astype(BF)

    def padded(values):
        return jnp.concatenate([values, jnp.zeros((values.shape[0], vec_ref.shape[1] - values.shape[1]), F32)], axis=1)

    rest = jnp.zeros((9, vec_ref.shape[1]), F32)
    vec_ref[...] = jnp.concatenate([padded(shared_ref[...]), padded(split_ref[...]), rest], axis=0).astype(BF)


def pack(joint, widen, output, narrow, shared, split, vec_cols, head_size):
    rows = joint.shape[0]
    shapes = [(rows, joint.shape[1] + output.shape[0]), (rows, widen.shape[1] + narrow.shape[0]), (16, vec_cols)]
    whole_of = lambda array: pl.BlockSpec(array.shape, lambda i: (0, 0))
    arrays = (joint, widen, output, narrow, shared, split)
    return pl.pallas_call(
        functools.partial(pack_kernel, head_size),
        grid=(1,),
        in_specs=[whole_of(array) for array in arrays],
        out_specs=[pl.BlockSpec(shape, lambda i: (0, 0)) for shape in shapes],
        out_shape=[jax.ShapeDtypeStruct(shape, BF) for shape in shapes],
        compiler_params=pltpu.CompilerParams(vmem_limit_bytes=63 * 2**20),
        name="pack",
    )(*arrays)


def on_device(
    tokens,
    cotangent,
    lengths,
    joint_weight,
    output_weight,
    widen_weight,
    narrow_weight,
    shared_vectors,
    split_vectors,
    joint_first,
    joint_second,
    output_first,
    output_second,
    widen_first,
    widen_second,
    narrow_first,
    narrow_second,
    shared_first,
    shared_second,
    split_first,
    split_second,
):
    n_dp, n_tensor = lax.axis_size("dp"), lax.axis_size("tensor")
    me = lax.axis_index("dp")
    head_cols = output_weight.shape[0]
    shared_cols, split_cols = shared_vectors.shape[1], split_vectors.shape[1]
    vec_cols = -(-max(shared_cols, split_cols) // 128) * 128
    head_size = D // HEADS
    near_shard, far_shard, vec_shard = pack(
        joint_weight, widen_weight, output_weight, narrow_weight, shared_vectors, split_vectors, vec_cols, head_size
    )
    if n_dp > 8:
        shared_all = lax.all_gather(shared_vectors.astype(BF), "dp", axis=1, tiled=True)
        split_all = lax.all_gather(split_vectors.astype(BF), "dp", axis=1, tiled=True)
        vec_shard = jnp.concatenate(
            [jnp.pad(shared_all, ((0, 0), (0, split_all.shape[1] - shared_all.shape[1]))), split_all], axis=0
        )
        vec_shard = jnp.pad(vec_shard, ((0, 9), (0, 0)))
    local_heads = head_cols // head_size
    total_rows = tokens.shape[0]
    block = min(512, total_rows)
    sums, vec_sum, square, input_grad, layer_output, _ = layer(
        lengths, tokens, cotangent, near_shard, far_shard, vec_shard, (shared_cols, split_cols), local_heads, head_size, HEADS, block, n_dp,
        n_tensor, 0,
    )
    if n_dp > 8:
        split_all = lax.psum(vec_sum[6:7], "dp")
        shared_all = lax.psum(vec_sum[:6], ("dp", "tensor"))
        square = square + jnp.sum(shared_all * shared_all) + lax.psum(jnp.sum(split_all * split_all), "tensor")
        shared_sum = lax.dynamic_slice(shared_all, (0, me * shared_cols), (6, shared_cols))
        split_sum = lax.dynamic_slice(split_all, (0, me * split_cols), (1, split_cols))
        vec_sum = jnp.concatenate(
            [
                jnp.pad(shared_sum, ((0, 0), (0, vec_cols - shared_cols))),
                jnp.pad(split_sum, ((0, 1), (0, vec_cols - split_cols))),
            ],
            axis=0,
        )
    states = (
        joint_weight, joint_first, joint_second, output_weight, output_first, output_second,
        widen_weight, widen_first, widen_second, narrow_weight, narrow_first, narrow_second,
        shared_vectors, shared_first, shared_second, split_vectors, split_first, split_second,
    )
    *updated, grad_norm = update(square, sums, vec_sum, states, head_size)
    return (layer_output, input_grad, jnp.sqrt(square[0, 0]), *updated)


def solution(mesh):
    in_specs = (
        P("dp", None),
        P("dp", None),
        P("dp"),
        P("dp", "tensor"),
        P("tensor", "dp"),
        P("dp", "tensor"),
        P("tensor", "dp"),
        P(None, "dp"),
        P("tensor", "dp"),
        P("dp", "tensor"),
        P("dp", "tensor"),
        P("tensor", "dp"),
        P("tensor", "dp"),
        P("dp", "tensor"),
        P("dp", "tensor"),
        P("tensor", "dp"),
        P("tensor", "dp"),
        P(None, "dp"),
        P(None, "dp"),
        P("tensor", "dp"),
        P("tensor", "dp"),
    )
    out_specs = (
        P("dp", None),
        P("dp", None),
        P(),
        P("dp", "tensor"),
        P("dp", "tensor"),
        P("dp", "tensor"),
        P("tensor", "dp"),
        P("tensor", "dp"),
        P("tensor", "dp"),
        P("dp", "tensor"),
        P("dp", "tensor"),
        P("dp", "tensor"),
        P("tensor", "dp"),
        P("tensor", "dp"),
        P("tensor", "dp"),
        P(None, "dp"),
        P(None, "dp"),
        P(None, "dp"),
        P("tensor", "dp"),
        P("tensor", "dp"),
        P("tensor", "dp"),
    )
    return jax.shard_map(
        on_device, mesh=mesh, in_specs=in_specs, out_specs=out_specs, check_vma=False
    )
```
